32 devices in a mesh: wide: 8 (over y, x, core), narrow: 4 (over z).
Axes of the slice: x: 2, y: 2, z: 4, core: 2. Of those that a mesh axis runs over, the one named last changes fastest.
Arguments:
- enc_in: bfloat16 [16384, 1024], P(('wide', 'narrow')), may hold values from -6 to 6
- dec_in: bfloat16 [16384, 1024], P(('wide', 'narrow')), may hold values from -6 to 6
- segment_ids: int32 [16384], P(('wide', 'narrow')), may hold values from 0 to 8, as said below
- enc_cot: bfloat16 [16384, 1024], P(('wide', 'narrow'))
- dec_cot: bfloat16 [16384, 1024], P(('wide', 'narrow'))
- enc_qkv: bfloat16 [3, 1024, 1024], P(None, 'wide'), may hold values from -0.1875 to 0.1875
- enc_wo: bfloat16 [1024, 1024], P('wide'), may hold values from -0.75 to 0.75
- enc_w_in: bfloat16 [1024, 4096], P('wide'), may hold values from -0.1875 to 0.1875
- enc_w_out: bfloat16 [4096, 1024], P('wide'), may hold values from -0.09375 to 0.09375
- enc_gains: bfloat16 [2, 1024], P(None, 'wide'), may hold values from 0.25 to 1.75
- dec_qkv: bfloat16 [6, 1024, 1024], P(None, 'wide'), may hold values from -0.1875 to 0.1875
- dec_wo: bfloat16 [2, 1024, 1024], P(None, 'wide'), may hold values from -0.75 to 0.75
- dec_w_in: bfloat16 [1024, 4096], P('wide'), may hold values from -0.1875 to 0.1875
- dec_w_out: bfloat16 [4096, 1024], P('wide'), may hold values from -0.09375 to 0.09375
- dec_gains: bfloat16 [3, 1024], P(None, 'wide'), may hold values from 0.25 to 1.75
- adapter_weights: float32 [4, 1024, 512], P(None, ('wide', 'narrow')), may hold values from -0.25 to 0.25
- adapter_momenta: float32 [4, 1024, 512], P(None, ('wide', 'narrow'))
- bias_in: float32 [2, 512], replicated, may hold values from -3 to 3
- bias_out: float32 [2, 1024], replicated, may hold values from -2 to 2
Outputs:
- enc_out: bfloat16 [16384, 1024], P(('wide', 'narrow'))
- dec_out: bfloat16 [16384, 1024], P(('wide', 'narrow'))
- grad_enc_in: float32 [16384, 1024], P(('wide', 'narrow'))
- grad_dec_in: float32 [16384, 1024], P(('wide', 'narrow'))
- grad_bias_in: float32 [2, 512], P(None, ('wide', 'narrow'))
- grad_bias_out: float32 [2, 1024], P(None, ('wide', 'narrow'))
- new_momenta: float32 [4, 1024, 512], P(None, ('wide', 'narrow'))
- new_weights: float32 [4, 1024, 512], P(None, ('wide', 'narrow'))
The draws below stay inside these ranges and needn't reach their ends.
Inputs may be any that keep to these rules, and one draw needn't show every extreme that they name: `segment_ids`: within each sequence of 1024 consecutive tokens the ids never fall, equal ids mark one document, and a sequence holds at most 9 documents.
All inputs are finite; a program needn't handle non-finite values.
Results may differ from the reference program's by a relative error of at most 0.02.
Values may be sent and summed in bfloat16 or wider, within the bound.
A program may use at most 448 MiB of HBM per device.

```python
import math
import jax
import jax.numpy as jnp
from jax import lax

D = 1024
HD = 64
FF = 4096
ADAPT = 512
SEQ = 1024
NS_ITERS = 5
TOKENS = 16384


def rising_rows(count, top_scale):
    return top_scale ** (jnp.arange(count, dtype=jnp.float32) / (count - 1))


def draw_segment_ids(key, part):
    key = jax.random.fold_in(key, 11)
    key_start, key_cuts = jax.random.split(key)
    sequences = TOKENS // SEQ
    longest = 3 * SEQ // 4
    starts = jax.random.randint(key_start, (sequences, 1), 0, SEQ - longest + 1)
    picks = jax.random.randint(key_cuts, (sequences, 6), 1, SEQ - longest + 1)
    cuts = jnp.where(picks <= starts, picks, picks + longest - 1)
    places = jnp.arange(SEQ, dtype=jnp.int32)[None, :, None]
    bounds = jnp.concatenate([starts, starts + longest, cuts], axis=1)[:, None, :]
    return jnp.sum((places >= bounds).astype(jnp.int32), axis=2).reshape(TOKENS)


def draw_enc_cot(key, part):
    key = jax.random.fold_in(key, 21)
    base_draw = jax.random.normal(key, (TOKENS, D), jnp.float32)
    top_scale = 3.0
    return (base_draw * rising_rows(TOKENS, top_scale)[:, None] * (2.0 / (1.0 + top_scale))).astype(jnp.bfloat16)


def draw_dec_cot(key, part):
    key = jax.random.fold_in(key, 22)
    base_draw = jax.random.normal(key, (TOKENS, D), jnp.float32)
    top_scale = 3.0
    return (base_draw * rising_rows(TOKENS, top_scale)[:, None] * (2.0 / (1.0 + top_scale))).astype(jnp.bfloat16)


def draw_adapter_momenta(key, part):
    key = jax.random.fold_in(key, 31)
    key_entries, key_columns = jax.random.split(key, 2)
    columns = 10.0 ** jax.random.uniform(key_columns, (4, 1, ADAPT), jnp.float32, -0.5, 0.5)
    entries = jax.random.normal(key_entries, (4, D, ADAPT), jnp.float32)
    return entries * (0.3 * rising_rows(D, 10.0))[None, :, None] * columns * TOKENS ** 0.5


def steps_of(key, shape, cuts, low, top_value):
    level, own = 1.0, jax.random.fold_in(key, 6)
    for axis_at, blocks in cuts:
        steps = jnp.exp(jax.random.uniform(jax.random.fold_in(own, axis_at), (blocks,), jnp.float32, low / len(cuts), top_value / len(cuts)))
        level = level * jnp.repeat(steps, shape[axis_at] // blocks).reshape([-1 if axis == axis_at else 1 for axis in range(len(shape))])
    return level


def gaussian(stream_key, shape, scale, most, cuts=(), kind=jnp.bfloat16):
    drawn = jax.random.normal(stream_key, shape, jnp.float32) * scale
    if len(cuts) > 0:
        drawn = steps_of(stream_key, shape, cuts, -0.22, 0.18) * drawn
    return jnp.clip(drawn, min=-most, max=most).astype(kind)


def setup_inputs(seed: int = 0) -> dict:
    key_of = jax.random.split(jax.random.key(seed), 20)
    enc_in = gaussian(key_of[0], (TOKENS, D), 1.0, 6.0, ((0, 32),))
    dec_in = gaussian(key_of[1], (TOKENS, D), 1.0, 6.0, ((0, 32),))
    segment_ids = draw_segment_ids(jax.random.fold_in(key_of[19], 71), 0)
    enc_cot = draw_enc_cot(jax.random.fold_in(key_of[19], 71), 0)
    dec_cot = draw_dec_cot(jax.random.fold_in(key_of[19], 71), 0)
    enc_qkv = gaussian(key_of[5], (3, D, D), D ** -0.5, 0.1875, ((1, 8),))
    enc_wo = gaussian(key_of[6], (D, D), (D // 16) ** -0.5, 0.75, ((0, 8),))
    enc_w_in = gaussian(key_of[7], (D, FF), D ** -0.5, 0.1875, ((0, 8),))
    enc_w_out = gaussian(key_of[8], (FF, D), FF ** -0.5, 0.09375, ((0, 8),))
    enc_gains = jnp.clip(1.0 + 0.15 * jax.random.normal(key_of[9], (2, D), jnp.float32), 0.25, 1.75).astype(jnp.bfloat16)
    dec_qkv = gaussian(key_of[10], (6, D, D), D ** -0.5, 0.1875, ((1, 8),))
    dec_wo = gaussian(key_of[11], (2, D, D), (D // 16) ** -0.5, 0.75, ((1, 8),))
    dec_w_in = gaussian(key_of[12], (D, FF), D ** -0.5, 0.1875, ((0, 8),))
    dec_w_out = gaussian(key_of[13], (FF, D), FF ** -0.5, 0.09375, ((0, 8),))
    dec_gains = jnp.clip(1.0 + 0.15 * jax.random.normal(key_of[14], (3, D), jnp.float32), 0.25, 1.75).astype(jnp.bfloat16)
    adapter_weights = gaussian(key_of[15], (4, D, ADAPT), ADAPT ** -0.5, 0.25, ((1, 32),), jnp.float32)
    adapter_momenta = draw_adapter_momenta(jax.random.fold_in(key_of[19], 71), 0)
    bias_in = gaussian(key_of[17], (2, ADAPT), 0.5, 3.0, (), jnp.float32)
    bias_out = gaussian(key_of[18], (2, D), 0.3, 2.0, (), jnp.float32)
    return {"enc_in": enc_in, "dec_in": dec_in, "segment_ids": segment_ids, "enc_cot": enc_cot, "dec_cot": dec_cot, "enc_qkv": enc_qkv, "enc_wo": enc_wo, "enc_w_in": enc_w_in, "enc_w_out": enc_w_out, "enc_gains": enc_gains, "dec_qkv": dec_qkv, "dec_wo": dec_wo, "dec_w_in": dec_w_in, "dec_w_out": dec_w_out, "dec_gains": dec_gains, "adapter_weights": adapter_weights, "adapter_momenta": adapter_momenta, "bias_in": bias_in, "bias_out": bias_out}


@jax.custom_vjp
def low(v):
    return lax.optimization_barrier(v.astype(jnp.bfloat16)).astype(jnp.float32)

@jax.custom_vjp
def low_back(v):
    return v

def low_keep(v):
    return (low(v), None)

def low_pass(kept, grad):
    return (grad,)

def back_keep(v):
    return (v, None)

def back_low(kept, grad):
    return (low(grad),)
low.defvjp(low_keep, low_pass)
low_back.defvjp(back_keep, back_low)
FULL_PRECISION = lax.Precision.HIGHEST
EPSILON = 1e-05
MASKED = -1e+30
NEWTON_LINEAR = 3.4445
NEWTON_QUADRATIC = -4.775
NEWTON_CUBIC = 2.0315
RATE = 0.7
DECAY = 0.5

def round_pair(tensor):
    return low(low_back(tensor))

def matmul(left_side, right_side):
    return jnp.dot(left_side, right_side, precision=FULL_PRECISION)

def layer_norm(tensor, gain_vector):
    average = lax.optimization_barrier(jnp.mean(tensor, axis=-1, keepdims=True))
    centred = tensor - average
    variance = lax.optimization_barrier(jnp.mean(centred * centred, axis=-1, keepdims=True))
    return centred * lax.rsqrt(variance + EPSILON) * gain_vector

def attention_one(queries, key_rows, value_rows, seg_ids, causal):
    length = queries.shape[0]
    heads_q = queries.reshape(length, -1, HD)
    heads_k = key_rows.reshape(length, -1, HD)
    heads_v = value_rows.reshape(length, -1, HD)
    scores = low_back(jnp.einsum('qhd,khd->hqk', heads_q, heads_k, precision=FULL_PRECISION) * HD ** (-0.5))
    allowed = seg_ids[:, None] == seg_ids[None, :]
    if causal:
        places = jnp.arange(length, dtype=jnp.int32)
        allowed = allowed & (places[None, :] <= places[:, None])
    weights = low(jax.nn.softmax(jnp.where(allowed[None], scores, MASKED), axis=-1))
    mixture = jnp.einsum('hqk,khd->qhd', weights, heads_v, precision=FULL_PRECISION)
    return round_pair(mixture.reshape(length, -1))

def attention_all(queries, key_rows, value_rows, segment_ids, causal):
    width = queries.shape[-1]

    def one_sequence(items):
        return attention_one(items[0], items[1], items[2], items[3], causal)
    blocks = lax.map(jax.checkpoint(one_sequence), (queries.reshape(-1, SEQ, width), key_rows.reshape(-1, SEQ, width), value_rows.reshape(-1, SEQ, width), segment_ids.reshape(-1, SEQ)))
    return blocks.reshape(-1, width)

def tail(hidden, up_proj, down_proj, adapt_in, adapt_out_t, bias_first, bias_second):
    hidden_low = low(hidden)
    upward = low_back(matmul(hidden_low, up_proj))
    ffn_out = low_back(matmul(low(jax.nn.gelu(upward, approximate=False)), down_proj))
    adapt_pre = low_back(matmul(hidden_low, adapt_in) + bias_first)
    adapt_out = low_back(matmul(low(jax.nn.gelu(adapt_pre, approximate=False)), adapt_out_t.T) + bias_second)
    return hidden + ffn_out + 4.0 * adapt_out

def reference(enc_in, dec_in, segment_ids, enc_cot, dec_cot, enc_qkv, enc_wo, enc_w_in, enc_w_out, enc_gains, dec_qkv, dec_wo, dec_w_in, dec_w_out, dec_gains, adapter_weights, adapter_momenta, bias_in, bias_out):
    enc_proj = enc_qkv.astype(jnp.float32)
    enc_out_proj = enc_wo.astype(jnp.float32)
    enc_up = enc_w_in.astype(jnp.float32)
    enc_down = enc_w_out.astype(jnp.float32)
    enc_gain_rows = enc_gains.astype(jnp.float32)
    dec_proj = dec_qkv.astype(jnp.float32)
    dec_out_proj = dec_wo.astype(jnp.float32)
    dec_up = dec_w_in.astype(jnp.float32)
    dec_down = dec_w_out.astype(jnp.float32)
    dec_gain_rows = dec_gains.astype(jnp.float32)

    def forward(enc_x, dec_x, adapters, first_bias, second_bias):
        adapter_low = low(adapters)
        enc_query = round_pair(matmul(enc_x, enc_proj[0]))
        enc_key = round_pair(matmul(enc_x, enc_proj[1]))
        enc_value = round_pair(matmul(enc_x, enc_proj[2]))
        enc_mix = attention_all(enc_query, enc_key, enc_value, segment_ids, False)
        enc_z1 = enc_x + low_back(matmul(enc_mix, enc_out_proj))
        enc_h1 = layer_norm(enc_z1, enc_gain_rows[0])
        encoded = layer_norm(tail(enc_h1, enc_up, enc_down, adapter_low[0], adapter_low[1], first_bias[0], second_bias[0]), enc_gain_rows[1])
        enc_low = low(encoded)
        self_query = round_pair(matmul(dec_x, dec_proj[0]))
        self_key = round_pair(matmul(dec_x, dec_proj[1]))
        self_value = round_pair(matmul(dec_x, dec_proj[2]))
        self_mix = attention_all(self_query, self_key, self_value, segment_ids, True)
        dec_z1 = dec_x + low_back(matmul(self_mix, dec_out_proj[0]))
        dec_y1 = layer_norm(dec_z1, dec_gain_rows[0])
        cross_query = round_pair(matmul(low(dec_y1), dec_proj[3]))
        cross_key = round_pair(matmul(enc_low, dec_proj[4]))
        cross_value = round_pair(matmul(enc_low, dec_proj[5]))
        cross_mix = attention_all(cross_query, cross_key, cross_value, segment_ids, False)
        dec_z2 = dec_y1 + low_back(matmul(cross_mix, dec_out_proj[1]))
        dec_y2 = layer_norm(dec_z2, dec_gain_rows[1])
        decoded = layer_norm(tail(dec_y2, dec_up, dec_down, adapter_low[2], adapter_low[3], first_bias[1], second_bias[1]), dec_gain_rows[2])
        return (encoded, decoded)
    outputs, pullback = jax.vjp(forward, enc_in.astype(jnp.float32), dec_in.astype(jnp.float32), adapter_weights, bias_in, bias_out)
    grad_enc, grad_dec, grad_adapters, grad_first, grad_second = pullback((enc_cot.astype(jnp.float32), dec_cot.astype(jnp.float32)))
    momenta = DECAY * adapter_momenta + grad_adapters
    frobenius = jnp.sqrt(lax.optimization_barrier(jnp.sum(momenta * momenta, axis=(1, 2))))[:, None, None]
    present_iterate = momenta / (frobenius + 1e-07)
    for iteration in range(NS_ITERS):
        gram_product = jnp.einsum('esn,esk->enk', present_iterate, present_iterate, precision=FULL_PRECISION)
        gram_squared = jnp.einsum('mab,mbc->mac', gram_product, gram_product, precision=FULL_PRECISION)
        present_iterate = NEWTON_LINEAR * present_iterate + jnp.einsum('wik,wkn->win', present_iterate, NEWTON_QUADRATIC * gram_product + NEWTON_CUBIC * gram_squared, precision=FULL_PRECISION)
    new_weights = adapter_weights - RATE * math.sqrt(max(1.0, D / ADAPT)) * present_iterate
    return (outputs[0].astype(jnp.bfloat16), outputs[1].astype(jnp.bfloat16), grad_enc, grad_dec, grad_first, grad_second, momenta, new_weights)
```

```python
import functools
import math

import jax
import jax.numpy as jnp
from jax import lax
from jax.experimental import pallas as pl
from jax.experimental.pallas import tpu as pltpu
from jax.sharding import PartitionSpec as P

D = 1024
HD = 64
ADAPT = 512
NS_ITERS = 5

EPSILON = 1e-05
MASKED = -1e30
NEWTON_LINEAR = 3.4445
NEWTON_QUADRATIC = -4.775
NEWTON_CUBIC = 2.0315
RATE = 0.7
DECAY = 0.5
FULL_PRECISION = lax.Precision.HIGHEST
LOG2E = 1.4426950408889634
PAIR = 2 * HD
VMEM_LIMIT = 56 * 1024 * 1024


def swap(array, axis, bit):
    return lax.ppermute(array, axis, [(i, i ^ bit) for i in range(lax.axis_size(axis))])


def bfloat(tensor):
    return tensor.astype(jnp.bfloat16)


def product(left_side, right_side):
    return jnp.dot(left_side, right_side, preferred_element_type=jnp.float32)


def contract(left_side, right_side, left_dim, right_dim):
    return lax.dot_general(
        left_side,
        right_side,
        (((left_dim,), (right_dim,)), ((), ())),
        preferred_element_type=jnp.float32,
    )


def product_t(left_side, right_side):
    return contract(left_side, right_side, 1, 1)


def product_rows(left_side, right_side):
    return contract(left_side, right_side, 0, 0)


def layer_norm(tensor, gain_vector):
    gain_full = gain_vector.astype(jnp.float32)
    average = jnp.mean(tensor, axis=-1, keepdims=True)
    centred = tensor - average
    inverse = lax.rsqrt(jnp.mean(centred * centred, axis=-1, keepdims=True) + EPSILON)
    normed = centred * inverse
    return (normed * gain_full, (normed, inverse, gain_full))


def norm_back(grad_out, stored):
    normed, inverse, gain_full = stored
    scaled = grad_out * gain_full
    return inverse * (
        scaled
        - jnp.mean(scaled, axis=-1, keepdims=True)
        - normed * jnp.mean(scaled * normed, axis=-1, keepdims=True)
    )


def gelu_both(tensor):
    phi = 0.5 * (1.0 + lax.erf(tensor * 0.7071067811865476))
    slope = phi + tensor * jnp.exp(-0.5 * tensor * tensor) * 0.3989422804014327
    return tensor * phi, slope


def fill_bias(half_ref, qid_ref, kid_own_ref, kid_far_ref, bias_ref, causal):
    rows = qid_ref.shape[1]
    qid = qid_ref[...]
    for part, kid_ref in enumerate((kid_own_ref, kid_far_ref)):
        allowed = kid_ref[...] == qid
        if causal:
            if part == 0:
                key_at = lax.broadcasted_iota(jnp.int32, (rows, rows), 0)
                query_at = lax.broadcasted_iota(jnp.int32, (rows, rows), 1)
                allowed = allowed & (key_at <= query_at)
            else:
                allowed = allowed & (half_ref[0] == 1)
        bias_ref[pl.ds(part * rows, rows), :] = jnp.where(allowed, 0.0, MASKED)


def head_mask(rows, head):
    return lax.broadcasted_iota(jnp.int32, (rows, PAIR), 1) // HD == head


def attend_kernel(
    causal,
    chunk,
    half_ref,
    qid_ref,
    kid_own_ref,
    kid_far_ref,
    q_ref,
    k_own_ref,
    k_far_ref,
    v_own_ref,
    v_far_ref,
    out_ref,
    lse_ref,
    bias_ref,
    score_ref,
):
    rows = q_ref.shape[0]

    @pl.when(pl.program_id(0) == 0)
    def _():
        fill_bias(half_ref, qid_ref, kid_own_ref, kid_far_ref, bias_ref, causal)

    queries = q_ref[...] * 0.125
    steps = [
        (part, at)
        for part in range(2)
        for at in range(0, rows, chunk)
    ]
    keys = (k_own_ref, k_far_ref)
    values = (v_own_ref, v_far_ref)
    mixes = []
    for head in range(2):
        q_head = jnp.where(head_mask(rows, head), queries, jnp.zeros_like(queries))
        peak = None
        for part, at in steps:
            place = pl.ds(part * rows + at, chunk)
            scores = product_t(keys[part][pl.ds(at, chunk), :], q_head)
            scores = scores * LOG2E + bias_ref[place, :]
            score_ref[head, place, :] = scores
            top = jnp.max(scores, axis=0, keepdims=True)
            peak = top if peak is None else jnp.maximum(peak, top)
        total, mix = None, None
        for part, at in steps:
            place = pl.ds(part * rows + at, chunk)
            raised = jnp.exp2(score_ref[head, place, :] - peak)
            share = jnp.sum(raised, axis=0, keepdims=True)
            piece = product_rows(values[part][pl.ds(at, chunk), :], bfloat(raised))
            total = share if total is None else total + share
            mix = piece if mix is None else mix + piece
        mixes.append((mix * (1.0 / total))[head * HD : (head + 1) * HD, :])
        lse_ref[0, pl.ds(head, 1), :] = peak + jnp.log2(total)
    out_ref[...] = bfloat(jnp.concatenate(mixes, axis=0).T)


def attend_back_kernel(
    causal,
    chunk,
    half_ref,
    qid_ref,
    kid_own_ref,
    kid_far_ref,
    q_ref,
    k_own_ref,
    k_far_ref,
    v_own_ref,
    v_far_ref,
    out_ref,
    grad_ref,
    lse_ref,
    dq_ref,
    dk_own_ref,
    dk_far_ref,
    dv_own_ref,
    dv_far_ref,
    bias_ref,
):
    rows = q_ref.shape[0]

    @pl.when(pl.program_id(0) == 0)
    def _():
        fill_bias(half_ref, qid_ref, kid_own_ref, kid_far_ref, bias_ref, causal)

    queries = q_ref[...] * 0.125
    grads = grad_ref[...]
    products = (grads.astype(jnp.float32) * out_ref[...].astype(jnp.float32)).T
    q_heads, g_heads, deltas, lses = [], [], [], []
    for head in range(2):
        chosen = head_mask(rows, head)
        q_heads.append(jnp.where(chosen, queries, jnp.zeros_like(queries)))
        g_heads.append(jnp.where(chosen, grads, jnp.zeros_like(grads)))
        deltas.append(jnp.sum(products[head * HD : (head + 1) * HD, :], axis=0, keepdims=True))
        lses.append(lse_ref[0, pl.ds(head, 1), :])
    grad_q = [None, None]
    for part in range(2):
        key_ref = (k_own_ref, k_far_ref)[part]
        value_ref = (v_own_ref, v_far_ref)[part]
        dk_ref = (dk_own_ref, dk_far_ref)[part]
        dv_ref = (dv_own_ref, dv_far_ref)[part]
        for at in range(0, rows, chunk):
            here = pl.ds(at, chunk)
            keys, values = key_ref[here, :], value_ref[here, :]
            grad_k, grad_v = None, None
            for head in range(2):
                scores = product_t(keys, q_heads[head])
                bias = bias_ref[pl.ds(part * rows + at, chunk), :]
                weights = jnp.exp2(scores * LOG2E + (bias - lses[head]))
                grad_w = product_t(values, g_heads[head])
                grad_s = bfloat(weights * (grad_w - deltas[head]))
                piece_v = product(bfloat(weights), g_heads[head])
                piece_k = product(grad_s, q_heads[head])
                piece_q = product_rows(keys, grad_s)
                grad_v = piece_v if grad_v is None else grad_v + piece_v
                grad_k = piece_k if grad_k is None else grad_k + piece_k
                grad_q[head] = piece_q if grad_q[head] is None else grad_q[head] + piece_q
            dk_ref[here, :] = grad_k.astype(dk_ref.dtype)
            dv_ref[here, :] = grad_v.astype(dv_ref.dtype)
    joined = jnp.concatenate([grad_q[h][h * HD : (h + 1) * HD, :] for h in range(2)], axis=0)
    dq_ref[...] = bfloat((joined * 0.125).T)


def attention_specs(rows):
    whole = lambda shape: pl.BlockSpec(shape, lambda i: (0,) * len(shape))
    columns = pl.BlockSpec((rows, PAIR), lambda i: (0, i))
    fixed = [
        pl.BlockSpec(memory_space=pltpu.SMEM),
        whole((1, rows)),
        whole((rows, 1)),
        whole((rows, 1)),
    ]
    return fixed, columns, pl.BlockSpec((1, 8, rows), lambda i: (i, 0, 0))


def attend(places, queries, keys, values, causal):
    rows, width = queries.shape
    pairs = width // PAIR
    fixed, columns, stat = attention_specs(rows)
    return pl.pallas_call(
        functools.partial(attend_kernel, causal, 256),
        grid=(pairs,),
        in_specs=fixed + [columns] * 5,
        out_specs=[columns, stat],
        out_shape=[
            jax.ShapeDtypeStruct((rows, width), jnp.bfloat16),
            jax.ShapeDtypeStruct((pairs, 8, rows), jnp.float32),
        ],
        scratch_shapes=[
            pltpu.VMEM((2 * rows, rows), jnp.float32),
            pltpu.VMEM((2, 2 * rows, rows), jnp.float32),
        ],
        compiler_params=pltpu.CompilerParams(vmem_limit_bytes=VMEM_LIMIT),
        cost_estimate=pl.CostEstimate(
            flops=32 * rows * rows * width, bytes_accessed=12 * rows * width, transcendentals=0
        ),
    )(*places, queries, *keys, *values)


def attend_back(places, grad_out, queries, keys, values, mix, lse, causal):
    rows, width = queries.shape
    pairs = width // PAIR
    fixed, columns, stat = attention_specs(rows)
    return pl.pallas_call(
        functools.partial(attend_back_kernel, causal, 256),
        grid=(pairs,),
        in_specs=fixed + [columns] * 7 + [stat],
        out_specs=[columns] * 5,
        out_shape=[
            jax.ShapeDtypeStruct((rows, width), jnp.bfloat16),
            jax.ShapeDtypeStruct((rows, width), jnp.float32),
            jax.ShapeDtypeStruct((rows, width), jnp.bfloat16),
            jax.ShapeDtypeStruct((rows, width), jnp.float32),
            jax.ShapeDtypeStruct((rows, width), jnp.bfloat16),
        ],
        scratch_shapes=[pltpu.VMEM((2 * rows, rows), jnp.float32)],
        compiler_params=pltpu.CompilerParams(vmem_limit_bytes=VMEM_LIMIT),
        cost_estimate=pl.CostEstimate(
            flops=80 * rows * rows * width, bytes_accessed=24 * rows * width, transcendentals=0
        ),
    )(*places, queries, *keys, *values, mix, grad_out, lse)


def tail_forward(hidden, up_proj, down_proj, adapt_in, adapt_out_t, bias_first, bias_second):
    hidden_low = bfloat(hidden)
    inner, up_slope = gelu_both(product(hidden_low, up_proj))
    ffn_out = product(bfloat(inner), down_proj)
    adapted, pre_slope = gelu_both(product(hidden_low, adapt_in) + bias_first)
    adapt_low = bfloat(adapted)
    adapt_out = product_t(adapt_low, adapt_out_t) + bias_second
    return (
        hidden + ffn_out + 4.0 * adapt_out,
        (hidden_low, up_slope, pre_slope, adapt_low),
    )


def tail_back(grad_total, stored, up_proj, down_proj, adapt_in, adapt_out_t):
    hidden_low, up_slope, pre_slope, adapt_low = stored
    grad_low = bfloat(grad_total)
    grad_up_low = bfloat(product_t(grad_low, down_proj) * up_slope)
    grad_adapt = bfloat(4.0 * grad_total)
    grad_out_matrix = product_rows(grad_adapt, adapt_low)
    grad_second = jnp.sum(grad_adapt.astype(jnp.float32), axis=0)
    grad_pre_low = bfloat(product(grad_adapt, adapt_out_t) * pre_slope)
    grad_in_matrix = product_rows(hidden_low, grad_pre_low)
    grad_first = jnp.sum(grad_pre_low.astype(jnp.float32), axis=0)
    grad_hidden = grad_total + product_t(grad_up_low, up_proj) + product_t(grad_pre_low, adapt_in)
    return (grad_hidden, grad_in_matrix, grad_out_matrix, grad_first, grad_second)


def halve(array, dim, axis, bit):
    mine = (lax.axis_index(axis) // bit) % 2
    keep = lax.dynamic_index_in_dim(array, mine, dim, keepdims=False)
    send = lax.dynamic_index_in_dim(array, 1 - mine, dim, keepdims=False)
    return keep + swap(send, axis, bit)


def axis_bits(axis):
    return [1 << b for b in range(lax.axis_size(axis).bit_length() - 1)]


def scatter_wide(first, second):
    bits = axis_bits("wide")
    results = []
    for array, order in ((first, bits[:1] + bits[1:]), (second, bits[:1] + bits[:0:-1])):
        array = array.reshape([2] * len(bits) + [-1, array.shape[-1]])
        left = list(reversed(bits))
        for bit in order:
            array = halve(array, left.index(bit), "wide", bit)
            left.remove(bit)
        results.append(array)
    return results


def gather_any_order(array, axis):
    blocks = array[None]
    for bit in axis_bits(axis):
        blocks = jnp.concatenate([blocks, swap(blocks, axis, bit)])
    return blocks


def sum_all(array):
    for axis in ("wide", "narrow"):
        for bit in axis_bits(axis):
            array = array + swap(array, axis, bit)
    return array


def exact(left_side, right_side):
    return jnp.dot(left_side, right_side, precision=FULL_PRECISION)


def newton_schulz(gram):
    eye = jnp.eye(gram.shape[0], dtype=jnp.float32)
    factor = None
    for step in range(NS_ITERS):
        squared = exact(gram, gram)
        poly = NEWTON_LINEAR * eye + NEWTON_QUADRATIC * gram + NEWTON_CUBIC * squared
        factor = poly if factor is None else exact(factor, poly)
        if step < NS_ITERS - 1:
            gram = exact(exact(gram, poly), poly)
    return factor


def shards(
    enc_in,
    dec_in,
    segment_ids,
    enc_cot,
    dec_cot,
    enc_qkv,
    enc_wo,
    enc_w_in,
    enc_w_out,
    enc_gains,
    dec_qkv,
    dec_wo,
    dec_w_in,
    dec_w_out,
    dec_gains,
    adapter_weights,
    adapter_momenta,
    bias_in,
    bias_out,
):
    adapters = lax.all_gather(bfloat(adapter_weights), ("wide", "narrow"), axis=1, tiled=True)
    enc_proj, enc_out_proj, enc_up, enc_down, enc_gain_rows = (
        lax.all_gather(enc_qkv, "wide", axis=1, tiled=True),
        lax.all_gather(enc_wo, "wide", axis=0, tiled=True),
        lax.all_gather(enc_w_in, "wide", axis=0, tiled=True),
        lax.all_gather(enc_w_out, "wide", axis=0, tiled=True),
        lax.all_gather(enc_gains, "wide", axis=1, tiled=True),
    )
    dec_proj, dec_out_proj, dec_up, dec_down, dec_gain_rows = (
        lax.all_gather(dec_qkv, "wide", axis=1, tiled=True),
        lax.all_gather(dec_wo, "wide", axis=1, tiled=True),
        lax.all_gather(dec_w_in, "wide", axis=0, tiled=True),
        lax.all_gather(dec_w_out, "wide", axis=0, tiled=True),
        lax.all_gather(dec_gains, "wide", axis=1, tiled=True),
    )
    partner = lambda array: swap(array, "narrow", 1)
    other_ids = partner(segment_ids)
    rows = enc_in.shape[0]
    half = (lax.axis_index("narrow") % 2).astype(jnp.int32).reshape(1)
    places = (half, segment_ids.reshape(1, rows), segment_ids.reshape(rows, 1), other_ids.reshape(rows, 1))

    enc_query = bfloat(product(enc_in, enc_proj[0]))
    enc_key = bfloat(product(enc_in, enc_proj[1]))
    enc_value = bfloat(product(enc_in, enc_proj[2]))
    self_query = bfloat(product(dec_in, dec_proj[0]))
    self_key = bfloat(product(dec_in, dec_proj[1]))
    self_value = bfloat(product(dec_in, dec_proj[2]))
    enc_keys, enc_values = (enc_key, partner(enc_key)), (enc_value, partner(enc_value))
    self_keys, self_values = (self_key, partner(self_key)), (self_value, partner(self_value))

    enc_mix, enc_lse = attend(places, enc_query, enc_keys, enc_values, False)
    enc_z1 = enc_in.astype(jnp.float32) + product(enc_mix, enc_out_proj)
    enc_h1, enc_norm1 = layer_norm(enc_z1, enc_gain_rows[0])
    enc_z2, enc_tail = tail_forward(
        enc_h1, enc_up, enc_down, adapters[0], adapters[1], bias_in[0], bias_out[0]
    )
    encoded, enc_norm2 = layer_norm(enc_z2, enc_gain_rows[1])
    enc_low = bfloat(encoded)
    cross_key = bfloat(product(enc_low, dec_proj[4]))
    cross_value = bfloat(product(enc_low, dec_proj[5]))
    cross_keys, cross_values = (cross_key, partner(cross_key)), (cross_value, partner(cross_value))

    self_mix, self_lse = attend(places, self_query, self_keys, self_values, True)
    dec_z1 = dec_in.astype(jnp.float32) + product(self_mix, dec_out_proj[0])
    dec_y1, dec_norm1 = layer_norm(dec_z1, dec_gain_rows[0])
    cross_query = bfloat(product(bfloat(dec_y1), dec_proj[3]))
    cross_mix, cross_lse = attend(places, cross_query, cross_keys, cross_values, False)
    dec_z2 = dec_y1 + product(cross_mix, dec_out_proj[1])
    dec_y2, dec_norm2 = layer_norm(dec_z2, dec_gain_rows[1])
    dec_z3, dec_tail = tail_forward(
        dec_y2, dec_up, dec_down, adapters[2], adapters[3], bias_in[1], bias_out[1]
    )
    decoded, dec_norm3 = layer_norm(dec_z3, dec_gain_rows[2])

    grad_z3 = norm_back(dec_cot.astype(jnp.float32), dec_norm3)
    grad_y2, grad_dec_down, grad_dec_up, grad_dec_first, grad_dec_second = tail_back(
        grad_z3, dec_tail, dec_up, dec_down, adapters[2], adapters[3]
    )
    dec_sums = scatter_wide(grad_dec_down, grad_dec_up)
    grad_z2 = norm_back(grad_y2, dec_norm2)
    grad_cross_mix = bfloat(product_t(bfloat(grad_z2), dec_out_proj[1]))
    cross_back = attend_back(
        places, grad_cross_mix, cross_query, cross_keys, cross_values, cross_mix, cross_lse, False
    )
    own = lambda near, far: bfloat(near + partner(far).astype(jnp.float32))
    cross_k_low = own(cross_back[1], cross_back[2])
    cross_v_low = own(cross_back[3], cross_back[4])
    grad_encoded = (
        enc_cot.astype(jnp.float32)
        + product_t(cross_k_low, dec_proj[4])
        + product_t(cross_v_low, dec_proj[5])
    )
    grad_ez2 = norm_back(grad_encoded, enc_norm2)
    grad_eh1, grad_enc_down, grad_enc_up, grad_enc_first, grad_enc_second = tail_back(
        grad_ez2, enc_tail, enc_up, enc_down, adapters[0], adapters[1]
    )
    enc_sums = scatter_wide(grad_enc_down, grad_enc_up)

    repeat = lax.axis_size("narrow") // 4
    spread = lambda array: jnp.repeat(array, repeat, axis=0) if repeat > 1 else array
    stacked = spread(jnp.stack(enc_sums + dec_sums))
    for bit in reversed(axis_bits("narrow")):
        stacked = halve(stacked.reshape(2, -1, *stacked.shape[1:]), 0, "narrow", bit)
    summed = stacked[0]
    to_matrix = lambda array: lax.all_to_all(
        spread(array), "narrow", split_axis=0, concat_axis=1, tiled=True
    )[0]
    to_rows = lambda array: lax.all_to_all(
        array[None], "narrow", split_axis=1, concat_axis=0, tiled=True
    )[::repeat]
    momentum = DECAY * to_matrix(adapter_momenta) + summed
    new_momenta = to_rows(momentum)
    everything = gather_any_order(momentum, "wide").reshape(-1, ADAPT)
    gram = lax.dot_general(
        everything, everything, (((0,), (0,)), ((), ())), precision=FULL_PRECISION
    )
    scale = 1.0 / (jnp.sqrt(jnp.trace(gram)) + 1e-07)
    factor = newton_schulz(gram * (scale * scale))
    orthogonal = to_rows(exact(momentum * scale, factor))
    new_weights = adapter_weights - RATE * math.sqrt(max(1.0, D / ADAPT)) * orthogonal

    grad_y1 = grad_z2 + product_t(cross_back[0], dec_proj[3])
    grad_z1 = norm_back(grad_y1, dec_norm1)
    grad_self_mix = bfloat(product_t(bfloat(grad_z1), dec_out_proj[0]))
    self_back = attend_back(
        places, grad_self_mix, self_query, self_keys, self_values, self_mix, self_lse, True
    )
    grad_dec = (
        grad_z1
        + product_t(self_back[0], dec_proj[0])
        + product_t(own(self_back[1], self_back[2]), dec_proj[1])
        + product_t(own(self_back[3], self_back[4]), dec_proj[2])
    )
    grad_ez1 = norm_back(grad_eh1, enc_norm1)
    grad_enc_mix = bfloat(product_t(bfloat(grad_ez1), enc_out_proj))
    enc_back = attend_back(
        places, grad_enc_mix, enc_query, enc_keys, enc_values, enc_mix, enc_lse, False
    )
    grad_enc = (
        grad_ez1
        + product_t(enc_back[0], enc_proj[0])
        + product_t(own(enc_back[1], enc_back[2]), enc_proj[1])
        + product_t(own(enc_back[3], enc_back[4]), enc_proj[2])
    )

    biases = sum_all(
        jnp.concatenate([grad_enc_first, grad_dec_first, grad_enc_second, grad_dec_second])
    )
    place = lax.axis_index("wide") * lax.axis_size("narrow") + lax.axis_index("narrow")
    devices = lax.axis_size("wide") * lax.axis_size("narrow")
    slices = lambda array: lax.dynamic_slice_in_dim(
        array.reshape(2, -1), place * (array.size // 2 // devices), array.size // 2 // devices, 1
    )
    grad_bias_in, grad_bias_out = slices(biases[: 2 * ADAPT]), slices(biases[2 * ADAPT :])
    return (
        enc_low,
        bfloat(decoded),
        grad_enc,
        grad_dec,
        grad_bias_in,
        grad_bias_out,
        new_momenta,
        new_weights,
    )


def solution(mesh):
    both = ("wide", "narrow")
    tokens = P(both, None)
    rows_first, rows_second = P("wide", None), P(None, "wide", None)
    adapters = P(None, both, None)
    in_specs = (
        tokens,
        tokens,
        P(both),
        tokens,
        tokens,
        rows_second,
        rows_first,
        rows_first,
        rows_first,
        P(None, "wide"),
        rows_second,
        rows_second,
        rows_first,
        rows_first,
        P(None, "wide"),
        adapters,
        adapters,
        P(),
        P(),
    )
    out_specs = (
        tokens,
        tokens,
        tokens,
        tokens,
        P(None, both),
        P(None, both),
        adapters,
        adapters,
    )
    return jax.shard_map(shards, mesh=mesh, in_specs=in_specs, out_specs=out_specs, check_vma=False)
```

```python
import functools
import math

import jax
import jax.numpy as jnp
from jax import lax
from jax.experimental import pallas as pl
from jax.experimental.pallas import tpu as pltpu
from jax.sharding import PartitionSpec as P

D = 1024
HD = 64
ADAPT = 512
NS_ITERS = 5

EPSILON = 1e-05
MASKED = -1e30
NEWTON_LINEAR = 3.4445
NEWTON_QUADRATIC = -4.775
NEWTON_CUBIC = 2.0315
RATE = 0.7
DECAY = 0.5
LOG2E = 1.4426950408889634
PAIR = 2 * HD
VMEM_LIMIT = 58 * 1024 * 1024
MESH = pl.DeviceIdType.MESH


def swap(array, axis, bit):
    return lax.ppermute(array, axis, [(i, i ^ bit) for i in range(lax.axis_size(axis))])


def bfloat(tensor):
    return tensor.astype(jnp.bfloat16)


def product(left_side, right_side):
    return jnp.dot(left_side, right_side, preferred_element_type=jnp.float32)


def contract(left_side, right_side, left_dim, right_dim):
    return lax.dot_general(
        left_side,
        right_side,
        (((left_dim,), (right_dim,)), ((), ())),
        preferred_element_type=jnp.float32,
    )


def product_t(left_side, right_side):
    return contract(left_side, right_side, 1, 1)


def product_rows(left_side, right_side):
    return contract(left_side, right_side, 0, 0)


def gelu_both(tensor):
    phi = 0.5 * (1.0 + lax.erf(tensor * 0.7071067811865476))
    slope = phi + tensor * jnp.exp(-0.5 * tensor * tensor) * 0.3989422804014327
    return tensor * phi, slope


def fill_bias(half_ref, qid_ref, kid_own_ref, kid_far_ref, bias_ref, causal):
    rows = qid_ref.shape[1]
    qid = qid_ref[...]
    for part, kid_ref in enumerate((kid_own_ref, kid_far_ref)):
        allowed = kid_ref[...] == qid
        if causal:
            if part == 0:
                key_at = lax.broadcasted_iota(jnp.int32, (rows, rows), 0)
                query_at = lax.broadcasted_iota(jnp.int32, (rows, rows), 1)
                allowed = allowed & (key_at <= query_at)
            else:
                allowed = allowed & (half_ref[0] == 1)
        bias_ref[pl.ds(part * rows, rows), :] = jnp.where(allowed, 0.0, MASKED)


def head_mask(rows, head):
    return lax.broadcasted_iota(jnp.int32, (rows, PAIR), 1) // HD == head


def attend_kernel(
    causal,
    chunk,
    half_ref,
    qid_ref,
    kid_own_ref,
    kid_far_ref,
    q_ref,
    k_own_ref,
    k_far_ref,
    v_own_ref,
    v_far_ref,
    out_ref,
    lse_ref,
    bias_ref,
    score_ref,
):
    rows = q_ref.shape[0]

    @pl.when(pl.program_id(0) == 0)
    def _():
        fill_bias(half_ref, qid_ref, kid_own_ref, kid_far_ref, bias_ref, causal)

    queries = q_ref[...] * 0.125
    steps = [
        (part, at)
        for part in range(2)
        for at in range(0, rows, chunk)
    ]
    keys = (k_own_ref, k_far_ref)
    values = (v_own_ref, v_far_ref)
    mixes = []
    for head in range(2):
        q_head = jnp.where(head_mask(rows, head), queries, jnp.zeros_like(queries))
        peak = None
        for part, at in steps:
            place = pl.ds(part * rows + at, chunk)
            scores = product_t(keys[part][pl.ds(at, chunk), :], q_head)
            scores = scores * LOG2E + bias_ref[place, :]
            score_ref[head, place, :] = scores
            top = jnp.max(scores, axis=0, keepdims=True)
            peak = top if peak is None else jnp.maximum(peak, top)
        total, mix = None, None
        for part, at in steps:
            place = pl.ds(part * rows + at, chunk)
            raised = jnp.exp2(score_ref[head, place, :] - peak)
            share = jnp.sum(raised, axis=0, keepdims=True)
            piece = product_rows(values[part][pl.ds(at, chunk), :], bfloat(raised))
            total = share if total is None else total + share
            mix = piece if mix is None else mix + piece
        mixes.append((mix * (1.0 / total))[head * HD : (head + 1) * HD, :])
        lse_ref[0, pl.ds(head, 1), :] = peak + jnp.log2(total)
    out_ref[...] = bfloat(jnp.concatenate(mixes, axis=0).T)


def attend_back_kernel(
    causal,
    chunk,
    half_ref,
    qid_ref,
    kid_own_ref,
    kid_far_ref,
    q_ref,
    k_own_ref,
    k_far_ref,
    v_own_ref,
    v_far_ref,
    out_ref,
    grad_ref,
    lse_ref,
    dq_ref,
    dk_own_ref,
    dk_far_ref,
    dv_own_ref,
    dv_far_ref,
    bias_ref,
):
    rows = q_ref.shape[0]

    @pl.when(pl.program_id(0) == 0)
    def _():
        fill_bias(half_ref, qid_ref, kid_own_ref, kid_far_ref, bias_ref, causal)

    queries = q_ref[...] * 0.125
    grads = grad_ref[...]
    products = (grads.astype(jnp.float32) * out_ref[...].astype(jnp.float32)).T
    q_heads, g_heads, deltas, lses = [], [], [], []
    for head in range(2):
        chosen = head_mask(rows, head)
        q_heads.append(jnp.where(chosen, queries, jnp.zeros_like(queries)))
        g_heads.append(jnp.where(chosen, grads, jnp.zeros_like(grads)))
        deltas.append(jnp.sum(products[head * HD : (head + 1) * HD, :], axis=0, keepdims=True))
        lses.append(lse_ref[0, pl.ds(head, 1), :])
    grad_q = [None, None]
    for part in range(2):
        key_ref = (k_own_ref, k_far_ref)[part]
        value_ref = (v_own_ref, v_far_ref)[part]
        dk_ref = (dk_own_ref, dk_far_ref)[part]
        dv_ref = (dv_own_ref, dv_far_ref)[part]
        for at in range(0, rows, chunk):
            here = pl.ds(at, chunk)
            keys, values = key_ref[here, :], value_ref[here, :]
            grad_k, grad_v = None, None
            for head in range(2):
                scores = product_t(keys, q_heads[head])
                bias = bias_ref[pl.ds(part * rows + at, chunk), :]
                weights = jnp.exp2(scores * LOG2E + (bias - lses[head]))
                grad_w = product_t(values, g_heads[head])
                grad_s = bfloat(weights * (grad_w - deltas[head]))
                piece_v = product(bfloat(weights), g_heads[head])
                piece_k = product(grad_s, q_heads[head])
                piece_q = product_rows(keys, grad_s)
                grad_v = piece_v if grad_v is None else grad_v + piece_v
                grad_k = piece_k if grad_k is None else grad_k + piece_k
                grad_q[head] = piece_q if grad_q[head] is None else grad_q[head] + piece_q
            dk_ref[here, :] = grad_k.astype(dk_ref.dtype)
            dv_ref[here, :] = grad_v.astype(dv_ref.dtype)
    joined = jnp.concatenate([grad_q[h][h * HD : (h + 1) * HD, :] for h in range(2)], axis=0)
    dq_ref[...] = bfloat((joined * 0.125).T)


def attention_specs(rows):
    whole = lambda shape: pl.BlockSpec(shape, lambda i: (0,) * len(shape))
    columns = pl.BlockSpec((rows, PAIR), lambda i: (0, i))
    fixed = [
        pl.BlockSpec(memory_space=pltpu.SMEM),
        whole((1, rows)),
        whole((rows, 1)),
        whole((rows, 1)),
    ]
    return fixed, columns, pl.BlockSpec((1, 8, rows), lambda i: (i, 0, 0))


def attend(places, queries, keys, values, causal):
    rows, width = queries.shape
    pairs = width // PAIR
    fixed, columns, stat = attention_specs(rows)
    return pl.pallas_call(
        functools.partial(attend_kernel, causal, 256),
        grid=(pairs,),
        in_specs=fixed + [columns] * 5,
        out_specs=[columns, stat],
        out_shape=[
            jax.ShapeDtypeStruct((rows, width), jnp.bfloat16),
            jax.ShapeDtypeStruct((pairs, 8, rows), jnp.float32),
        ],
        scratch_shapes=[
            pltpu.VMEM((2 * rows, rows), jnp.float32),
            pltpu.VMEM((2, 2 * rows, rows), jnp.float32),
        ],
        compiler_params=pltpu.CompilerParams(vmem_limit_bytes=VMEM_LIMIT),
        cost_estimate=pl.CostEstimate(
            flops=32 * rows * rows * width, bytes_accessed=12 * rows * width, transcendentals=0
        ),
    )(*places, queries, *keys, *values)


def attend_back(places, grad_out, queries, keys, values, mix, lse, causal):
    rows, width = queries.shape
    pairs = width // PAIR
    fixed, columns, stat = attention_specs(rows)
    return pl.pallas_call(
        functools.partial(attend_back_kernel, causal, 256),
        grid=(pairs,),
        in_specs=fixed + [columns] * 7 + [stat],
        out_specs=[columns] * 5,
        out_shape=[
            jax.ShapeDtypeStruct((rows, width), jnp.bfloat16),
        ]
        * 5,
        scratch_shapes=[pltpu.VMEM((2 * rows, rows), jnp.float32)],
        compiler_params=pltpu.CompilerParams(vmem_limit_bytes=VMEM_LIMIT),
        cost_estimate=pl.CostEstimate(
            flops=80 * rows * rows * width, bytes_accessed=24 * rows * width, transcendentals=0
        ),
    )(*places, queries, *keys, *values, mix, grad_out, lse)


def flipped(me, bits):
    place = me
    bit = 1
    while bit <= bits:
        if bits & bit:
            place = place + bit * (1 - 2 * lax.rem(lax.div(me, bit), 2))
        bit *= 2
    return place


class Loader:
    def __init__(self, sems):
        self.local, self.send, self.recv, self.stored = sems
        self.copies, self.stores = [], []
        self.me = lax.axis_index("wide")
        self.sibling = {"wide": flipped(self.me, 1)}
        barrier = pltpu.get_barrier_semaphore()
        pl.semaphore_signal(barrier, inc=1, device_id=self.sibling, device_id_type=MESH)
        pl.semaphore_wait(barrier, 1)

    def fetch(self, pieces, offset, height, target, columns=slice(None)):
        block = len(self.copies)
        copies = []
        for i, piece in enumerate(pieces):
            at = pl.multiple_of(flipped(self.me, 2 * i) * height, height)
            source = piece.at[pl.ds(offset, height), columns]
            place = target.at[pl.ds(at, height), columns]
            near = pltpu.make_async_copy(source, place, self.local.at[block, i])
            far = pltpu.make_async_remote_copy(
                source,
                place,
                self.send.at[block, i],
                self.recv.at[block, i],
                device_id=self.sibling,
                device_id_type=MESH,
            )
            near.start()
            far.start()
            copies.append((near, far))
        self.copies.append(copies)
        return block

    def arrived(self, block, target, out):
        for near, far in self.copies[block]:
            near.wait()
            far.wait_recv()
        store = pltpu.make_async_copy(target, out, self.stored.at[block])
        store.start()
        self.stores.append(store)

    def finish(self):
        for copies in self.copies:
            for _, far in copies:
                far.wait_send()
        for store in self.stores:
            store.wait()


def loader_sems(blocks, pieces):
    dma = pltpu.SemaphoreType.DMA
    return [dma((blocks, pieces))] * 3 + [dma((blocks,))]


def load(weights, targets, sem):
    for j, (weight, target) in enumerate(zip(weights, targets)):
        pltpu.make_async_copy(weight, target, sem.at[j]).start()


def loaded(target, sem):
    pltpu.make_async_copy(target, target, sem).wait()


def tiles(body, width, step):
    @pl.loop(0, width // step)
    def _(i):
        body(pl.ds(pl.multiple_of(i * step, step), step))


ROWS = 64
TILE = 256
STAT = 128


def normalise(z_ref, n_ref, r_ref, gain, low_ref):
    def body(rows):
        z = z_ref[rows, :]
        centred = z - jnp.mean(z, axis=-1, keepdims=True)
        inverse = lax.rsqrt(jnp.mean(centred * centred, axis=-1, keepdims=True) + EPSILON)
        normed = centred * inverse
        n_ref[rows, :] = normed
        r_ref[rows, :] = jnp.broadcast_to(inverse, (ROWS, STAT))
        if low_ref is not None:
            low_ref[rows, :] = bfloat(normed * gain)

    tiles(body, z_ref.shape[0], ROWS)


def normalise_back(read_grad, n_ref, r_ref, gain, dz_ref, low_ref):
    def body(rows):
        scaled = read_grad(rows) * gain
        normed = n_ref[rows, :]
        dz = r_ref[rows, :][:, :1] * (
            scaled
            - jnp.mean(scaled, axis=-1, keepdims=True)
            - normed * jnp.mean(scaled * normed, axis=-1, keepdims=True)
        )
        dz_ref[rows, :] = dz
        low_ref[rows, :] = bfloat(dz)

    tiles(body, n_ref.shape[0], ROWS)


def project_kernel(n, height, offsets, x_ref, far_ref, *refs):
    count = len(offsets)
    pieces, outs, full, (weight, *sems) = refs[:n], refs[n:-6], refs[-6], refs[-5:]
    loader = Loader(sems)
    for j, offset in enumerate(offsets):
        loader.fetch(pieces, offset, height, weight.at[j])
    for j in range(count):
        loader.arrived(j, weight.at[j], full.at[j])
        far = outs[count + j - (count - 2)] if j >= count - 2 else None

        def body(columns):
            outs[j][:, columns] = bfloat(product(x_ref[...], weight[j, :, columns]))
            if far is not None:
                far[:, columns] = bfloat(product(far_ref[...], weight[j, :, columns]))

        tiles(body, outs[j].shape[1], TILE)
    loader.finish()


def settle_kernel(n, height, wo_at, q_at, gain_rows, x_ref, mix_ref, gains_ref, *refs):
    pieces, refs = refs[:n], refs[n:]
    if q_at is None:
        n_ref, r_ref, full, weight, z_ref, *sems = refs
        low_ref = None
    else:
        n_ref, r_ref, q_ref, full, weight, z_ref, low_ref, *sems = refs
    loader = Loader(sems)
    loader.fetch(pieces, wo_at, height, weight.at[0])
    if q_at is not None:
        loader.fetch(pieces, q_at, height, weight.at[1])
    loader.arrived(0, weight.at[0], full.at[0])

    def project(columns):
        x = x_ref[:, columns].astype(jnp.float32)
        if gain_rows[0] is not None:
            x = x * gains_ref[pl.ds(gain_rows[0], 1), columns]
        z_ref[:, columns] = x + product(mix_ref[...], weight[0, :, columns])

    tiles(project, z_ref.shape[1], TILE)
    gain = gains_ref[pl.ds(gain_rows[1], 1), :]
    normalise(z_ref, n_ref, r_ref, gain, low_ref)
    if q_at is not None:
        loader.arrived(1, weight.at[1], full.at[1])

        def query(columns):
            q_ref[:, columns] = bfloat(product(low_ref[...], weight[1, :, columns]))

        tiles(query, q_ref.shape[1], TILE)
    loader.finish()


def tail_up_kernel(n, height, up_at, gain_row, n_ref, gains_ref, *refs):
    pieces = refs[:n]
    slope_hbm, inner_hbm, full, up, low_ref, slope_ref, inner_ref, out_sem, *sems = refs[n:]
    blocks = up.shape[0]
    loader = Loader(sems)
    for j in range(blocks):
        loader.fetch(pieces, up_at + j * height, height, up.at[j])
    gain = gains_ref[pl.ds(gain_row, 1), :]

    def lower(rows):
        low_ref[rows, :] = bfloat(n_ref[rows, :] * gain)

    tiles(lower, n_ref.shape[0], ROWS)
    width = up.shape[2]
    outs = []
    for j in range(blocks):
        loader.arrived(j, up.at[j], full.at[j])

        def upward(columns):
            inner, slope = gelu_both(product(low_ref[...], up[j, :, columns]))
            place = pl.ds(pl.multiple_of(j * width + columns.start, TILE), TILE)
            inner_ref[:, place] = bfloat(inner)
            slope_ref[:, place] = bfloat(slope)

        tiles(upward, width, TILE)
        columns = pl.ds(j * width, width)
        for i, (ref, hbm) in enumerate(((inner_ref, inner_hbm), (slope_ref, slope_hbm))):
            out = pltpu.make_async_copy(ref.at[:, columns], hbm.at[:, columns], out_sem.at[i, j])
            out.start()
            outs.append(out)
    loader.finish()
    for out in outs:
        out.wait()


def tail_down_kernel(n, height, offsets, gain_rows, n_ref, inner_ref, gains_ref, first_ref, second_ref, *refs):
    pieces, refs = refs[:n], refs[n:]
    pre_slope_ref, adapt_ref, n_out_ref, r_out_ref, out_ref, down_full, adapt_full = refs[:7]
    down, adapt, low_ref, z_ref, *sems = refs[7:]
    down_at, adapt_at = offsets
    width = z_ref.shape[1]
    loader = Loader(sems)
    loader.fetch(pieces, adapt_at, height, adapt)
    for at in range(0, width, TILE):
        loader.fetch(pieces, down_at, down.shape[0] // width * height, down, pl.ds(at, TILE))
    gain = gains_ref[pl.ds(gain_rows[0], 1), :]

    def lower(rows):
        low_ref[rows, :] = bfloat(n_ref[rows, :] * gain)

    tiles(lower, n_ref.shape[0], ROWS)
    loader.arrived(0, adapt, adapt_full)

    def adapting(columns):
        pre = product(low_ref[...], adapt[:, columns]) + first_ref[:, columns]
        adapted, slope = gelu_both(pre)
        adapt_ref[:, columns] = bfloat(adapted)
        pre_slope_ref[:, columns] = bfloat(slope)

    tiles(adapting, ADAPT, TILE)
    for i, at in enumerate(range(0, width, TILE)):
        columns = pl.ds(at, TILE)
        loader.arrived(1 + i, down.at[:, columns], down_full.at[:, columns])
        h = n_ref[:, columns] * gains_ref[pl.ds(gain_rows[0], 1), columns]
        ffn = product(inner_ref[...], down[:, columns])
        adapted = product_t(adapt_ref[...], adapt[columns, ADAPT:]) + second_ref[:, columns]
        z_ref[:, columns] = h + ffn + 4.0 * adapted
    normalise(z_ref, n_out_ref, r_out_ref, gains_ref[pl.ds(gain_rows[1], 1), :], out_ref)
    loader.finish()


def tail_back_kernel(height, gain_rows, more, *refs):
    (cot_ref, n2_ref, r2_ref, n1_ref, r1_ref, gains_ref, slope_hbm, pre_slope_ref, adapt_low_ref) = refs[:9]
    refs = refs[9:]
    (up_hbm, down_hbm, adapt_hbm, wo_hbm), refs = refs[:4], refs[4:]
    if more:
        far_ref, refs = refs[0], refs[1:]
    dz_ref, dmix_ref, matrices_ref, g_first_ref, g_second_ref = refs[:5]
    up, down, adapt, wo, dt_ref, e_ref, low_ref, du_ref, dpre_ref, sem = refs[5:]
    blocks = up.shape[0]
    load(
        [adapt_hbm, down_hbm, slope_hbm, up_hbm, wo_hbm.at[0]],
        [adapt, down, du_ref, up, wo],
        sem,
    )
    gain1 = gains_ref[pl.ds(gain_rows[0], 1), :]
    gain2 = gains_ref[pl.ds(gain_rows[1], 1), :]

    def lower(rows):
        low_ref[rows, :] = bfloat(n1_ref[rows, :] * gain1)

    tiles(lower, n1_ref.shape[0], ROWS)

    def arriving(rows):
        grad = cot_ref[rows, :].astype(jnp.float32)
        return grad + far_ref[rows, :].astype(jnp.float32) if more else grad

    normalise_back(arriving, n2_ref, r2_ref, gain2, dt_ref, e_ref)
    loaded(adapt, sem.at[0])

    def adapting(columns):
        back = 4.0 * product(e_ref[...], adapt[:, pl.ds(ADAPT + columns.start, TILE)])
        dpre_ref[:, columns] = bfloat(back * pre_slope_ref[:, columns].astype(jnp.float32))

    tiles(adapting, ADAPT, TILE)
    g_first_ref[...] = jnp.sum(dpre_ref[...].astype(jnp.float32), axis=0, keepdims=True)
    g_second_ref[...] = 4.0 * jnp.sum(e_ref[...].astype(jnp.float32), axis=0, keepdims=True)

    wide = max(height, STAT)

    def matrices(columns):
        down_grad = bfloat(product_rows(low_ref[:, columns], dpre_ref[...]))
        up_grad = bfloat(4.0 * product_rows(e_ref[:, columns], adapt_low_ref[...]))
        for i in range(wide // height):
            block, rows = columns.start // height + i, slice(i * height, (i + 1) * height)
            matrices_ref[block, :height, :] = down_grad[rows, :]
            matrices_ref[block, height:, :] = up_grad[rows, :]

    tiles(matrices, low_ref.shape[1], wide)
    loaded(down, sem.at[1])
    loaded(du_ref, sem.at[2])

    def inner(columns):
        back = product_t(e_ref[...], down[columns, :])
        du_ref[:, columns] = bfloat(back * du_ref[:, columns].astype(jnp.float32))

    tiles(inner, du_ref.shape[1], TILE)
    loaded(up, sem.at[3])
    width = up.shape[2]

    def hidden(columns):
        total = dt_ref[:, columns] + product_t(dpre_ref[...], adapt[columns, :ADAPT])
        for j in range(blocks):
            total += product_t(du_ref[:, j * width : (j + 1) * width], up[j, columns, :])
        dt_ref[:, columns] = total

    tiles(hidden, dt_ref.shape[1], TILE)
    normalise_back(lambda rows: dt_ref[rows, :], n1_ref, r1_ref, gain1, dz_ref, e_ref)
    loaded(wo, sem.at[4])

    def mixing(columns):
        dmix_ref[:, columns] = bfloat(product_t(e_ref[...], wo[columns, :]))

    tiles(mixing, dmix_ref.shape[1], TILE)


def query_back_kernel(gain_row, dz_ref, dq_ref, n_ref, r_ref, gains_ref, weights, *refs):
    dz_out_ref, dmix_ref, weight, dy_ref, e_ref, sem = refs
    load([weights.at[1], weights.at[0]], [weight.at[0], weight.at[1]], sem)
    loaded(weight.at[0], sem.at[0])

    def back(columns):
        dy_ref[:, columns] = dz_ref[:, columns] + product_t(dq_ref[...], weight[0, columns, :])

    tiles(back, dy_ref.shape[1], TILE)
    gain = gains_ref[pl.ds(gain_row, 1), :]
    normalise_back(lambda rows: dy_ref[rows, :], n_ref, r_ref, gain, dz_out_ref, e_ref)
    loaded(weight.at[1], sem.at[1])

    def mixing(columns):
        dmix_ref[:, columns] = bfloat(product_t(e_ref[...], weight[1, columns, :]))

    tiles(mixing, dmix_ref.shape[1], TILE)


def back_kernel(indices, bases, *refs):
    count = len(indices)
    base_refs, grads = refs[:bases], refs[bases : bases + count]
    weights, out_ref, weight, sem = refs[bases + count :]
    load([weights.at[i] for i in indices], [weight.at[j] for j in range(count)], sem)
    for j in range(count):
        loaded(weight.at[j], sem.at[j])

    def back(columns):
        total = None
        for base in base_refs:
            part = base[:, columns].astype(jnp.float32)
            total = part if total is None else total + part
        for j in range(count):
            part = product_t(grads[j][...], weight[j, columns, :])
            total = part if total is None else total + part
        out_ref[:, columns] = total.astype(out_ref.dtype)

    tiles(back, out_ref.shape[1], TILE)


def split(value):
    high = bfloat(value)
    return high, bfloat(value - high.astype(jnp.float32))


def put_left(ref, value):
    high, low = split(value)
    ref[:, :ADAPT] = high
    ref[:, ADAPT : 2 * ADAPT] = high
    ref[:, 2 * ADAPT :] = low


def put_right(ref, value):
    high, low = split(value)
    ref[:ADAPT, :] = high
    ref[ADAPT : 2 * ADAPT, :] = low
    ref[2 * ADAPT :, :] = high


def multiply(out_ref, left, right):
    def body(columns):
        out_ref[:, columns] = product(left[...], right[:, columns])

    tiles(body, ADAPT, TILE)


def muon_kernel(parts, *refs):
    rows_refs, (out_ref, high, low, gram, poly, factor, left, right, rows_left) = refs[:parts], refs[parts:]
    rows = rows_refs[0].shape[0]
    for i, ref in enumerate(rows_refs):
        high[i * rows : (i + 1) * rows, :], low[i * rows : (i + 1) * rows, :] = split(ref[...])

    def square(columns):
        gram[:, columns] = (
            product_rows(high[...], high[:, columns])
            + product_rows(high[...], low[:, columns])
            + product_rows(low[...], high[:, columns])
        )

    tiles(square, ADAPT, TILE)
    eye = lax.broadcasted_iota(jnp.int32, (ADAPT, ADAPT), 0) == lax.broadcasted_iota(
        jnp.int32, (ADAPT, ADAPT), 1
    )
    scale = 1.0 / (jnp.sqrt(jnp.sum(jnp.where(eye, gram[...], 0.0), keepdims=True)) + 1e-07)
    gram[...] = gram[...] * (scale * scale)

    def polynomial():
        put_left(left, gram[...])
        put_right(right, gram[...])
        multiply(poly, left, right)
        poly[...] = (
            jnp.where(eye, NEWTON_LINEAR, 0.0) + NEWTON_QUADRATIC * gram[...] + NEWTON_CUBIC * poly[...]
        )
        put_right(right, poly[...])

    def advance():
        multiply(gram, left, right)
        put_left(left, gram[...])
        multiply(gram, left, right)

    polynomial()
    factor[...] = poly[...]
    advance()

    @pl.loop(0, NS_ITERS - 2)
    def _(i):
        polynomial()
        advance()
        put_left(left, factor[...])
        multiply(factor, left, right)

    polynomial()
    put_left(left, factor[...])
    multiply(factor, left, right)
    put_right(right, factor[...])
    put_left(rows_left, rows_refs[0][...] * scale)
    multiply(out_ref, rows_left, right)


HBM = pl.BlockSpec(memory_space=pltpu.HBM)
IN_VMEM = pl.BlockSpec(memory_space=pltpu.VMEM)
F32, BF16 = jnp.float32, jnp.bfloat16


def call(kernel, ins, specs, outs, scratch, flops, collective_id=None):
    return pl.pallas_call(
        kernel,
        in_specs=specs,
        out_specs=[IN_VMEM if len(out) == 2 else HBM for out in outs],
        out_shape=[jax.ShapeDtypeStruct(*out[:2]) for out in outs],
        scratch_shapes=scratch,
        compiler_params=pltpu.CompilerParams(
            vmem_limit_bytes=VMEM_LIMIT,
            collective_id=collective_id,
            has_side_effects=collective_id is not None,
        ),
        cost_estimate=pl.CostEstimate(
            flops=flops, bytes_accessed=sum(a.size * a.dtype.itemsize for a in ins), transcendentals=0
        ),
    )(*ins)


def squares(count):
    return pltpu.VMEM((count, D, D), BF16)


def stored(*shape):
    return (shape, BF16, HBM)


def project(collective_id, x, far, pieces, offsets):
    rows = x.shape[0]
    count, n = len(offsets), len(pieces.arrays)
    return call(
        functools.partial(project_kernel, n, pieces.height, offsets),
        [x, far, *pieces.arrays],
        [IN_VMEM] * 2 + [HBM] * n,
        [((rows, D), BF16)] * (count + 2) + [stored(count, D, D)],
        [squares(count), *loader_sems(count, n)],
        2 * rows * D * D * (count + 2),
        collective_id,
    )


def settle(collective_id, x, mix, gains, pieces, wo_at, q_at, gain_rows):
    rows = x.shape[0]
    n = len(pieces.arrays)
    count = 1 if q_at is None else 2
    outs = [((rows, D), F32), ((rows, STAT), F32)]
    scratch = [squares(count), pltpu.VMEM((rows, D), F32)]
    if q_at is not None:
        outs.append(((rows, D), BF16))
        scratch.append(pltpu.VMEM((rows, D), BF16))
    return call(
        functools.partial(settle_kernel, n, pieces.height, wo_at, q_at, gain_rows),
        [x, mix, gains, *pieces.arrays],
        [IN_VMEM] * 3 + [HBM] * n,
        outs + [stored(count, D, D)],
        scratch + loader_sems(count, n),
        2 * rows * D * D * count,
        collective_id,
    )


def tail_up(collective_id, normed, gains, pieces, up_at, gain_row):
    rows = normed.shape[0]
    n = len(pieces.arrays)
    blocks = 4
    hidden = blocks * D
    return call(
        functools.partial(tail_up_kernel, n, pieces.height, up_at, gain_row),
        [normed, gains, *pieces.arrays],
        [IN_VMEM] * 2 + [HBM] * n,
        [stored(rows, hidden), stored(rows, hidden), stored(blocks, D, D)],
        [
            squares(blocks),
            pltpu.VMEM((rows, D), BF16),
            pltpu.VMEM((rows, hidden), BF16),
            pltpu.VMEM((rows, hidden), BF16),
            pltpu.SemaphoreType.DMA((2, blocks)),
            *loader_sems(blocks, n),
        ],
        8 * rows * D * D,
        collective_id,
    )


def tail_down(collective_id, normed, inner, gains, bias_first, bias_second, pieces, offsets, gain_rows):
    rows, hidden = inner.shape
    n = len(pieces.arrays)
    return call(
        functools.partial(tail_down_kernel, n, pieces.height, offsets, gain_rows),
        [normed, inner, gains, bias_first[None], bias_second[None], *pieces.arrays],
        [IN_VMEM] * 5 + [HBM] * n,
        [
            ((rows, ADAPT), BF16),
            ((rows, ADAPT), BF16),
            ((rows, D), F32),
            ((rows, STAT), F32),
            ((rows, D), BF16),
            stored(hidden, D),
            stored(D, D),
        ],
        [
            pltpu.VMEM((hidden, D), BF16),
            pltpu.VMEM((D, D), BF16),
            pltpu.VMEM((rows, D), BF16),
            pltpu.VMEM((rows, D), F32),
            *loader_sems(1 + D // TILE, n),
        ],
        10 * rows * D * D,
        collective_id,
    )


def tail_back(height, cot, second, first, gains, slope, pre_slope, adapt_low, weights, gain_rows, more=()):
    rows = cot.shape[0]
    hidden = slope.shape[1]
    return call(
        functools.partial(tail_back_kernel, height, gain_rows, bool(more)),
        [cot, *second, *first, gains, slope, pre_slope, adapt_low, *weights, *more],
        [IN_VMEM] * 6 + [HBM] + [IN_VMEM] * 2 + [HBM] * 4 + [IN_VMEM] * len(more),
        [
            ((rows, D), F32),
            ((rows, D), BF16),
            ((D // height, 2 * height, ADAPT), BF16),
            ((1, ADAPT), F32),
            ((1, D), F32),
        ],
        [
            squares(hidden // D),
            pltpu.VMEM((hidden, D), BF16),
            pltpu.VMEM((D, D), BF16),
            pltpu.VMEM((D, D), BF16),
            pltpu.VMEM((rows, D), F32),
            pltpu.VMEM((rows, D), BF16),
            pltpu.VMEM((rows, D), BF16),
            pltpu.VMEM((rows, hidden), BF16),
            pltpu.VMEM((rows, ADAPT), BF16),
            pltpu.SemaphoreType.DMA((5,)),
        ],
        24 * rows * D * D,
    )


def query_back(dz, dq, first, gains, weights, gain_row):
    rows = dz.shape[0]
    return call(
        functools.partial(query_back_kernel, gain_row),
        [dz, dq, *first, gains, weights],
        [IN_VMEM] * 5 + [HBM],
        [((rows, D), F32), ((rows, D), BF16)],
        [
            squares(2),
            pltpu.VMEM((rows, D), F32),
            pltpu.VMEM((rows, D), BF16),
            pltpu.SemaphoreType.DMA((2,)),
        ],
        4 * rows * D * D,
    )


def back(bases, grads, weights, indices, dtype):
    rows = grads[0].shape[0]
    count = len(indices)
    return call(
        functools.partial(back_kernel, indices, len(bases)),
        [*bases, *grads, weights],
        [IN_VMEM] * (len(bases) + count) + [HBM],
        [((rows, D), dtype)],
        [squares(count), pltpu.SemaphoreType.DMA((count,))],
        2 * rows * D * D * count,
    )[0]


def muon(parts):
    rows = parts[0].shape[0]
    full = pltpu.VMEM((ADAPT, ADAPT), F32)
    return call(
        functools.partial(muon_kernel, len(parts)),
        parts,
        [IN_VMEM] * len(parts),
        [((rows, ADAPT), F32)],
        [
            pltpu.VMEM((rows * len(parts), ADAPT), BF16),
            pltpu.VMEM((rows * len(parts), ADAPT), BF16),
            full,
            full,
            full,
            pltpu.VMEM((ADAPT, 3 * ADAPT), BF16),
            pltpu.VMEM((3 * ADAPT, ADAPT), BF16),
            pltpu.VMEM((rows, 3 * ADAPT), BF16),
        ],
        20 * 6 * ADAPT**3,
    )[0]


def axis_bits(axis):
    return [1 << b for b in range(lax.axis_size(axis).bit_length() - 1)]


def tie(array, *others):
    return lax.optimization_barrier((array, *others))[0]


class Gather:
    def __init__(self, array, height):
        self.height = height
        self.array = array

    def begin(self, *after):
        array = tie(self.array, *after) if after else self.array
        bits = axis_bits("wide")
        self.pieces = {0: self.array}
        for bit in bits[1:3]:
            self.pieces[bit] = swap(array, "wide", bit)
        return self

    def across(self, *after):
        bits = axis_bits("wide")
        near, far = bits[1:3]
        pieces = self.pieces
        even = lax.axis_index("wide") % 2 == 0
        chosen = jnp.where(even, pieces[near], pieces[far])
        pieces[near | far] = lax.ppermute(
            tie(chosen, *after) if after else chosen,
            "wide",
            [(i, i ^ (near if i % 2 else far)) for i in range(lax.axis_size("wide"))],
        )
        for bit in bits[3:]:
            for r in list(pieces):
                pieces[r | bit] = swap(pieces[r], "wide", bit)
        self.arrays = [pieces[r] for r in range(0, lax.axis_size("wide"), 2)]
        return self

    def marks(self):
        return list(self.pieces.values())[1:3]


def gather_any_order(array, axis):
    blocks = array[None]
    for bit in axis_bits(axis):
        blocks = jnp.concatenate([blocks, swap(blocks, axis, bit)])
    return blocks


def shards(
    enc_in,
    dec_in,
    segment_ids,
    enc_cot,
    dec_cot,
    enc_qkv,
    enc_wo,
    enc_w_in,
    enc_w_out,
    enc_gains,
    dec_qkv,
    dec_wo,
    dec_w_in,
    dec_w_out,
    dec_gains,
    adapter_weights,
    adapter_momenta,
    bias_in,
    bias_out,
):
    height = enc_wo.shape[0]
    stack = lambda *arrays: jnp.concatenate([a.reshape(-1, D) for a in arrays])
    columns = lambda array: [array[:, j * D : (j + 1) * D] for j in range(array.shape[1] // D)]
    found = gather_any_order(bfloat(adapter_weights), "narrow")
    found = found[lax.axis_index("narrow") ^ jnp.arange(lax.axis_size("narrow"))]
    adapters = found.transpose(1, 0, 2, 3).reshape(4, height, ADAPT)
    beside = lambda l: jnp.concatenate([adapters[2 * l], adapters[2 * l + 1]], axis=1)
    gain_rows = jnp.concatenate([enc_gains, dec_gains])
    gain_block = jnp.pad(gain_rows, ((0, 16 - gain_rows.shape[0]), (0, D - height)))
    gather = lambda array: Gather(array, height)
    enc_first = gather(stack(enc_qkv, gain_block))
    dec_first = gather(stack(dec_qkv[:3]))
    enc_up = gather(stack(enc_wo, *columns(enc_w_in)))
    enc_down = gather(stack(enc_w_out, beside(0)))
    dec_second = gather(stack(dec_wo, dec_qkv[3:]))
    dec_up = gather(stack(*columns(dec_w_in)))
    dec_down = gather(stack(dec_w_out, beside(1)))

    partner = lambda array: swap(array, "narrow", 1)
    other_ids = partner(segment_ids)
    rows = enc_in.shape[0]
    half = (lax.axis_index("narrow") % 2).astype(jnp.int32).reshape(1)
    places = (half, segment_ids.reshape(1, rows), segment_ids.reshape(rows, 1), other_ids.reshape(rows, 1))
    at = lambda i: i * height

    enc_first.begin()
    enc_far, dec_far = partner(enc_in), partner(dec_in)
    dec_first.begin(*enc_first.marks())
    enc_first.across()
    enc_up.begin(enc_first.arrays[-1])
    enc_query, enc_key, enc_value, enc_key_far, enc_value_far, enc_qkv_full = project(
        0, enc_in, enc_far, enc_first, (at(0), at(1), at(2))
    )
    enc_keys, enc_values = (enc_key, enc_key_far), (enc_value, enc_value_far)
    count = lax.axis_size("wide")
    found = jnp.stack([p[at(3) : at(3) + 8, :height] for p in enc_first.arrays])
    found = jnp.concatenate([found, swap(found, "wide", 1)])
    order = lax.axis_index("wide") ^ jnp.arange(count)
    order = order // 2 + order % 2 * (count // 2)
    gains = found[order].transpose(1, 0, 2).reshape(8, D).astype(jnp.float32)

    dec_first.across(enc_value)
    enc_mix, enc_lse = attend(places, enc_query, enc_keys, enc_values, False)
    enc_up.across(enc_mix)
    enc_down.begin(enc_mix)
    self_query, self_key, self_value, self_key_far, self_value_far, dec_qkv_full = project(
        1, tie(dec_in, enc_mix), dec_far, dec_first, (at(0), at(1), at(2))
    )
    self_keys, self_values = (self_key, self_key_far), (self_value, self_value_far)
    dec_second.begin(self_value)
    self_mix, self_lse = attend(places, self_query, self_keys, self_values, True)
    enc_down.across(self_mix)
    *enc_norm1, enc_wo_full = settle(
        2, enc_in, tie(enc_mix, self_mix), gains, enc_up, at(0), None, (None, 0)
    )
    enc_slope, enc_inner, enc_up_full = tail_up(3, enc_norm1[0], gains, enc_up, at(1), 0)
    dec_second.across(enc_inner)
    dec_up.begin(enc_inner)
    enc_pre_slope, enc_adapt, *enc_norm2, enc_low, enc_down_full, enc_adapt_full = tail_down(
        4, enc_norm1[0], enc_inner, gains, bias_in[0], bias_out[0], enc_down, (0, at(4)), (0, 1)
    )
    *dec_norm1, cross_query, dec_q_full = settle(
        5, dec_in, tie(self_mix, enc_low), gains, dec_second, at(0), at(2), (None, 2)
    )
    dec_down.begin(cross_query)
    cross_key, cross_value, cross_key_far, cross_value_far, dec_kv_full = project(
        6, tie(enc_low, cross_query), partner(enc_low), dec_second, (at(3), at(4))
    )
    cross_keys, cross_values = (cross_key, cross_key_far), (cross_value, cross_value_far)
    dec_up.across(cross_key)
    cross_mix, cross_lse = attend(places, cross_query, cross_keys, cross_values, False)
    dec_down.across(cross_mix)
    *dec_norm2, dec_wo_full = settle(
        7, dec_norm1[0], cross_mix, gains, dec_second, at(1), None, (2, 3)
    )
    dec_slope, dec_inner, dec_up_full = tail_up(8, dec_norm2[0], gains, dec_up, at(0), 3)
    dec_pre_slope, dec_adapt, *dec_norm3, dec_low, dec_down_full, dec_adapt_full = tail_down(
        9, dec_norm2[0], dec_inner, gains, bias_in[1], bias_out[1], dec_down, (0, at(4)), (3, 4)
    )

    grad_z2, grad_cross_mix, dec_matrices, grad_dec_first, grad_dec_second = tail_back(
        height,
        dec_cot,
        dec_norm3,
        dec_norm2,
        gains,
        dec_slope,
        dec_pre_slope,
        dec_adapt,
        (dec_up_full, dec_down_full, dec_adapt_full, dec_wo_full),
        (3, 4),
    )
    exchange = lambda array, axis: lax.all_to_all(array, axis, split_axis=0, concat_axis=0, tiled=True)
    total = lambda array: jnp.sum(array.astype(jnp.float32), axis=0)
    dec_matrices = exchange(dec_matrices, "wide")
    cross_back = attend_back(
        places, grad_cross_mix, cross_query, cross_keys, cross_values, cross_mix, cross_lse, False
    )
    far_encoded = back((), (cross_back[2], cross_back[4]), dec_kv_full, (0, 1), BF16)
    near_encoded = partner(far_encoded)
    grad_encoded = back(
        (tie(enc_cot, far_encoded),), (cross_back[1], cross_back[3]), dec_kv_full, (0, 1), F32
    )
    dec_sums = total(tie(dec_matrices, cross_back[0]))
    grad_z1, grad_self_mix = query_back(
        tie(grad_z2, grad_encoded),
        cross_back[0],
        dec_norm1,
        gains,
        dec_q_full,
        2,
    )
    grad_ez1, grad_enc_mix, enc_matrices, grad_enc_first, grad_enc_second = tail_back(
        height,
        tie(grad_encoded, grad_z1),
        enc_norm2,
        enc_norm1,
        gains,
        enc_slope,
        enc_pre_slope,
        enc_adapt,
        (enc_up_full, enc_down_full, enc_adapt_full, enc_wo_full),
        (0, 1),
        (near_encoded,),
    )
    enc_matrices = exchange(enc_matrices, "wide")

    devices = lax.axis_size("wide") * lax.axis_size("narrow")
    slices = lambda first, second: jnp.concatenate([first, second]).reshape(2, devices, -1).transpose(1, 0, 2)
    firsts = slices(grad_enc_first, grad_dec_first)
    seconds = slices(grad_enc_second, grad_dec_second)
    biases = jnp.concatenate([firsts.reshape(devices, -1), seconds.reshape(devices, -1)], axis=1)
    used = biases.shape[1]
    biases = jnp.pad(biases, ((0, 0), (0, -used % STAT)))
    biases = jnp.sum(exchange(biases, ("wide", "narrow")), axis=0)[:used]
    grad_bias_in = biases[: firsts[0].size].reshape(firsts.shape[1:])
    grad_bias_out = biases[firsts[0].size :].reshape(seconds.shape[1:])

    self_back = attend_back(
        places, tie(grad_self_mix, grad_ez1), self_query, self_keys, self_values, self_mix, self_lse, True
    )

    repeat = lax.axis_size("narrow") // 4
    spread = lambda array: jnp.repeat(array, repeat, axis=0) if repeat > 1 else array
    to_matrix = lambda array: lax.all_to_all(
        spread(array), "narrow", split_axis=0, concat_axis=1, tiled=True
    )[0]
    to_rows = lambda array: lax.all_to_all(
        array[None], "narrow", split_axis=1, concat_axis=0, tiled=True
    )[::repeat]
    old_momentum = to_matrix(tie(adapter_momenta, cross_back[0]))
    sums = jnp.concatenate([total(tie(enc_matrices, self_back[0])), dec_sums])
    sums = spread(bfloat(sums).reshape(4, height, ADAPT))
    enc_back = attend_back(
        places, tie(grad_enc_mix, sums), enc_query, enc_keys, enc_values, enc_mix, enc_lse, False
    )
    summed = exchange(sums, "narrow")
    momentum = DECAY * old_momentum + total(tie(summed, enc_back[0]))
    parts = [momentum] + [swap(momentum, "wide", r) for r in range(1, lax.axis_size("wide"))]
    new_momenta = to_rows(momentum)

    far_dec = back(
        (), (tie(self_back[2], momentum), self_back[4]), dec_qkv_full, (1, 2), BF16
    )
    near_dec = partner(far_dec)
    far_enc = back((), (tie(enc_back[2], far_dec), enc_back[4]), enc_qkv_full, (1, 2), BF16)
    near_enc = partner(far_enc)
    grad_dec = back(
        (tie(grad_z1, far_enc), near_dec),
        (self_back[0], self_back[1], self_back[3]),
        dec_qkv_full,
        (0, 1, 2),
        F32,
    )
    orthogonal = muon([parts[0], tie(parts[1], grad_dec), *parts[2:]])
    grad_enc = back(
        (tie(grad_ez1, orthogonal), near_enc),
        (enc_back[0], enc_back[1], enc_back[3]),
        enc_qkv_full,
        (0, 1, 2),
        F32,
    )
    new_weights = adapter_weights - RATE * math.sqrt(max(1.0, D / ADAPT)) * to_rows(orthogonal)
    return (
        enc_low,
        dec_low,
        grad_enc,
        grad_dec,
        grad_bias_in,
        grad_bias_out,
        new_momenta,
        new_weights,
    )


def solution(mesh):
    both = ("wide", "narrow")
    tokens = P(both, None)
    rows_first, rows_second = P("wide", None), P(None, "wide", None)
    adapters = P(None, both, None)
    in_specs = (
        tokens,
        tokens,
        P(both),
        tokens,
        tokens,
        rows_second,
        rows_first,
        rows_first,
        rows_first,
        P(None, "wide"),
        rows_second,
        rows_second,
        rows_first,
        rows_first,
        P(None, "wide"),
        adapters,
        adapters,
        P(),
        P(),
    )
    out_specs = (
        tokens,
        tokens,
        tokens,
        tokens,
        P(None, both),
        P(None, both),
        adapters,
        adapters,
    )
    return jax.shard_map(shards, mesh=mesh, in_specs=in_specs, out_specs=out_specs, check_vma=False)
```

```python
import functools
import math

import jax
import jax.numpy as jnp
from jax import lax
from jax.experimental import pallas as pl
from jax.experimental.pallas import tpu as pltpu
from jax.sharding import PartitionSpec as P

D = 1024
HD = 64
ADAPT = 512
NS_ITERS = 5

EPSILON = 1e-05
MASKED = -1e30
NEWTON_LINEAR = 3.4445
NEWTON_QUADRATIC = -4.775
NEWTON_CUBIC = 2.0315
RATE = 0.7
DECAY = 0.5
LOG2E = 1.4426950408889634
PAIR = 2 * HD
VMEM_LIMIT = 58 * 1024 * 1024
MESH = pl.DeviceIdType.MESH


def swap(array, axis, bit):
    return lax.ppermute(array, axis, [(i, i ^ bit) for i in range(lax.axis_size(axis))])


def bfloat(tensor):
    return tensor.astype(jnp.bfloat16)


def product(left_side, right_side):
    return jnp.dot(left_side, right_side, preferred_element_type=jnp.float32)


def contract(left_side, right_side, left_dim, right_dim):
    return lax.dot_general(
        left_side,
        right_side,
        (((left_dim,), (right_dim,)), ((), ())),
        preferred_element_type=jnp.float32,
    )


def product_t(left_side, right_side):
    return contract(left_side, right_side, 1, 1)


def product_rows(left_side, right_side):
    return contract(left_side, right_side, 0, 0)


def gelu_both(tensor):
    phi = 0.5 * (1.0 + lax.erf(tensor * 0.7071067811865476))
    slope = phi + tensor * jnp.exp(-0.5 * tensor * tensor) * 0.3989422804014327
    return tensor * phi, slope


def fill_bias(half_ref, qid_ref, kid_own_ref, kid_far_ref, bias_ref, causal):
    rows = qid_ref.shape[1]
    qid = qid_ref[...]
    for part, kid_ref in enumerate((kid_own_ref, kid_far_ref)):
        allowed = kid_ref[...] == qid
        if causal:
            if part == 0:
                key_at = lax.broadcasted_iota(jnp.int32, (rows, rows), 0)
                query_at = lax.broadcasted_iota(jnp.int32, (rows, rows), 1)
                allowed = allowed & (key_at <= query_at)
            else:
                allowed = allowed & (half_ref[0] == 1)
        bias_ref[pl.ds(part * rows, rows), :] = jnp.where(allowed, 0.0, MASKED)


def head_mask(rows, head):
    return lax.broadcasted_iota(jnp.int32, (rows, PAIR), 1) // HD == head


def attend_kernel(
    causal,
    chunk,
    half_ref,
    qid_ref,
    kid_own_ref,
    kid_far_ref,
    q_ref,
    k_own_ref,
    k_far_ref,
    v_own_ref,
    v_far_ref,
    out_ref,
    lse_ref,
    bias_ref,
    score_ref,
):
    rows = q_ref.shape[0]

    @pl.when(pl.program_id(0) == 0)
    def _():
        fill_bias(half_ref, qid_ref, kid_own_ref, kid_far_ref, bias_ref, causal)

    queries = q_ref[...] * 0.125
    steps = [
        (part, at)
        for part in range(2)
        for at in range(0, rows, chunk)
    ]
    keys = (k_own_ref, k_far_ref)
    values = (v_own_ref, v_far_ref)
    mixes = []
    for head in range(2):
        q_head = jnp.where(head_mask(rows, head), queries, jnp.zeros_like(queries))
        peak = None
        for part, at in steps:
            place = pl.ds(part * rows + at, chunk)
            scores = product_t(keys[part][pl.ds(at, chunk), :], q_head)
            scores = scores * LOG2E + bias_ref[place, :]
            score_ref[head, place, :] = scores
            top = jnp.max(scores, axis=0, keepdims=True)
            peak = top if peak is None else jnp.maximum(peak, top)
        total, mix = None, None
        for part, at in steps:
            place = pl.ds(part * rows + at, chunk)
            raised = jnp.exp2(score_ref[head, place, :] - peak)
            share = jnp.sum(raised, axis=0, keepdims=True)
            piece = product_rows(values[part][pl.ds(at, chunk), :], bfloat(raised))
            total = share if total is None else total + share
            mix = piece if mix is None else mix + piece
        mixes.append((mix * (1.0 / total))[head * HD : (head + 1) * HD, :])
        lse_ref[0, pl.ds(head, 1), :] = peak + jnp.log2(total)
    out_ref[...] = bfloat(jnp.concatenate(mixes, axis=0).T)


def attend_back_kernel(
    causal,
    chunk,
    half_ref,
    qid_ref,
    kid_own_ref,
    kid_far_ref,
    q_ref,
    k_own_ref,
    k_far_ref,
    v_own_ref,
    v_far_ref,
    out_ref,
    grad_ref,
    lse_ref,
    dq_ref,
    dk_own_ref,
    dk_far_ref,
    dv_own_ref,
    dv_far_ref,
    bias_ref,
):
    rows = q_ref.shape[0]

    @pl.when(pl.program_id(0) == 0)
    def _():
        fill_bias(half_ref, qid_ref, kid_own_ref, kid_far_ref, bias_ref, causal)

    queries = q_ref[...] * 0.125
    grads = grad_ref[...]
    products = (grads.astype(jnp.float32) * out_ref[...].astype(jnp.float32)).T
    q_heads, g_heads, deltas, lses = [], [], [], []
    for head in range(2):
        chosen = head_mask(rows, head)
        q_heads.append(jnp.where(chosen, queries, jnp.zeros_like(queries)))
        g_heads.append(jnp.where(chosen, grads, jnp.zeros_like(grads)))
        deltas.append(jnp.sum(products[head * HD : (head + 1) * HD, :], axis=0, keepdims=True))
        lses.append(lse_ref[0, pl.ds(head, 1), :])
    grad_q = [None, None]
    for part in range(2):
        key_ref = (k_own_ref, k_far_ref)[part]
        value_ref = (v_own_ref, v_far_ref)[part]
        dk_ref = (dk_own_ref, dk_far_ref)[part]
        dv_ref = (dv_own_ref, dv_far_ref)[part]
        for at in range(0, rows, chunk):
            here = pl.ds(at, chunk)
            keys, values = key_ref[here, :], value_ref[here, :]
            grad_k, grad_v = None, None
            for head in range(2):
                scores = product_t(keys, q_heads[head])
                bias = bias_ref[pl.ds(part * rows + at, chunk), :]
                weights = jnp.exp2(scores * LOG2E + (bias - lses[head]))
                grad_w = product_t(values, g_heads[head])
                grad_s = bfloat(weights * (grad_w - deltas[head]))
                piece_v = product(bfloat(weights), g_heads[head])
                piece_k = product(grad_s, q_heads[head])
                piece_q = product_rows(keys, grad_s)
                grad_v = piece_v if grad_v is None else grad_v + piece_v
                grad_k = piece_k if grad_k is None else grad_k + piece_k
                grad_q[head] = piece_q if grad_q[head] is None else grad_q[head] + piece_q
            dk_ref[here, :] = grad_k.astype(dk_ref.dtype)
            dv_ref[here, :] = grad_v.astype(dv_ref.dtype)
    joined = jnp.concatenate([grad_q[h][h * HD : (h + 1) * HD, :] for h in range(2)], axis=0)
    dq_ref[...] = bfloat((joined * 0.125).T)


def attention_specs(rows):
    whole = lambda shape: pl.BlockSpec(shape, lambda i: (0,) * len(shape))
    columns = pl.BlockSpec((rows, PAIR), lambda i: (0, i))
    fixed = [
        pl.BlockSpec(memory_space=pltpu.SMEM),
        whole((1, rows)),
        whole((rows, 1)),
        whole((rows, 1)),
    ]
    return fixed, columns, pl.BlockSpec((1, 8, rows), lambda i: (i, 0, 0))


def attend(places, queries, keys, values, causal):
    rows, width = queries.shape
    pairs = width // PAIR
    fixed, columns, stat = attention_specs(rows)
    return pl.pallas_call(
        functools.partial(attend_kernel, causal, 256),
        grid=(pairs,),
        in_specs=fixed + [columns] * 5,
        out_specs=[columns, stat],
        out_shape=[
            jax.ShapeDtypeStruct((rows, width), jnp.bfloat16),
            jax.ShapeDtypeStruct((pairs, 8, rows), jnp.float32),
        ],
        scratch_shapes=[
            pltpu.VMEM((2 * rows, rows), jnp.float32),
            pltpu.VMEM((2, 2 * rows, rows), jnp.float32),
        ],
        compiler_params=pltpu.CompilerParams(vmem_limit_bytes=VMEM_LIMIT),
        cost_estimate=pl.CostEstimate(
            flops=32 * rows * rows * width, bytes_accessed=12 * rows * width, transcendentals=0
        ),
    )(*places, queries, *keys, *values)


def attend_back(places, grad_out, queries, keys, values, mix, lse, causal, after=()):
    rows, width = queries.shape
    pairs = width // PAIR
    fixed, columns, stat = attention_specs(rows)
    return pl.pallas_call(
        lambda *refs: attend_back_kernel(causal, 256, *refs[:12], *refs[12 + len(after) :]),
        grid=(pairs,),
        in_specs=fixed + [columns] * 7 + [stat] + [HBM] * len(after),
        out_specs=[columns] * 5,
        out_shape=[
            jax.ShapeDtypeStruct((rows, width), jnp.bfloat16),
        ]
        * 5,
        scratch_shapes=[pltpu.VMEM((2 * rows, rows), jnp.float32)],
        compiler_params=pltpu.CompilerParams(vmem_limit_bytes=VMEM_LIMIT),
        cost_estimate=pl.CostEstimate(
            flops=80 * rows * rows * width, bytes_accessed=24 * rows * width, transcendentals=0
        ),
    )(*places, queries, *keys, *values, mix, grad_out, lse, *after)


def flipped(me, bits):
    place = me
    bit = 1
    while bit <= bits:
        if bits & bit:
            place = place + bit * (1 - 2 * lax.rem(lax.div(me, bit), 2))
        bit *= 2
    return place


class Loader:
    def __init__(self, sems):
        self.local, self.send, self.recv, self.stored = sems
        self.copies, self.stores = [], []
        self.me = lax.axis_index("wide")
        self.sibling = {"wide": flipped(self.me, 1)}
        barrier = pltpu.get_barrier_semaphore()
        pl.semaphore_signal(barrier, inc=1, device_id=self.sibling, device_id_type=MESH)
        pl.semaphore_wait(barrier, 1)

    def fetch(self, pieces, offset, height, target, columns=slice(None)):
        block = len(self.copies)
        copies = []
        for i, piece in enumerate(pieces):
            at = pl.multiple_of(flipped(self.me, 2 * i) * height, height)
            source = piece.at[pl.ds(offset, height), columns]
            place = target.at[pl.ds(at, height), columns]
            near = pltpu.make_async_copy(source, place, self.local.at[block, i])
            far = pltpu.make_async_remote_copy(
                source,
                place,
                self.send.at[block, i],
                self.recv.at[block, i],
                device_id=self.sibling,
                device_id_type=MESH,
            )
            near.start()
            far.start()
            copies.append((near, far))
        self.copies.append(copies)
        return block

    def arrived(self, block, target, out):
        for near, far in self.copies[block]:
            near.wait()
            far.wait_recv()
        store = pltpu.make_async_copy(target, out, self.stored.at[block])
        store.start()
        self.stores.append(store)

    def finish(self):
        for copies in self.copies:
            for _, far in copies:
                far.wait_send()
        for store in self.stores:
            store.wait()


def loader_sems(blocks, pieces):
    dma = pltpu.SemaphoreType.DMA
    return [dma((blocks, pieces))] * 3 + [dma((blocks,))]


def load(weights, targets, sem):
    for j, (weight, target) in enumerate(zip(weights, targets)):
        pltpu.make_async_copy(weight, target, sem.at[j]).start()


def loaded(target, sem):
    pltpu.make_async_copy(target, target, sem).wait()


def tiles(body, width, step):
    @pl.loop(0, width // step)
    def _(i):
        body(pl.ds(pl.multiple_of(i * step, step), step))


ROWS = 64
TILE = 512
STAT = 128


def normalise(z_ref, n_ref, r_ref, gain, low_ref):
    def body(rows):
        z = z_ref[rows, :]
        centred = z - jnp.mean(z, axis=-1, keepdims=True)
        inverse = lax.rsqrt(jnp.mean(centred * centred, axis=-1, keepdims=True) + EPSILON)
        normed = centred * inverse
        n_ref[rows, :] = normed
        r_ref[rows, :] = jnp.broadcast_to(inverse, (ROWS, STAT))
        if low_ref is not None:
            low_ref[rows, :] = bfloat(normed * gain)

    tiles(body, z_ref.shape[0], ROWS)


def normalise_back(read_grad, n_ref, r_ref, gain, dz_ref, low_ref):
    def body(rows):
        scaled = read_grad(rows) * gain
        normed = n_ref[rows, :]
        dz = r_ref[rows, :][:, :1] * (
            scaled
            - jnp.mean(scaled, axis=-1, keepdims=True)
            - normed * jnp.mean(scaled * normed, axis=-1, keepdims=True)
        )
        dz_ref[rows, :] = dz
        low_ref[rows, :] = bfloat(dz)

    tiles(body, n_ref.shape[0], ROWS)


def project_kernel(n, height, offsets, x_ref, far_ref, *refs):
    count = len(offsets)
    pieces, outs, full, (weight, *sems) = refs[:n], refs[n:-6], refs[-6], refs[-5:]
    loader = Loader(sems)
    for j, offset in enumerate(offsets):
        loader.fetch(pieces, offset, height, weight.at[j])
    for j in range(count):
        loader.arrived(j, weight.at[j], full.at[j])
        far = outs[count + j - (count - 2)] if j >= count - 2 else None

        def body(columns):
            outs[j][:, columns] = bfloat(product(x_ref[...], weight[j, :, columns]))
            if far is not None:
                far[:, columns] = bfloat(product(far_ref[...], weight[j, :, columns]))

        tiles(body, outs[j].shape[1], TILE)
    loader.finish()


def settle_kernel(n, height, wo_at, q_at, gain_rows, x_ref, mix_ref, gains_ref, *refs):
    pieces, refs = refs[:n], refs[n:]
    if q_at is None:
        n_ref, r_ref, full, weight, z_ref, *sems = refs
        low_ref = None
    else:
        n_ref, r_ref, q_ref, full, weight, z_ref, low_ref, *sems = refs
    loader = Loader(sems)
    loader.fetch(pieces, wo_at, height, weight.at[0])
    if q_at is not None:
        loader.fetch(pieces, q_at, height, weight.at[1])
    loader.arrived(0, weight.at[0], full.at[0])

    def project(columns):
        x = x_ref[:, columns].astype(jnp.float32)
        if gain_rows[0] is not None:
            x = x * gains_ref[pl.ds(gain_rows[0], 1), columns]
        z_ref[:, columns] = x + product(mix_ref[...], weight[0, :, columns])

    tiles(project, z_ref.shape[1], TILE)
    gain = gains_ref[pl.ds(gain_rows[1], 1), :]
    normalise(z_ref, n_ref, r_ref, gain, low_ref)
    if q_at is not None:
        loader.arrived(1, weight.at[1], full.at[1])

        def query(columns):
            q_ref[:, columns] = bfloat(product(low_ref[...], weight[1, :, columns]))

        tiles(query, q_ref.shape[1], TILE)
    loader.finish()


def tail_up_kernel(n, height, up_at, gain_row, n_ref, gains_ref, *refs):
    pieces = refs[:n]
    slope_hbm, inner_hbm, full, up, low_ref, slope_ref, inner_ref, out_sem, *sems = refs[n:]
    blocks = up.shape[0]
    loader = Loader(sems)
    for j in range(blocks):
        loader.fetch(pieces, up_at + j * height, height, up.at[j])
    gain = gains_ref[pl.ds(gain_row, 1), :]

    def lower(rows):
        low_ref[rows, :] = bfloat(n_ref[rows, :] * gain)

    tiles(lower, n_ref.shape[0], ROWS)
    width = up.shape[2]
    outs = []
    for j in range(blocks):
        loader.arrived(j, up.at[j], full.at[j])

        def upward(columns):
            inner, slope = gelu_both(product(low_ref[...], up[j, :, columns]))
            place = pl.ds(pl.multiple_of(j * width + columns.start, TILE), TILE)
            inner_ref[:, place] = bfloat(inner)
            slope_ref[:, place] = bfloat(slope)

        tiles(upward, width, TILE)
        columns = pl.ds(j * width, width)
        for i, (ref, hbm) in enumerate(((inner_ref, inner_hbm), (slope_ref, slope_hbm))):
            out = pltpu.make_async_copy(ref.at[:, columns], hbm.at[:, columns], out_sem.at[i, j])
            out.start()
            outs.append(out)
    loader.finish()
    for out in outs:
        out.wait()


def tail_down_kernel(n, height, offsets, gain_rows, n_ref, inner_ref, gains_ref, first_ref, second_ref, *refs):
    pieces, refs = refs[:n], refs[n:]
    pre_slope_ref, adapt_ref, n_out_ref, r_out_ref, out_ref, down_full, adapt_full = refs[:7]
    down, adapt, low_ref, z_ref, *sems = refs[7:]
    down_at, adapt_at = offsets
    width = z_ref.shape[1]
    loader = Loader(sems)
    loader.fetch(pieces, adapt_at, height, adapt)
    for at in range(0, width, TILE):
        loader.fetch(pieces, down_at, down.shape[0] // width * height, down, pl.ds(at, TILE))
    gain = gains_ref[pl.ds(gain_rows[0], 1), :]

    def lower(rows):
        low_ref[rows, :] = bfloat(n_ref[rows, :] * gain)

    tiles(lower, n_ref.shape[0], ROWS)
    loader.arrived(0, adapt, adapt_full)

    def adapting(columns):
        pre = product(low_ref[...], adapt[:, columns]) + first_ref[:, columns]
        adapted, slope = gelu_both(pre)
        adapt_ref[:, columns] = bfloat(adapted)
        pre_slope_ref[:, columns] = bfloat(slope)

    tiles(adapting, ADAPT, TILE)
    for i, at in enumerate(range(0, width, TILE)):
        columns = pl.ds(at, TILE)
        loader.arrived(1 + i, down.at[:, columns], down_full.at[:, columns])
        h = n_ref[:, columns] * gains_ref[pl.ds(gain_rows[0], 1), columns]
        ffn = product(inner_ref[...], down[:, columns])
        adapted = product_t(adapt_ref[...], adapt[columns, ADAPT:]) + second_ref[:, columns]
        z_ref[:, columns] = h + ffn + 4.0 * adapted
    normalise(z_ref, n_out_ref, r_out_ref, gains_ref[pl.ds(gain_rows[1], 1), :], out_ref)
    loader.finish()


def tail_back_kernel(height, gain_rows, more, *refs):
    (cot_ref, n2_ref, r2_ref, n1_ref, r1_ref, gains_ref, slope_hbm, pre_slope_ref, adapt_low_ref) = refs[:9]
    refs = refs[9:]
    (up_hbm, down_hbm, adapt_hbm, wo_hbm), refs = refs[:4], refs[4:]
    if more:
        far_ref, refs = refs[0], refs[1:]
    out_ref, dz_ref, dmix_ref, matrices_ref, g_first_ref, g_second_ref = refs[:6]
    up, down, adapt, wo, dt_ref, e_ref, low_ref, du_ref, dpre_ref, sem = refs[6:]
    blocks = up.shape[0]
    load(
        [adapt_hbm, down_hbm, slope_hbm, up_hbm, wo_hbm.at[0]],
        [adapt, down, du_ref, up, wo],
        sem,
    )
    gain1 = gains_ref[pl.ds(gain_rows[0], 1), :]
    gain2 = gains_ref[pl.ds(gain_rows[1], 1), :]

    def lower(rows):
        low_ref[rows, :] = bfloat(n1_ref[rows, :] * gain1)
        out_ref[rows, :] = bfloat(n2_ref[rows, :] * gain2)

    tiles(lower, n1_ref.shape[0], ROWS)

    def arriving(rows):
        grad = cot_ref[rows, :].astype(jnp.float32)
        return grad + far_ref[rows, :].astype(jnp.float32) if more else grad

    normalise_back(arriving, n2_ref, r2_ref, gain2, dt_ref, e_ref)
    loaded(adapt, sem.at[0])

    def adapting(columns):
        back = 4.0 * product(e_ref[...], adapt[:, pl.ds(ADAPT + columns.start, TILE)])
        dpre_ref[:, columns] = bfloat(back * pre_slope_ref[:, columns].astype(jnp.float32))

    tiles(adapting, ADAPT, TILE)
    g_first_ref[...] = jnp.sum(dpre_ref[...].astype(jnp.float32), axis=0, keepdims=True)
    g_second_ref[...] = 4.0 * jnp.sum(e_ref[...].astype(jnp.float32), axis=0, keepdims=True)

    wide = max(height, STAT)

    def matrices(columns):
        down_grad = bfloat(product_rows(low_ref[:, columns], dpre_ref[...]))
        up_grad = bfloat(4.0 * product_rows(e_ref[:, columns], adapt_low_ref[...]))
        for i in range(wide // height):
            block, rows = columns.start // height + i, slice(i * height, (i + 1) * height)
            matrices_ref[block, :height, :] = down_grad[rows, :]
            matrices_ref[block, height:, :] = up_grad[rows, :]

    tiles(matrices, low_ref.shape[1], wide)
    loaded(down, sem.at[1])
    loaded(du_ref, sem.at[2])

    def inner(columns):
        back = product_t(e_ref[...], down[columns, :])
        du_ref[:, columns] = bfloat(back * du_ref[:, columns].astype(jnp.float32))

    tiles(inner, du_ref.shape[1], TILE)
    loaded(up, sem.at[3])
    width = up.shape[2]

    def hidden(columns):
        total = dt_ref[:, columns] + product_t(dpre_ref[...], adapt[columns, :ADAPT])
        for j in range(blocks):
            total += product_t(du_ref[:, j * width : (j + 1) * width], up[j, columns, :])
        dt_ref[:, columns] = total

    tiles(hidden, dt_ref.shape[1], TILE)
    normalise_back(lambda rows: dt_ref[rows, :], n1_ref, r1_ref, gain1, dz_ref, e_ref)
    loaded(wo, sem.at[4])

    def mixing(columns):
        dmix_ref[:, columns] = bfloat(product_t(e_ref[...], wo[columns, :]))

    tiles(mixing, dmix_ref.shape[1], TILE)


def query_back_kernel(gain_row, dz_ref, dq_ref, n_ref, r_ref, gains_ref, weights, *refs):
    dz_out_ref, dmix_ref, weight, dy_ref, e_ref, sem = refs
    load([weights.at[1], weights.at[0]], [weight.at[0], weight.at[1]], sem)
    loaded(weight.at[0], sem.at[0])

    def back(columns):
        dy_ref[:, columns] = dz_ref[:, columns] + product_t(dq_ref[...], weight[0, columns, :])

    tiles(back, dy_ref.shape[1], TILE)
    gain = gains_ref[pl.ds(gain_row, 1), :]
    normalise_back(lambda rows: dy_ref[rows, :], n_ref, r_ref, gain, dz_out_ref, e_ref)
    loaded(weight.at[1], sem.at[1])

    def mixing(columns):
        dmix_ref[:, columns] = bfloat(product_t(e_ref[...], weight[1, columns, :]))

    tiles(mixing, dmix_ref.shape[1], TILE)


def back_kernel(indices, bases, *refs):
    count = len(indices)
    base_refs, grads = refs[:bases], refs[bases : bases + count]
    weights, out_ref, weight, sem = refs[bases + count :]
    load([weights.at[i] for i in indices], [weight.at[j] for j in range(count)], sem)
    for j in range(count):
        loaded(weight.at[j], sem.at[j])

    def back(columns):
        total = None
        for base in base_refs:
            part = base[:, columns].astype(jnp.float32)
            total = part if total is None else total + part
        for j in range(count):
            part = product_t(grads[j][...], weight[j, columns, :])
            total = part if total is None else total + part
        out_ref[:, columns] = total.astype(out_ref.dtype)

    tiles(back, out_ref.shape[1], TILE)


def split(value):
    high = bfloat(value)
    return high, bfloat(value - high.astype(jnp.float32))


def put_left(ref, value):
    high, low = split(value)
    ref[:, :ADAPT] = high
    ref[:, ADAPT : 2 * ADAPT] = high
    ref[:, 2 * ADAPT :] = low


def put_right(ref, value):
    high, low = split(value)
    ref[:ADAPT, :] = high
    ref[ADAPT : 2 * ADAPT, :] = low
    ref[2 * ADAPT :, :] = high


def multiply(out_ref, left, right):
    def body(columns):
        out_ref[:, columns] = product(left[...], right[:, columns])

    tiles(body, ADAPT, TILE)


def muon_kernel(parts, *refs):
    rows_refs, (out_ref, high, low, gram, poly, factor, left, right, rows_left) = refs[:parts], refs[parts:]
    rows = rows_refs[0].shape[0]
    for i, ref in enumerate(rows_refs):
        high[i * rows : (i + 1) * rows, :], low[i * rows : (i + 1) * rows, :] = split(ref[...])

    def square(columns):
        gram[:, columns] = (
            product_rows(high[...], high[:, columns])
            + product_rows(high[...], low[:, columns])
            + product_rows(low[...], high[:, columns])
        )

    tiles(square, ADAPT, TILE)
    eye = lax.broadcasted_iota(jnp.int32, (ADAPT, ADAPT), 0) == lax.broadcasted_iota(
        jnp.int32, (ADAPT, ADAPT), 1
    )
    scale = 1.0 / (jnp.sqrt(jnp.sum(jnp.where(eye, gram[...], 0.0), keepdims=True)) + 1e-07)
    gram[...] = gram[...] * (scale * scale)

    def polynomial():
        put_left(left, gram[...])
        put_right(right, gram[...])
        multiply(poly, left, right)
        poly[...] = (
            jnp.where(eye, NEWTON_LINEAR, 0.0) + NEWTON_QUADRATIC * gram[...] + NEWTON_CUBIC * poly[...]
        )
        put_right(right, poly[...])

    def advance():
        multiply(gram, left, right)
        put_left(left, gram[...])
        multiply(gram, left, right)

    polynomial()
    factor[...] = poly[...]
    advance()

    @pl.loop(0, NS_ITERS - 2)
    def _(i):
        polynomial()
        advance()
        put_left(left, factor[...])
        multiply(factor, left, right)

    polynomial()
    put_left(left, factor[...])
    multiply(factor, left, right)
    put_right(right, factor[...])
    put_left(rows_left, rows_refs[0][...] * scale)
    multiply(out_ref, rows_left, right)


HBM = pl.BlockSpec(memory_space=pltpu.HBM)
IN_VMEM = pl.BlockSpec(memory_space=pltpu.VMEM)
F32, BF16 = jnp.float32, jnp.bfloat16


def call(kernel, ins, specs, outs, scratch, flops, collective_id=None, after=()):
    if after:
        inner, first = kernel, len(ins)
        kernel = lambda *refs: inner(*refs[:first], *refs[first + len(after) :])
        ins, specs = [*ins, *after], [*specs, *[HBM] * len(after)]
    return pl.pallas_call(
        kernel,
        in_specs=specs,
        out_specs=[IN_VMEM if len(out) == 2 else HBM for out in outs],
        out_shape=[jax.ShapeDtypeStruct(*out[:2]) for out in outs],
        scratch_shapes=scratch,
        compiler_params=pltpu.CompilerParams(
            vmem_limit_bytes=VMEM_LIMIT,
            collective_id=collective_id,
            has_side_effects=collective_id is not None,
        ),
        cost_estimate=pl.CostEstimate(
            flops=flops, bytes_accessed=sum(a.size * a.dtype.itemsize for a in ins), transcendentals=0
        ),
    )(*ins)


def squares(count):
    return pltpu.VMEM((count, D, D), BF16)


def stored(*shape):
    return (shape, BF16, HBM)


def project(collective_id, x, far, pieces, offsets):
    rows = x.shape[0]
    count, n = len(offsets), len(pieces.arrays)
    return call(
        functools.partial(project_kernel, n, pieces.height, offsets),
        [x, far, *pieces.arrays],
        [IN_VMEM] * 2 + [HBM] * n,
        [((rows, D), BF16)] * (count + 2) + [stored(count, D, D)],
        [squares(count), *loader_sems(count, n)],
        2 * rows * D * D * (count + 2),
        collective_id,
    )


def settle(collective_id, x, mix, gains, pieces, wo_at, q_at, gain_rows, after=()):
    rows = x.shape[0]
    n = len(pieces.arrays)
    count = 1 if q_at is None else 2
    outs = [((rows, D), F32), ((rows, STAT), F32)]
    scratch = [squares(count), pltpu.VMEM((rows, D), F32)]
    if q_at is not None:
        outs.append(((rows, D), BF16))
        scratch.append(pltpu.VMEM((rows, D), BF16))
    return call(
        functools.partial(settle_kernel, n, pieces.height, wo_at, q_at, gain_rows),
        [x, mix, gains, *pieces.arrays],
        [IN_VMEM] * 3 + [HBM] * n,
        outs + [stored(count, D, D)],
        scratch + loader_sems(count, n),
        2 * rows * D * D * count,
        collective_id,
        after,
    )


def tail_up(collective_id, normed, gains, pieces, up_at, gain_row):
    rows = normed.shape[0]
    n = len(pieces.arrays)
    blocks = 4
    hidden = blocks * D
    return call(
        functools.partial(tail_up_kernel, n, pieces.height, up_at, gain_row),
        [normed, gains, *pieces.arrays],
        [IN_VMEM] * 2 + [HBM] * n,
        [stored(rows, hidden), stored(rows, hidden), stored(blocks, D, D)],
        [
            squares(blocks),
            pltpu.VMEM((rows, D), BF16),
            pltpu.VMEM((rows, hidden), BF16),
            pltpu.VMEM((rows, hidden), BF16),
            pltpu.SemaphoreType.DMA((2, blocks)),
            *loader_sems(blocks, n),
        ],
        8 * rows * D * D,
        collective_id,
    )


def tail_down(collective_id, normed, inner, gains, bias_first, bias_second, pieces, offsets, gain_rows):
    rows, hidden = inner.shape
    n = len(pieces.arrays)
    return call(
        functools.partial(tail_down_kernel, n, pieces.height, offsets, gain_rows),
        [normed, inner, gains, bias_first[None], bias_second[None], *pieces.arrays],
        [IN_VMEM] * 5 + [HBM] * n,
        [
            ((rows, ADAPT), BF16),
            ((rows, ADAPT), BF16),
            ((rows, D), F32),
            ((rows, STAT), F32),
            ((rows, D), BF16),
            stored(hidden, D),
            stored(D, D),
        ],
        [
            pltpu.VMEM((hidden, D), BF16),
            pltpu.VMEM((D, D), BF16),
            pltpu.VMEM((rows, D), BF16),
            pltpu.VMEM((rows, D), F32),
            *loader_sems(1 + D // TILE, n),
        ],
        10 * rows * D * D,
        collective_id,
    )


def tail_back(height, cot, second, first, gains, slope, pre_slope, adapt_low, weights, gain_rows, more=()):
    rows = cot.shape[0]
    hidden = slope.shape[1]
    return call(
        functools.partial(tail_back_kernel, height, gain_rows, bool(more)),
        [cot, *second, *first, gains, slope, pre_slope, adapt_low, *weights, *more],
        [IN_VMEM] * 6 + [HBM] + [IN_VMEM] * 2 + [HBM] * 4 + [IN_VMEM] * len(more),
        [
            ((rows, D), BF16),
            ((rows, D), F32),
            ((rows, D), BF16),
            ((D // height, 2 * height, ADAPT), BF16),
            ((1, ADAPT), F32),
            ((1, D), F32),
        ],
        [
            squares(hidden // D),
            pltpu.VMEM((hidden, D), BF16),
            pltpu.VMEM((D, D), BF16),
            pltpu.VMEM((D, D), BF16),
            pltpu.VMEM((rows, D), F32),
            pltpu.VMEM((rows, D), BF16),
            pltpu.VMEM((rows, D), BF16),
            pltpu.VMEM((rows, hidden), BF16),
            pltpu.VMEM((rows, ADAPT), BF16),
            pltpu.SemaphoreType.DMA((5,)),
        ],
        24 * rows * D * D,
    )


def query_back(dz, dq, first, gains, weights, gain_row):
    rows = dz.shape[0]
    return call(
        functools.partial(query_back_kernel, gain_row),
        [dz, dq, *first, gains, weights],
        [IN_VMEM] * 5 + [HBM],
        [((rows, D), F32), ((rows, D), BF16)],
        [
            squares(2),
            pltpu.VMEM((rows, D), F32),
            pltpu.VMEM((rows, D), BF16),
            pltpu.SemaphoreType.DMA((2,)),
        ],
        4 * rows * D * D,
    )


def back(bases, grads, weights, indices, dtype):
    rows = grads[0].shape[0]
    count = len(indices)
    return call(
        functools.partial(back_kernel, indices, len(bases)),
        [*bases, *grads, weights],
        [IN_VMEM] * (len(bases) + count) + [HBM],
        [((rows, D), dtype)],
        [squares(count), pltpu.SemaphoreType.DMA((count,))],
        2 * rows * D * D * count,
    )[0]


def muon(parts):
    rows = parts[0].shape[0]
    full = pltpu.VMEM((ADAPT, ADAPT), F32)
    return call(
        functools.partial(muon_kernel, len(parts)),
        parts,
        [IN_VMEM] * len(parts),
        [((rows, ADAPT), F32)],
        [
            pltpu.VMEM((rows * len(parts), ADAPT), BF16),
            pltpu.VMEM((rows * len(parts), ADAPT), BF16),
            full,
            full,
            full,
            pltpu.VMEM((ADAPT, 3 * ADAPT), BF16),
            pltpu.VMEM((3 * ADAPT, ADAPT), BF16),
            pltpu.VMEM((rows, 3 * ADAPT), BF16),
        ],
        20 * 6 * ADAPT**3,
    )[0]


def axis_bits(axis):
    return [1 << b for b in range(lax.axis_size(axis).bit_length() - 1)]


def tie(array, *others):
    return lax.optimization_barrier((array, *others))[0]


class Gather:
    def __init__(self, array, height):
        self.height = height
        self.array = array

    def begin(self, *after):
        array = tie(self.array, *after) if after else self.array
        bits = axis_bits("wide")
        self.pieces = {0: self.array}
        for bit in bits[1:3]:
            self.pieces[bit] = swap(array, "wide", bit)
        return self

    def across(self, *after):
        bits = axis_bits("wide")
        near, far = bits[1:3]
        pieces = self.pieces
        even = lax.axis_index("wide") % 2 == 0
        first, second = pieces[near], pieces[far]
        if after:
            first, second, *_ = lax.optimization_barrier((first, second, *after))
        pieces[near | far] = lax.ppermute(
            jnp.where(even, first, second),
            "wide",
            [(i, i ^ (near if i % 2 else far)) for i in range(lax.axis_size("wide"))],
        )
        for bit in bits[3:]:
            for r in list(pieces):
                pieces[r | bit] = swap(pieces[r], "wide", bit)
        self.arrays = [pieces[r] for r in range(0, lax.axis_size("wide"), 2)]
        return self

    def marks(self):
        return list(self.pieces.values())[1:3]


def gather_any_order(array, axis):
    blocks = array[None]
    for bit in axis_bits(axis):
        blocks = jnp.concatenate([blocks, swap(blocks, axis, bit)])
    return blocks


def shards(
    enc_in,
    dec_in,
    segment_ids,
    enc_cot,
    dec_cot,
    enc_qkv,
    enc_wo,
    enc_w_in,
    enc_w_out,
    enc_gains,
    dec_qkv,
    dec_wo,
    dec_w_in,
    dec_w_out,
    dec_gains,
    adapter_weights,
    adapter_momenta,
    bias_in,
    bias_out,
):
    height = enc_wo.shape[0]
    stack = lambda *arrays: jnp.concatenate([a.reshape(-1, D) for a in arrays])
    columns = lambda array: [array[:, j * D : (j + 1) * D] for j in range(array.shape[1] // D)]
    gain_rows = jnp.concatenate([enc_gains, dec_gains])
    gain_block = jnp.pad(gain_rows, ((0, 16 - gain_rows.shape[0]), (0, D - height)))
    gather = lambda array: Gather(array, height)
    enc_first = gather(stack(enc_qkv, gain_block))
    dec_first = gather(stack(dec_qkv[:3]))
    enc_up = gather(stack(enc_wo, *columns(enc_w_in)))
    dec_second = gather(stack(dec_wo, dec_qkv[3:]))
    dec_up = gather(stack(*columns(dec_w_in)))

    count = lax.axis_size("wide")
    partner = lambda array: swap(array, "narrow", 1)
    rows = enc_in.shape[0]
    half = (lax.axis_index("narrow") % 2).astype(jnp.int32).reshape(1)
    at = lambda i: i * height

    enc_first.begin()
    enc_far = partner(enc_in)
    enc_first.across()
    begun = enc_first.arrays[-1]
    dec_first.begin(begun)
    dec_far = partner(tie(dec_in, begun))
    other_ids = partner(tie(segment_ids, begun))
    places = (half, segment_ids.reshape(1, rows), segment_ids.reshape(rows, 1), other_ids.reshape(rows, 1))
    found = gather_any_order(bfloat(tie(adapter_weights, begun)), "narrow")
    found = found[lax.axis_index("narrow") ^ jnp.arange(lax.axis_size("narrow"))]
    adapters = found.transpose(1, 0, 2, 3).reshape(4, height, ADAPT)
    beside = lambda l: jnp.concatenate([adapters[2 * l], adapters[2 * l + 1]], axis=1)
    enc_query, enc_key, enc_value, enc_key_far, enc_value_far, enc_qkv_full = project(
        0, tie(enc_in, begun), enc_far, enc_first, (at(0), at(1), at(2))
    )
    enc_keys, enc_values = (enc_key, enc_key_far), (enc_value, enc_value_far)

    repeat = lax.axis_size("narrow") // 4
    spread = lambda array: jnp.repeat(array, repeat, axis=0) if repeat > 1 else array
    to_matrix = lambda array: lax.all_to_all(
        spread(array), "narrow", split_axis=0, concat_axis=1, tiled=True
    )[0]
    to_rows = lambda array: lax.all_to_all(
        array[None], "narrow", split_axis=1, concat_axis=0, tiled=True
    )[::repeat]

    dec_first.across(enc_value)
    enc_up.begin(enc_value)
    enc_mix, enc_lse = attend(places, enc_query, enc_keys, enc_values, False)
    found = jnp.stack([p[at(3) : at(3) + 8, :height] for p in enc_first.arrays])
    found = jnp.concatenate([found, swap(tie(found, enc_mix), "wide", 1)])
    order = lax.axis_index("wide") ^ jnp.arange(count)
    order = order // 2 + order % 2 * (count // 2)
    gains = found[order].transpose(1, 0, 2).reshape(8, D).astype(jnp.float32)
    enc_down = gather(stack(enc_w_out, tie(beside(0), enc_mix)))
    dec_down = gather(stack(dec_w_out, tie(beside(1), enc_mix)))
    enc_down.begin(enc_mix)
    self_query, self_key, self_value, self_key_far, self_value_far, dec_qkv_full = project(
        1, tie(dec_in, enc_mix), dec_far, dec_first, (at(0), at(1), at(2))
    )
    self_keys, self_values = (self_key, self_key_far), (self_value, self_value_far)
    enc_up.across(self_value)
    self_mix, self_lse = attend(places, self_query, self_keys, self_values, True)
    dec_second.begin(self_mix)
    *enc_norm1, enc_wo_full = settle(
        2, enc_in, tie(enc_mix, self_mix), gains, enc_up, at(0), None, (None, 0)
    )
    enc_down.across(enc_norm1[0])
    enc_slope, enc_inner, enc_up_full = tail_up(3, enc_norm1[0], gains, enc_up, at(1), 0)
    dec_up.begin(enc_inner)
    enc_pre_slope, enc_adapt, *enc_norm2, enc_low, enc_down_full, enc_adapt_full = tail_down(
        4, enc_norm1[0], enc_inner, gains, bias_in[0], bias_out[0], enc_down, (0, at(4)), (0, 1)
    )
    enc_low_far = partner(enc_low)
    dec_second.across(enc_low)
    *dec_norm1, cross_query, dec_q_full = settle(
        5, dec_in, tie(self_mix, enc_low), gains, dec_second, at(0), at(2), (None, 2)
    )
    dec_down.begin(cross_query)
    cross_key, cross_value, cross_key_far, cross_value_far, dec_kv_full = project(
        6, tie(enc_low, cross_query), enc_low_far, dec_second, (at(3), at(4))
    )
    cross_keys, cross_values = (cross_key, cross_key_far), (cross_value, cross_value_far)
    dec_up.across(cross_key)
    cross_mix, cross_lse = attend(places, cross_query, cross_keys, cross_values, False)
    dec_down.across(cross_mix)
    *dec_norm2, dec_wo_full = settle(
        7, dec_norm1[0], cross_mix, gains, dec_second, at(1), None, (2, 3)
    )
    dec_slope, dec_inner, dec_up_full = tail_up(8, dec_norm2[0], gains, dec_up, at(0), 3)
    dec_pre_slope, dec_adapt, *dec_norm3, _, dec_down_full, dec_adapt_full = tail_down(
        9, dec_norm2[0], dec_inner, gains, bias_in[1], bias_out[1], dec_down, (0, at(4)), (3, 4)
    )

    dec_out, grad_z2, grad_cross_mix, dec_matrices, grad_dec_first, grad_dec_second = tail_back(
        height,
        dec_cot,
        dec_norm3,
        dec_norm2,
        gains,
        dec_slope,
        dec_pre_slope,
        dec_adapt,
        (dec_up_full, dec_down_full, dec_adapt_full, dec_wo_full),
        (3, 4),
    )
    exchange = lambda array, axis: lax.all_to_all(array, axis, split_axis=0, concat_axis=0, tiled=True)
    total = lambda array: jnp.sum(array.astype(jnp.float32), axis=0)
    dec_matrices = exchange(dec_matrices, "wide")
    cross_back = attend_back(
        places, grad_cross_mix, cross_query, cross_keys, cross_values, cross_mix, cross_lse, False
    )
    dec_sums = total(tie(dec_matrices, cross_back[0]))
    far_encoded = back((), (tie(cross_back[2], dec_sums), cross_back[4]), dec_kv_full, (0, 1), BF16)
    near_encoded = partner(far_encoded)
    grad_encoded = back(
        (tie(enc_cot, far_encoded),), (cross_back[1], cross_back[3]), dec_kv_full, (0, 1), F32
    )
    grad_z1, grad_self_mix = query_back(
        tie(grad_z2, grad_encoded),
        cross_back[0],
        dec_norm1,
        gains,
        dec_q_full,
        2,
    )
    enc_out, grad_ez1, grad_enc_mix, enc_matrices, grad_enc_first, grad_enc_second = tail_back(
        height,
        tie(grad_encoded, grad_z1),
        enc_norm2,
        enc_norm1,
        gains,
        enc_slope,
        enc_pre_slope,
        enc_adapt,
        (enc_up_full, enc_down_full, enc_adapt_full, enc_wo_full),
        (0, 1),
        (near_encoded,),
    )
    old_momentum = to_matrix(tie(adapter_momenta, grad_z1))
    enc_matrices = exchange(tie(enc_matrices, old_momentum), "wide")

    self_back = attend_back(
        places, tie(grad_self_mix, grad_ez1), self_query, self_keys, self_values, self_mix, self_lse, True, (old_momentum,)
    )

    sums = jnp.concatenate([total(tie(enc_matrices, self_back[0])), dec_sums])
    sums = spread(bfloat(sums).reshape(4, height, ADAPT))
    enc_back = attend_back(
        places, tie(grad_enc_mix, sums), enc_query, enc_keys, enc_values, enc_mix, enc_lse, False
    )
    summed = exchange(sums, "narrow")
    momentum = DECAY * old_momentum + total(tie(summed, enc_back[0]))
    parts = [momentum] + [swap(momentum, "wide", r) for r in range(1, lax.axis_size("wide"))]
    new_momenta = to_rows(momentum)

    far_dec = back(
        (), (tie(self_back[2], momentum), self_back[4]), dec_qkv_full, (1, 2), BF16
    )
    near_dec = partner(far_dec)
    far_enc = back((), (tie(enc_back[2], far_dec), enc_back[4]), enc_qkv_full, (1, 2), BF16)
    near_enc = partner(far_enc)
    grad_dec = back(
        (tie(grad_z1, far_enc), near_dec),
        (self_back[0], self_back[1], self_back[3]),
        dec_qkv_full,
        (0, 1, 2),
        F32,
    )
    devices = lax.axis_size("wide") * lax.axis_size("narrow")
    slices = lambda first, second: jnp.concatenate([first, second]).reshape(2, devices, -1).transpose(1, 0, 2)
    firsts = slices(tie(grad_enc_first, far_enc), grad_dec_first)
    seconds = slices(tie(grad_enc_second, far_enc), grad_dec_second)
    biases = jnp.concatenate([firsts.reshape(devices, -1), seconds.reshape(devices, -1)], axis=1)
    used = biases.shape[1]
    biases = jnp.pad(biases, ((0, 0), (0, -used % STAT)))
    biases = jnp.sum(exchange(biases, ("wide", "narrow")), axis=0)[:used]
    grad_bias_in = biases[: firsts[0].size].reshape(firsts.shape[1:])
    grad_bias_out = biases[firsts[0].size :].reshape(seconds.shape[1:])

    orthogonal = muon([parts[0], tie(parts[1], grad_dec), *parts[2:]])
    grad_enc = back(
        (tie(grad_ez1, orthogonal), near_enc),
        (enc_back[0], enc_back[1], enc_back[3]),
        enc_qkv_full,
        (0, 1, 2),
        F32,
    )
    new_weights = adapter_weights - RATE * math.sqrt(max(1.0, D / ADAPT)) * to_rows(orthogonal)
    return (
        enc_out,
        dec_out,
        grad_enc,
        grad_dec,
        grad_bias_in,
        grad_bias_out,
        new_momenta,
        new_weights,
    )


def solution(mesh):
    both = ("wide", "narrow")
    tokens = P(both, None)
    rows_first, rows_second = P("wide", None), P(None, "wide", None)
    adapters = P(None, both, None)
    in_specs = (
        tokens,
        tokens,
        P(both),
        tokens,
        tokens,
        rows_second,
        rows_first,
        rows_first,
        rows_first,
        P(None, "wide"),
        rows_second,
        rows_second,
        rows_first,
        rows_first,
        P(None, "wide"),
        adapters,
        adapters,
        P(),
        P(),
    )
    out_specs = (
        tokens,
        tokens,
        tokens,
        tokens,
        P(None, both),
        P(None, both),
        adapters,
        adapters,
    )
    return jax.shard_map(shards, mesh=mesh, in_specs=in_specs, out_specs=out_specs, check_vma=False)
```

```python
import functools
import math

import jax
import jax.numpy as jnp
from jax import lax
from jax.experimental import pallas as pl
from jax.experimental.pallas import tpu as pltpu
from jax.sharding import PartitionSpec as P

D = 1024
HD = 64
ADAPT = 512
NS_ITERS = 5

EPSILON = 1e-05
MASKED = -1e30
NEWTON_LINEAR = 3.4445
NEWTON_QUADRATIC = -4.775
NEWTON_CUBIC = 2.0315
RATE = 0.7
DECAY = 0.5
LOG2E = 1.4426950408889634
PAIR = 2 * HD
VMEM_LIMIT = 58 * 1024 * 1024
MESH = pl.DeviceIdType.MESH


def swap(array, axis, bit):
    return lax.ppermute(array, axis, [(i, i ^ bit) for i in range(lax.axis_size(axis))])


def bfloat(tensor):
    return tensor.astype(jnp.bfloat16)


def product(left_side, right_side):
    return jnp.dot(left_side, right_side, preferred_element_type=jnp.float32)


def contract(left_side, right_side, left_dim, right_dim):
    return lax.dot_general(
        left_side,
        right_side,
        (((left_dim,), (right_dim,)), ((), ())),
        preferred_element_type=jnp.float32,
    )


def product_t(left_side, right_side):
    return contract(left_side, right_side, 1, 1)


def product_rows(left_side, right_side):
    return contract(left_side, right_side, 0, 0)


def gelu_both(tensor):
    phi = 0.5 * (1.0 + lax.erf(tensor * 0.7071067811865476))
    slope = phi + tensor * jnp.exp(-0.5 * tensor * tensor) * 0.3989422804014327
    return tensor * phi, slope


def fill_bias(half_ref, qid_ref, kid_own_ref, kid_far_ref, bias_ref, causal):
    rows = qid_ref.shape[1]
    qid = qid_ref[...]
    for part, kid_ref in enumerate((kid_own_ref, kid_far_ref)):
        allowed = kid_ref[...] == qid
        if causal:
            if part == 0:
                key_at = lax.broadcasted_iota(jnp.int32, (rows, rows), 0)
                query_at = lax.broadcasted_iota(jnp.int32, (rows, rows), 1)
                allowed = allowed & (key_at <= query_at)
            else:
                allowed = allowed & (half_ref[0] == 1)
        bias_ref[pl.ds(part * rows, rows), :] = jnp.where(allowed, 0.0, MASKED)


def head_mask(rows, head):
    return lax.broadcasted_iota(jnp.int32, (rows, PAIR), 1) // HD == head


def attend_kernel(
    causal,
    chunk,
    half_ref,
    qid_ref,
    kid_own_ref,
    kid_far_ref,
    q_ref,
    k_own_ref,
    k_far_ref,
    v_own_ref,
    v_far_ref,
    out_ref,
    lse_ref,
    bias_ref,
    score_ref,
):
    rows = q_ref.shape[0]

    @pl.when(pl.program_id(0) == 0)
    def _():
        fill_bias(half_ref, qid_ref, kid_own_ref, kid_far_ref, bias_ref, causal)

    queries = q_ref[...] * 0.125
    steps = [
        (part, at)
        for part in range(2)
        for at in range(0, rows, chunk)
    ]
    keys = (k_own_ref, k_far_ref)
    values = (v_own_ref, v_far_ref)
    mixes = []
    for head in range(2):
        q_head = jnp.where(head_mask(rows, head), queries, jnp.zeros_like(queries))
        peak = None
        for part, at in steps:
            place = pl.ds(part * rows + at, chunk)
            scores = product_t(keys[part][pl.ds(at, chunk), :], q_head)
            scores = scores * LOG2E + bias_ref[place, :]
            score_ref[head, place, :] = scores
            top = jnp.max(scores, axis=0, keepdims=True)
            peak = top if peak is None else jnp.maximum(peak, top)
        total, mix = None, None
        for part, at in steps:
            place = pl.ds(part * rows + at, chunk)
            raised = jnp.exp2(score_ref[head, place, :] - peak)
            share = jnp.sum(raised, axis=0, keepdims=True)
            piece = product_rows(values[part][pl.ds(at, chunk), :], bfloat(raised))
            total = share if total is None else total + share
            mix = piece if mix is None else mix + piece
        mixes.append((mix * (1.0 / total))[head * HD : (head + 1) * HD, :])
        lse_ref[0, pl.ds(head, 1), :] = peak + jnp.log2(total)
    out_ref[...] = bfloat(jnp.concatenate(mixes, axis=0).T)


def attend_back_kernel(
    causal,
    chunk,
    half_ref,
    qid_ref,
    kid_own_ref,
    kid_far_ref,
    q_ref,
    k_own_ref,
    k_far_ref,
    v_own_ref,
    v_far_ref,
    out_ref,
    grad_ref,
    lse_ref,
    dq_ref,
    dk_own_ref,
    dk_far_ref,
    dv_own_ref,
    dv_far_ref,
    bias_ref,
):
    rows = q_ref.shape[0]

    @pl.when(pl.program_id(0) == 0)
    def _():
        fill_bias(half_ref, qid_ref, kid_own_ref, kid_far_ref, bias_ref, causal)

    queries = q_ref[...] * 0.125
    grads = grad_ref[...]
    products = (grads.astype(jnp.float32) * out_ref[...].astype(jnp.float32)).T
    q_heads, g_heads, deltas, lses = [], [], [], []
    for head in range(2):
        chosen = head_mask(rows, head)
        q_heads.append(jnp.where(chosen, queries, jnp.zeros_like(queries)))
        g_heads.append(jnp.where(chosen, grads, jnp.zeros_like(grads)))
        deltas.append(jnp.sum(products[head * HD : (head + 1) * HD, :], axis=0, keepdims=True))
        lses.append(lse_ref[0, pl.ds(head, 1), :])
    grad_q = [None, None]
    for part in range(2):
        key_ref = (k_own_ref, k_far_ref)[part]
        value_ref = (v_own_ref, v_far_ref)[part]
        dk_ref = (dk_own_ref, dk_far_ref)[part]
        dv_ref = (dv_own_ref, dv_far_ref)[part]
        for at in range(0, rows, chunk):
            here = pl.ds(at, chunk)
            keys, values = key_ref[here, :], value_ref[here, :]
            grad_k, grad_v = None, None
            for head in range(2):
                scores = product_t(keys, q_heads[head])
                bias = bias_ref[pl.ds(part * rows + at, chunk), :]
                weights = jnp.exp2(scores * LOG2E + (bias - lses[head]))
                grad_w = product_t(values, g_heads[head])
                grad_s = bfloat(weights * (grad_w - deltas[head]))
                piece_v = product(bfloat(weights), g_heads[head])
                piece_k = product(grad_s, q_heads[head])
                piece_q = product_rows(keys, grad_s)
                grad_v = piece_v if grad_v is None else grad_v + piece_v
                grad_k = piece_k if grad_k is None else grad_k + piece_k
                grad_q[head] = piece_q if grad_q[head] is None else grad_q[head] + piece_q
            dk_ref[here, :] = grad_k.astype(dk_ref.dtype)
            dv_ref[here, :] = grad_v.astype(dv_ref.dtype)
    joined = jnp.concatenate([grad_q[h][h * HD : (h + 1) * HD, :] for h in range(2)], axis=0)
    dq_ref[...] = bfloat((joined * 0.125).T)


def attention_specs(rows):
    whole = lambda shape: pl.BlockSpec(shape, lambda i: (0,) * len(shape))
    columns = pl.BlockSpec((rows, PAIR), lambda i: (0, i))
    fixed = [
        pl.BlockSpec(memory_space=pltpu.SMEM),
        whole((1, rows)),
        whole((rows, 1)),
        whole((rows, 1)),
    ]
    return fixed, columns, pl.BlockSpec((1, 8, rows), lambda i: (i, 0, 0))


def attend(places, queries, keys, values, causal):
    rows, width = queries.shape
    pairs = width // PAIR
    fixed, columns, stat = attention_specs(rows)
    return pl.pallas_call(
        functools.partial(attend_kernel, causal, 256),
        grid=(pairs,),
        in_specs=fixed + [columns] * 5,
        out_specs=[columns, stat],
        out_shape=[
            jax.ShapeDtypeStruct((rows, width), jnp.bfloat16),
            jax.ShapeDtypeStruct((pairs, 8, rows), jnp.float32),
        ],
        scratch_shapes=[
            pltpu.VMEM((2 * rows, rows), jnp.float32),
            pltpu.VMEM((2, 2 * rows, rows), jnp.float32),
        ],
        compiler_params=pltpu.CompilerParams(vmem_limit_bytes=VMEM_LIMIT),
        cost_estimate=pl.CostEstimate(
            flops=32 * rows * rows * width, bytes_accessed=12 * rows * width, transcendentals=0
        ),
    )(*places, queries, *keys, *values)


def attend_back(places, grad_out, queries, keys, values, mix, lse, causal, after=()):
    rows, width = queries.shape
    pairs = width // PAIR
    fixed, columns, stat = attention_specs(rows)
    return pl.pallas_call(
        lambda *refs: attend_back_kernel(causal, 256, *refs[:12], *refs[12 + len(after) :]),
        grid=(pairs,),
        in_specs=fixed + [columns] * 7 + [stat] + [HBM] * len(after),
        out_specs=[columns] * 5,
        out_shape=[
            jax.ShapeDtypeStruct((rows, width), jnp.bfloat16),
        ]
        * 5,
        scratch_shapes=[pltpu.VMEM((2 * rows, rows), jnp.float32)],
        compiler_params=pltpu.CompilerParams(vmem_limit_bytes=VMEM_LIMIT),
        cost_estimate=pl.CostEstimate(
            flops=80 * rows * rows * width, bytes_accessed=24 * rows * width, transcendentals=0
        ),
    )(*places, queries, *keys, *values, mix, grad_out, lse, *after)


def flipped(me, bits):
    place = me
    bit = 1
    while bit <= bits:
        if bits & bit:
            place = place + bit * (1 - 2 * lax.rem(lax.div(me, bit), 2))
        bit *= 2
    return place


def place_of(me, piece):
    odd = lax.rem(me, 2)
    place = me
    if piece % 4 in (1, 2):
        first, second = (2, 4) if piece % 4 == 1 else (4, 2)
        place = flipped(me, first) * (1 - odd) + flipped(me, second) * odd
    elif piece % 4 == 3:
        place = flipped(me, 6)
    return place + (flipped(me, 2 * (piece - piece % 4)) - me)


class Loader:
    def __init__(self, sems):
        self.local, self.send, self.recv, self.stored = sems
        self.copies, self.stores = [], []
        self.me = lax.axis_index("wide")
        self.sibling = {"wide": flipped(self.me, 1)}
        barrier = pltpu.get_barrier_semaphore()
        pl.semaphore_signal(barrier, inc=1, device_id=self.sibling, device_id_type=MESH)
        pl.semaphore_wait(barrier, 1)

    def fetch(self, pieces, offset, height, target, columns=slice(None)):
        block = len(self.copies)
        copies = []
        for i, piece in enumerate(pieces):
            at = pl.multiple_of(place_of(self.me, i) * height, height)
            source = piece.at[pl.ds(offset, height), columns]
            place = target.at[pl.ds(at, height), columns]
            near = pltpu.make_async_copy(source, place, self.local.at[block, i])
            far = pltpu.make_async_remote_copy(
                source,
                place,
                self.send.at[block, i],
                self.recv.at[block, i],
                device_id=self.sibling,
                device_id_type=MESH,
            )
            near.start()
            far.start()
            copies.append((near, far))
        self.copies.append(copies)
        return block

    def arrived(self, block, target, out):
        for near, far in self.copies[block]:
            near.wait()
            far.wait_recv()
        store = pltpu.make_async_copy(target, out, self.stored.at[block])
        store.start()
        self.stores.append(store)

    def finish(self):
        for copies in self.copies:
            for _, far in copies:
                far.wait_send()
        for store in self.stores:
            store.wait()


def loader_sems(blocks, pieces):
    dma = pltpu.SemaphoreType.DMA
    return [dma((blocks, pieces))] * 3 + [dma((blocks,))]


def load(weights, targets, sem):
    for j, (weight, target) in enumerate(zip(weights, targets)):
        pltpu.make_async_copy(weight, target, sem.at[j]).start()


def loaded(target, sem):
    pltpu.make_async_copy(target, target, sem).wait()


def tiles(body, width, step):
    @pl.loop(0, width // step)
    def _(i):
        body(pl.ds(pl.multiple_of(i * step, step), step))


ROWS = 64
TILE = 512
STAT = 128
BIAS_ROWS = 16


def normalise(z_ref, n_ref, r_ref, gain, low_ref):
    def body(rows):
        z = z_ref[rows, :]
        centred = z - jnp.mean(z, axis=-1, keepdims=True)
        inverse = lax.rsqrt(jnp.mean(centred * centred, axis=-1, keepdims=True) + EPSILON)
        normed = centred * inverse
        n_ref[rows, :] = normed
        r_ref[rows, :] = jnp.broadcast_to(inverse, (ROWS, STAT))
        if low_ref is not None:
            low_ref[rows, :] = bfloat(normed * gain)

    tiles(body, z_ref.shape[0], ROWS)


def normalise_back(read_grad, n_ref, r_ref, gain, dz_ref, low_ref):
    def body(rows):
        scaled = read_grad(rows) * gain
        normed = n_ref[rows, :]
        dz = r_ref[rows, :][:, :1] * (
            scaled
            - jnp.mean(scaled, axis=-1, keepdims=True)
            - normed * jnp.mean(scaled * normed, axis=-1, keepdims=True)
        )
        dz_ref[rows, :] = dz
        low_ref[rows, :] = bfloat(dz)

    tiles(body, n_ref.shape[0], ROWS)


def project_kernel(n, height, offsets, x_ref, far_ref, *refs):
    count = len(offsets)
    pieces, outs, full, (weight, *sems) = refs[:n], refs[n:-6], refs[-6], refs[-5:]
    loader = Loader(sems)
    for j, offset in enumerate(offsets):
        loader.fetch(pieces, offset, height, weight.at[j])
    for j in range(count):
        loader.arrived(j, weight.at[j], full.at[j])
        far = outs[count + j - (count - 2)] if j >= count - 2 else None

        def body(columns):
            outs[j][:, columns] = bfloat(product(x_ref[...], weight[j, :, columns]))
            if far is not None:
                far[:, columns] = bfloat(product(far_ref[...], weight[j, :, columns]))

        tiles(body, outs[j].shape[1], TILE)
    loader.finish()


def settle_kernel(n, height, wo_at, q_at, gain_rows, x_ref, mix_ref, gains_ref, *refs):
    pieces, refs = refs[:n], refs[n:]
    if q_at is None:
        n_ref, r_ref, full, weight, z_ref, *sems = refs
        low_ref = None
    else:
        n_ref, r_ref, q_ref, full, weight, z_ref, low_ref, *sems = refs
    loader = Loader(sems)
    loader.fetch(pieces, wo_at, height, weight.at[0])
    if q_at is not None:
        loader.fetch(pieces, q_at, height, weight.at[1])
    loader.arrived(0, weight.at[0], full.at[0])

    def project(columns):
        x = x_ref[:, columns].astype(jnp.float32)
        if gain_rows[0] is not None:
            x = x * gains_ref[pl.ds(gain_rows[0], 1), columns]
        z_ref[:, columns] = x + product(mix_ref[...], weight[0, :, columns])

    tiles(project, z_ref.shape[1], TILE)
    gain = gains_ref[pl.ds(gain_rows[1], 1), :]
    normalise(z_ref, n_ref, r_ref, gain, low_ref)
    if q_at is not None:
        loader.arrived(1, weight.at[1], full.at[1])

        def query(columns):
            q_ref[:, columns] = bfloat(product(low_ref[...], weight[1, :, columns]))

        tiles(query, q_ref.shape[1], TILE)
    loader.finish()


def tail_up_kernel(n, height, up_at, gain_row, n_ref, gains_ref, *refs):
    pieces = refs[:n]
    slope_hbm, inner_hbm, full, up, low_ref, slope_ref, inner_ref, out_sem, *sems = refs[n:]
    blocks = up.shape[0]
    loader = Loader(sems)
    for j in range(blocks):
        loader.fetch(pieces, up_at + j * height, height, up.at[j])
    gain = gains_ref[pl.ds(gain_row, 1), :]

    def lower(rows):
        low_ref[rows, :] = bfloat(n_ref[rows, :] * gain)

    tiles(lower, n_ref.shape[0], ROWS)
    width = up.shape[2]
    outs = []
    for j in range(blocks):
        loader.arrived(j, up.at[j], full.at[j])

        def upward(columns):
            inner, slope = gelu_both(product(low_ref[...], up[j, :, columns]))
            place = pl.ds(pl.multiple_of(j * width + columns.start, TILE), TILE)
            inner_ref[:, place] = bfloat(inner)
            slope_ref[:, place] = bfloat(slope)

        tiles(upward, width, TILE)
        columns = pl.ds(j * width, width)
        for i, (ref, hbm) in enumerate(((inner_ref, inner_hbm), (slope_ref, slope_hbm))):
            out = pltpu.make_async_copy(ref.at[:, columns], hbm.at[:, columns], out_sem.at[i, j])
            out.start()
            outs.append(out)
    loader.finish()
    for out in outs:
        out.wait()


def tail_down_kernel(n, height, offsets, gain_rows, n_ref, inner_ref, gains_ref, first_ref, second_ref, *refs):
    pieces, refs = refs[:n], refs[n:]
    pre_slope_ref, adapt_ref, n_out_ref, r_out_ref, out_ref, down_full, adapt_full = refs[:7]
    down, adapt, low_ref, z_ref, *sems = refs[7:]
    down_at, adapt_at = offsets
    width = z_ref.shape[1]
    loader = Loader(sems)
    loader.fetch(pieces, adapt_at, height, adapt)
    for at in range(0, width, TILE):
        loader.fetch(pieces, down_at, down.shape[0] // width * height, down, pl.ds(at, TILE))
    gain = gains_ref[pl.ds(gain_rows[0], 1), :]

    def lower(rows):
        low_ref[rows, :] = bfloat(n_ref[rows, :] * gain)

    tiles(lower, n_ref.shape[0], ROWS)
    loader.arrived(0, adapt, adapt_full)

    def adapting(columns):
        pre = product(low_ref[...], adapt[:, columns]) + first_ref[:, columns]
        adapted, slope = gelu_both(pre)
        adapt_ref[:, columns] = bfloat(adapted)
        pre_slope_ref[:, columns] = bfloat(slope)

    tiles(adapting, ADAPT, TILE)
    for i, at in enumerate(range(0, width, TILE)):
        columns = pl.ds(at, TILE)
        loader.arrived(1 + i, down.at[:, columns], down_full.at[:, columns])
        h = n_ref[:, columns] * gains_ref[pl.ds(gain_rows[0], 1), columns]
        ffn = product(inner_ref[...], down[:, columns])
        adapted = product_t(adapt_ref[...], adapt[columns, ADAPT:]) + second_ref[:, columns]
        z_ref[:, columns] = h + ffn + 4.0 * adapted
    normalise(z_ref, n_out_ref, r_out_ref, gains_ref[pl.ds(gain_rows[1], 1), :], out_ref)
    loader.finish()


def tail_back_kernel(height, gain_rows, more, *refs):
    (cot_ref, n2_ref, r2_ref, n1_ref, r1_ref, gains_ref, slope_hbm, pre_slope_ref, adapt_low_ref) = refs[:9]
    refs = refs[9:]
    (up_hbm, down_hbm, adapt_hbm, wo_hbm), refs = refs[:4], refs[4:]
    if more:
        far_ref, refs = refs[0], refs[1:]
    out_ref, dz_ref, dmix_ref, matrices_ref = refs[:4]
    up, down, adapt, wo, dt_ref, e_ref, low_ref, du_ref, dpre_ref, sem = refs[4:]
    blocks = up.shape[0]
    load(
        [adapt_hbm, down_hbm, slope_hbm, up_hbm, wo_hbm.at[0]],
        [adapt, down, du_ref, up, wo],
        sem,
    )
    gain1 = gains_ref[pl.ds(gain_rows[0], 1), :]
    gain2 = gains_ref[pl.ds(gain_rows[1], 1), :]

    def lower(rows):
        low_ref[rows, :] = bfloat(n1_ref[rows, :] * gain1)
        out_ref[rows, :] = bfloat(n2_ref[rows, :] * gain2)

    tiles(lower, n1_ref.shape[0], ROWS)

    def arriving(rows):
        grad = cot_ref[rows, :].astype(jnp.float32)
        return grad + far_ref[rows, :].astype(jnp.float32) if more else grad

    normalise_back(arriving, n2_ref, r2_ref, gain2, dt_ref, e_ref)
    loaded(adapt, sem.at[0])

    def adapting(columns):
        back = 4.0 * product(e_ref[...], adapt[:, pl.ds(ADAPT + columns.start, TILE)])
        dpre_ref[:, columns] = bfloat(back * pre_slope_ref[:, columns].astype(jnp.float32))

    tiles(adapting, ADAPT, TILE)
    first = jnp.sum(dpre_ref[...].astype(jnp.float32), axis=0, keepdims=True)
    second = 4.0 * jnp.sum(e_ref[...].astype(jnp.float32), axis=0, keepdims=True)
    row = lax.broadcasted_iota(jnp.int32, (BIAS_ROWS, ADAPT), 0)
    biases = jnp.where(row == 1, second[:, :ADAPT], jnp.where(row == 2, second[:, ADAPT:], 0.0))
    biases = bfloat(jnp.where(row == 0, first, biases))
    for block in range(matrices_ref.shape[0]):
        matrices_ref[block, 2 * height :, :] = biases

    wide = max(height, STAT)

    def matrices(columns):
        down_grad = bfloat(product_rows(low_ref[:, columns], dpre_ref[...]))
        up_grad = bfloat(4.0 * product_rows(e_ref[:, columns], adapt_low_ref[...]))
        for i in range(wide // height):
            block, rows = columns.start // height + i, slice(i * height, (i + 1) * height)
            matrices_ref[block, :height, :] = down_grad[rows, :]
            matrices_ref[block, height : 2 * height, :] = up_grad[rows, :]

    tiles(matrices, low_ref.shape[1], wide)
    loaded(down, sem.at[1])
    loaded(du_ref, sem.at[2])

    def inner(columns):
        back = product_t(e_ref[...], down[columns, :])
        du_ref[:, columns] = bfloat(back * du_ref[:, columns].astype(jnp.float32))

    tiles(inner, du_ref.shape[1], TILE)
    loaded(up, sem.at[3])
    width = up.shape[2]

    def hidden(columns):
        total = dt_ref[:, columns] + product_t(dpre_ref[...], adapt[columns, :ADAPT])
        for j in range(blocks):
            total += product_t(du_ref[:, j * width : (j + 1) * width], up[j, columns, :])
        dt_ref[:, columns] = total

    tiles(hidden, dt_ref.shape[1], TILE)
    normalise_back(lambda rows: dt_ref[rows, :], n1_ref, r1_ref, gain1, dz_ref, e_ref)
    loaded(wo, sem.at[4])

    def mixing(columns):
        dmix_ref[:, columns] = bfloat(product_t(e_ref[...], wo[columns, :]))

    tiles(mixing, dmix_ref.shape[1], TILE)


def query_back_kernel(gain_row, dz_ref, dq_ref, n_ref, r_ref, gains_ref, weights, *refs):
    dz_out_ref, dmix_ref, weight, dy_ref, e_ref, sem = refs
    load([weights.at[1], weights.at[0]], [weight.at[0], weight.at[1]], sem)
    loaded(weight.at[0], sem.at[0])

    def back(columns):
        dy_ref[:, columns] = dz_ref[:, columns] + product_t(dq_ref[...], weight[0, columns, :])

    tiles(back, dy_ref.shape[1], TILE)
    gain = gains_ref[pl.ds(gain_row, 1), :]
    normalise_back(lambda rows: dy_ref[rows, :], n_ref, r_ref, gain, dz_out_ref, e_ref)
    loaded(weight.at[1], sem.at[1])

    def mixing(columns):
        dmix_ref[:, columns] = bfloat(product_t(e_ref[...], weight[1, columns, :]))

    tiles(mixing, dmix_ref.shape[1], TILE)


def back_kernel(indices, bases, *refs):
    count = len(indices)
    base_refs, grads = refs[:bases], refs[bases : bases + count]
    weights, out_ref, weight, sem = refs[bases + count :]
    load([weights.at[i] for i in indices], [weight.at[j] for j in range(count)], sem)
    for j in range(count):
        loaded(weight.at[j], sem.at[j])

    def back(columns):
        total = None
        for base in base_refs:
            part = base[:, columns].astype(jnp.float32)
            total = part if total is None else total + part
        for j in range(count):
            part = product_t(grads[j][...], weight[j, columns, :])
            total = part if total is None else total + part
        out_ref[:, columns] = total.astype(out_ref.dtype)

    tiles(back, out_ref.shape[1], TILE)


def split(value):
    high = bfloat(value)
    return high, bfloat(value - high.astype(jnp.float32))


def put_left(ref, value):
    high, low = split(value)
    ref[:, :ADAPT] = high
    ref[:, ADAPT : 2 * ADAPT] = high
    ref[:, 2 * ADAPT :] = low


def put_right(ref, value):
    high, low = split(value)
    ref[:ADAPT, :] = high
    ref[ADAPT : 2 * ADAPT, :] = low
    ref[2 * ADAPT :, :] = high


def multiply(out_ref, left, right):
    def body(columns):
        out_ref[:, columns] = product(left[...], right[:, columns])

    tiles(body, ADAPT, TILE)


def muon_kernel(parts, *refs):
    rows_refs, (out_ref, high, low, gram, poly, left, right, rows_left) = refs[:parts], refs[parts:]
    rows = rows_refs[0].shape[0]
    for i, ref in enumerate(rows_refs):
        high[i * rows : (i + 1) * rows, :], low[i * rows : (i + 1) * rows, :] = split(ref[...])

    def square(columns):
        gram[:, columns] = (
            product_rows(high[...], high[:, columns])
            + product_rows(high[...], low[:, columns])
            + product_rows(low[...], high[:, columns])
        )

    tiles(square, ADAPT, TILE)
    eye = lax.broadcasted_iota(jnp.int32, (ADAPT, ADAPT), 0) == lax.broadcasted_iota(
        jnp.int32, (ADAPT, ADAPT), 1
    )
    scale = 1.0 / (jnp.sqrt(jnp.sum(jnp.where(eye, gram[...], 0.0), keepdims=True)) + 1e-07)
    gram[...] = gram[...] * (scale * scale)

    def polynomial():
        put_left(left, gram[...])
        put_right(right, gram[...])
        multiply(poly, left, right)
        poly[...] = (
            jnp.where(eye, NEWTON_LINEAR, 0.0) + NEWTON_QUADRATIC * gram[...] + NEWTON_CUBIC * poly[...]
        )
        put_right(right, poly[...])
        put_left(rows_left, out_ref[...])
        multiply(out_ref, rows_left, right)

    def advance():
        multiply(gram, left, right)
        put_left(left, gram[...])
        multiply(gram, left, right)

    out_ref[...] = rows_refs[0][...] * scale

    @pl.loop(0, NS_ITERS - 1)
    def _(i):
        polynomial()
        advance()

    polynomial()


HBM = pl.BlockSpec(memory_space=pltpu.HBM)
IN_VMEM = pl.BlockSpec(memory_space=pltpu.VMEM)
F32, BF16 = jnp.float32, jnp.bfloat16


def call(kernel, ins, specs, outs, scratch, flops, collective_id=None, after=()):
    if after:
        inner, first = kernel, len(ins)
        kernel = lambda *refs: inner(*refs[:first], *refs[first + len(after) :])
        ins, specs = [*ins, *after], [*specs, *[HBM] * len(after)]
    return pl.pallas_call(
        kernel,
        in_specs=specs,
        out_specs=[IN_VMEM if len(out) == 2 else HBM for out in outs],
        out_shape=[jax.ShapeDtypeStruct(*out[:2]) for out in outs],
        scratch_shapes=scratch,
        compiler_params=pltpu.CompilerParams(
            vmem_limit_bytes=VMEM_LIMIT,
            collective_id=collective_id,
            has_side_effects=collective_id is not None,
        ),
        cost_estimate=pl.CostEstimate(
            flops=flops, bytes_accessed=sum(a.size * a.dtype.itemsize for a in ins), transcendentals=0
        ),
    )(*ins)


def squares(count):
    return pltpu.VMEM((count, D, D), BF16)


def stored(*shape):
    return (shape, BF16, HBM)


def project(collective_id, x, far, pieces, offsets):
    rows = x.shape[0]
    count, n = len(offsets), len(pieces.arrays)
    return call(
        functools.partial(project_kernel, n, pieces.height, offsets),
        [x, far, *pieces.arrays],
        [IN_VMEM] * 2 + [HBM] * n,
        [((rows, D), BF16)] * (count + 2) + [stored(count, D, D)],
        [squares(count), *loader_sems(count, n)],
        2 * rows * D * D * (count + 2),
        collective_id,
    )


def settle(collective_id, x, mix, gains, pieces, wo_at, q_at, gain_rows, after=()):
    rows = x.shape[0]
    n = len(pieces.arrays)
    count = 1 if q_at is None else 2
    outs = [((rows, D), F32), ((rows, STAT), F32)]
    scratch = [squares(count), pltpu.VMEM((rows, D), F32)]
    if q_at is not None:
        outs.append(((rows, D), BF16))
        scratch.append(pltpu.VMEM((rows, D), BF16))
    return call(
        functools.partial(settle_kernel, n, pieces.height, wo_at, q_at, gain_rows),
        [x, mix, gains, *pieces.arrays],
        [IN_VMEM] * 3 + [HBM] * n,
        outs + [stored(count, D, D)],
        scratch + loader_sems(count, n),
        2 * rows * D * D * count,
        collective_id,
        after,
    )


def tail_up(collective_id, normed, gains, pieces, up_at, gain_row):
    rows = normed.shape[0]
    n = len(pieces.arrays)
    blocks = 4
    hidden = blocks * D
    return call(
        functools.partial(tail_up_kernel, n, pieces.height, up_at, gain_row),
        [normed, gains, *pieces.arrays],
        [IN_VMEM] * 2 + [HBM] * n,
        [stored(rows, hidden), stored(rows, hidden), stored(blocks, D, D)],
        [
            squares(blocks),
            pltpu.VMEM((rows, D), BF16),
            pltpu.VMEM((rows, hidden), BF16),
            pltpu.VMEM((rows, hidden), BF16),
            pltpu.SemaphoreType.DMA((2, blocks)),
            *loader_sems(blocks, n),
        ],
        8 * rows * D * D,
        collective_id,
    )


def tail_down(collective_id, normed, inner, gains, bias_first, bias_second, pieces, offsets, gain_rows):
    rows, hidden = inner.shape
    n = len(pieces.arrays)
    return call(
        functools.partial(tail_down_kernel, n, pieces.height, offsets, gain_rows),
        [normed, inner, gains, bias_first[None], bias_second[None], *pieces.arrays],
        [IN_VMEM] * 5 + [HBM] * n,
        [
            ((rows, ADAPT), BF16),
            ((rows, ADAPT), BF16),
            ((rows, D), F32),
            ((rows, STAT), F32),
            ((rows, D), BF16),
            stored(hidden, D),
            stored(D, D),
        ],
        [
            pltpu.VMEM((hidden, D), BF16),
            pltpu.VMEM((D, D), BF16),
            pltpu.VMEM((rows, D), BF16),
            pltpu.VMEM((rows, D), F32),
            *loader_sems(1 + D // TILE, n),
        ],
        10 * rows * D * D,
        collective_id,
    )


def tail_back(height, cot, second, first, gains, slope, pre_slope, adapt_low, weights, gain_rows, more=()):
    rows = cot.shape[0]
    hidden = slope.shape[1]
    return call(
        functools.partial(tail_back_kernel, height, gain_rows, bool(more)),
        [cot, *second, *first, gains, slope, pre_slope, adapt_low, *weights, *more],
        [IN_VMEM] * 6 + [HBM] + [IN_VMEM] * 2 + [HBM] * 4 + [IN_VMEM] * len(more),
        [
            ((rows, D), BF16),
            ((rows, D), F32),
            ((rows, D), BF16),
            ((D // height, 2 * height + BIAS_ROWS, ADAPT), BF16),
        ],
        [
            squares(hidden // D),
            pltpu.VMEM((hidden, D), BF16),
            pltpu.VMEM((D, D), BF16),
            pltpu.VMEM((D, D), BF16),
            pltpu.VMEM((rows, D), F32),
            pltpu.VMEM((rows, D), BF16),
            pltpu.VMEM((rows, D), BF16),
            pltpu.VMEM((rows, hidden), BF16),
            pltpu.VMEM((rows, ADAPT), BF16),
            pltpu.SemaphoreType.DMA((5,)),
        ],
        24 * rows * D * D,
    )


def query_back(dz, dq, first, gains, weights, gain_row):
    rows = dz.shape[0]
    return call(
        functools.partial(query_back_kernel, gain_row),
        [dz, dq, *first, gains, weights],
        [IN_VMEM] * 5 + [HBM],
        [((rows, D), F32), ((rows, D), BF16)],
        [
            squares(2),
            pltpu.VMEM((rows, D), F32),
            pltpu.VMEM((rows, D), BF16),
            pltpu.SemaphoreType.DMA((2,)),
        ],
        4 * rows * D * D,
    )


def back(bases, grads, weights, indices, dtype):
    rows = grads[0].shape[0]
    count = len(indices)
    return call(
        functools.partial(back_kernel, indices, len(bases)),
        [*bases, *grads, weights],
        [IN_VMEM] * (len(bases) + count) + [HBM],
        [((rows, D), dtype)],
        [squares(count), pltpu.SemaphoreType.DMA((count,))],
        2 * rows * D * D * count,
    )[0]


def muon(parts):
    rows = parts[0].shape[0]
    full = pltpu.VMEM((ADAPT, ADAPT), F32)
    return call(
        functools.partial(muon_kernel, len(parts)),
        parts,
        [IN_VMEM] * len(parts),
        [((rows, ADAPT), F32)],
        [
            pltpu.VMEM((rows * len(parts), ADAPT), BF16),
            pltpu.VMEM((rows * len(parts), ADAPT), BF16),
            full,
            full,
            pltpu.VMEM((ADAPT, 3 * ADAPT), BF16),
            pltpu.VMEM((3 * ADAPT, ADAPT), BF16),
            pltpu.VMEM((rows, 3 * ADAPT), BF16),
        ],
        20 * 6 * ADAPT**3,
    )[0]


def axis_bits(axis):
    return [1 << b for b in range(lax.axis_size(axis).bit_length() - 1)]


def tie(array, *others):
    return lax.optimization_barrier((array, *others))[0]


class Gather:
    def __init__(self, array, height):
        self.height = height
        self.array = array

    def begin(self, *after):
        array = tie(self.array, *after) if after else self.array
        steps = ((2, 4), (4, 2))
        self.arrays = [self.array] + [
            lax.ppermute(
                array, "wide", [(i, i ^ steps[i % 2][which]) for i in range(lax.axis_size("wide"))]
            )
            for which in range(2)
        ]
        return self

    def across(self, *after):
        first = tie(self.arrays[1], *after) if after else self.arrays[1]
        self.arrays.append(
            lax.ppermute(
                first, "wide", [(i, i ^ (2 if i % 2 else 4)) for i in range(lax.axis_size("wide"))]
            )
        )
        for bit in axis_bits("wide")[3:]:
            self.arrays += [swap(piece, "wide", bit) for piece in self.arrays]
        return self


def gather_any_order(array, axis):
    blocks = array[None]
    for bit in axis_bits(axis):
        blocks = jnp.concatenate([blocks, swap(blocks, axis, bit)])
    return blocks


def shards(
    enc_in,
    dec_in,
    segment_ids,
    enc_cot,
    dec_cot,
    enc_qkv,
    enc_wo,
    enc_w_in,
    enc_w_out,
    enc_gains,
    dec_qkv,
    dec_wo,
    dec_w_in,
    dec_w_out,
    dec_gains,
    adapter_weights,
    adapter_momenta,
    bias_in,
    bias_out,
):
    height = enc_wo.shape[0]
    stack = lambda *arrays: jnp.concatenate([a.reshape(-1, D) for a in arrays])
    columns = lambda array: [array[:, j * D : (j + 1) * D] for j in range(array.shape[1] // D)]
    gain_rows = jnp.concatenate([enc_gains, dec_gains])
    gain_block = jnp.pad(gain_rows, ((0, 16 - gain_rows.shape[0]), (0, D - height)))
    gather = lambda array: Gather(array, height)
    enc_first = gather(stack(enc_qkv, gain_block))
    dec_first = gather(stack(dec_qkv[:3]))
    enc_up = gather(stack(enc_wo, *columns(enc_w_in)))
    dec_second = gather(stack(dec_wo[0], dec_qkv[3]))
    dec_third = gather(stack(dec_qkv[4:], dec_wo[1]))
    dec_up = gather(stack(*columns(dec_w_in)))

    count = lax.axis_size("wide")
    partner = lambda array: swap(array, "narrow", 1)
    rows = enc_in.shape[0]
    half = (lax.axis_index("narrow") % 2).astype(jnp.int32).reshape(1)
    at = lambda i: i * height

    enc_first.begin()
    enc_far = partner(enc_in)
    enc_first.across()
    begun = enc_first.arrays[-1]
    dec_first.begin(begun)
    dec_far = partner(tie(dec_in, begun))
    other_ids = partner(tie(segment_ids, begun))
    places = (half, segment_ids.reshape(1, rows), segment_ids.reshape(rows, 1), other_ids.reshape(rows, 1))
    found = gather_any_order(bfloat(tie(adapter_weights, begun)), "narrow")
    found = found[lax.axis_index("narrow") ^ jnp.arange(lax.axis_size("narrow"))]
    adapters = found.transpose(1, 0, 2, 3).reshape(4, height, ADAPT)
    beside = lambda l: jnp.concatenate([adapters[2 * l], adapters[2 * l + 1]], axis=1)
    enc_query, enc_key, enc_value, enc_key_far, enc_value_far, enc_qkv_full = project(
        0, tie(enc_in, begun), enc_far, enc_first, (at(0), at(1), at(2))
    )
    enc_keys, enc_values = (enc_key, enc_key_far), (enc_value, enc_value_far)

    repeat = lax.axis_size("narrow") // 4
    spread = lambda array: jnp.repeat(array, repeat, axis=0) if repeat > 1 else array
    exchange = lambda array, axis: lax.all_to_all(array, axis, split_axis=0, concat_axis=0, tiled=True)
    to_matrix = lambda array: exchange(spread(array), "narrow").reshape(-1, ADAPT)
    to_rows = lambda array: exchange(
        array.reshape(lax.axis_size("narrow"), -1, ADAPT), "narrow"
    )[::repeat]

    dec_first.across(enc_value)
    enc_up.begin(enc_value)
    enc_mix, enc_lse = attend(places, enc_query, enc_keys, enc_values, False)
    found = jnp.stack([p[at(3) : at(3) + 8, :height] for p in enc_first.arrays])
    found = jnp.concatenate([found, swap(tie(found, enc_mix), "wide", 1)])
    me = lax.axis_index("wide")
    apart = me ^ jnp.arange(count)
    odd = ((me ^ apart) & 1) == 1
    low = apart & 6
    piece = jnp.where(low == 0, 0, jnp.where(low == 6, 3, jnp.where((low == 2) ^ odd, 1, 2)))
    order = (apart & 1) * (count // 2) + (apart >> 3) * 4 + piece
    gains = found[order].transpose(1, 0, 2).reshape(8, D).astype(jnp.float32)
    enc_down = gather(stack(enc_w_out, tie(beside(0), enc_mix)))
    dec_down = gather(stack(dec_w_out, tie(beside(1), enc_mix)))
    enc_down.begin(enc_mix)
    self_query, self_key, self_value, self_key_far, self_value_far, dec_qkv_full = project(
        1, tie(dec_in, enc_mix), dec_far, dec_first, (at(0), at(1), at(2))
    )
    self_keys, self_values = (self_key, self_key_far), (self_value, self_value_far)
    enc_up.across(self_value)
    self_mix, self_lse = attend(places, self_query, self_keys, self_values, True)
    dec_second.begin(self_mix)
    *enc_norm1, enc_wo_full = settle(
        2, enc_in, tie(enc_mix, self_mix), gains, enc_up, at(0), None, (None, 0)
    )
    enc_down.across(enc_norm1[0])
    enc_slope, enc_inner, enc_up_full = tail_up(3, enc_norm1[0], gains, enc_up, at(1), 0)
    dec_second.across(enc_inner)
    dec_third.begin(enc_inner)
    enc_pre_slope, enc_adapt, *enc_norm2, enc_low, enc_down_full, enc_adapt_full = tail_down(
        4, enc_norm1[0], enc_inner, gains, bias_in[0], bias_out[0], enc_down, (0, at(4)), (0, 1)
    )
    enc_low_far = partner(enc_low)
    dec_third.across(enc_low)
    *dec_norm1, cross_query, dec_q_full = settle(
        5, dec_in, tie(self_mix, enc_low), gains, dec_second, at(0), at(1), (None, 2)
    )
    dec_up.begin(cross_query)
    dec_down.begin(cross_query)
    cross_key, cross_value, cross_key_far, cross_value_far, dec_kv_full = project(
        6, tie(enc_low, cross_query), enc_low_far, dec_third, (at(0), at(1))
    )
    cross_keys, cross_values = (cross_key, cross_key_far), (cross_value, cross_value_far)
    dec_up.across(cross_key)
    cross_mix, cross_lse = attend(places, cross_query, cross_keys, cross_values, False)
    *dec_norm2, dec_wo_full = settle(
        7, dec_norm1[0], cross_mix, gains, dec_third, at(2), None, (2, 3)
    )
    dec_down.across(dec_norm2[0])
    dec_slope, dec_inner, dec_up_full = tail_up(8, dec_norm2[0], gains, dec_up, at(0), 3)
    dec_pre_slope, dec_adapt, *dec_norm3, _, dec_down_full, dec_adapt_full = tail_down(
        9, dec_norm2[0], dec_inner, gains, bias_in[1], bias_out[1], dec_down, (0, at(4)), (3, 4)
    )

    dec_out, grad_z2, grad_cross_mix, dec_matrices = tail_back(
        height,
        dec_cot,
        dec_norm3,
        dec_norm2,
        gains,
        dec_slope,
        dec_pre_slope,
        dec_adapt,
        (dec_up_full, dec_down_full, dec_adapt_full, dec_wo_full),
        (3, 4),
    )
    total = lambda array: jnp.sum(array.astype(jnp.float32), axis=0)
    dec_matrices = exchange(dec_matrices, "wide")
    cross_back = attend_back(
        places, grad_cross_mix, cross_query, cross_keys, cross_values, cross_mix, cross_lse, False
    )
    dec_sums = total(tie(dec_matrices, cross_back[0]))
    far_encoded = back((), (tie(cross_back[2], dec_sums), cross_back[4]), dec_kv_full, (0, 1), BF16)
    near_encoded = partner(far_encoded)
    grad_encoded = back(
        (tie(enc_cot, far_encoded),), (cross_back[1], cross_back[3]), dec_kv_full, (0, 1), F32
    )
    grad_z1, grad_self_mix = query_back(
        tie(grad_z2, grad_encoded),
        cross_back[0],
        dec_norm1,
        gains,
        dec_q_full,
        2,
    )
    enc_out, grad_ez1, grad_enc_mix, enc_matrices = tail_back(
        height,
        tie(grad_encoded, grad_z1),
        enc_norm2,
        enc_norm1,
        gains,
        enc_slope,
        enc_pre_slope,
        enc_adapt,
        (enc_up_full, enc_down_full, enc_adapt_full, enc_wo_full),
        (0, 1),
        (near_encoded,),
    )
    old_momentum = to_matrix(tie(adapter_momenta, grad_z1))
    enc_matrices = exchange(tie(enc_matrices, old_momentum), "wide")

    self_back = attend_back(
        places, tie(grad_self_mix, grad_ez1), self_query, self_keys, self_values, self_mix, self_lse, True, (old_momentum,)
    )

    enc_sums = total(tie(enc_matrices, self_back[0]))
    sums = [array[at(i) : at(i + 1)] for array in (enc_sums, dec_sums) for i in range(2)]
    biases = jnp.concatenate([array[at(2) : at(2) + BIAS_ROWS // 2] for array in (enc_sums, dec_sums)])
    sums = jnp.stack([jnp.concatenate([array, biases]) for array in sums])
    sums = spread(bfloat(sums))
    enc_back = attend_back(
        places, tie(grad_enc_mix, sums), enc_query, enc_keys, enc_values, enc_mix, enc_lse, False
    )
    summed = exchange(sums, "narrow")
    summed = total(tie(summed, enc_back[0]))
    momentum = DECAY * old_momentum + summed[:height]
    layers = summed[height:].reshape(2, -1, ADAPT)
    place = lax.axis_index("wide") * lax.axis_size("narrow") + lax.axis_index("narrow")
    devices = lax.axis_size("wide") * lax.axis_size("narrow")
    own_part = lambda array: lax.dynamic_slice_in_dim(
        array, place * (array.shape[1] // devices), array.shape[1] // devices, 1
    )
    grad_bias_in, grad_bias_out = own_part(layers[:, 0]), own_part(layers[:, 1:3].reshape(2, D))
    parts = [momentum] + [swap(momentum, "wide", r) for r in range(1, lax.axis_size("wide"))]
    new_momenta = to_rows(momentum)

    far_dec = back(
        (), (tie(self_back[2], momentum), self_back[4]), dec_qkv_full, (1, 2), BF16
    )
    near_dec = partner(far_dec)
    far_enc = back((), (tie(enc_back[2], far_dec), enc_back[4]), enc_qkv_full, (1, 2), BF16)
    near_enc = partner(far_enc)
    grad_dec = back(
        (tie(grad_z1, far_enc), near_dec),
        (self_back[0], self_back[1], self_back[3]),
        dec_qkv_full,
        (0, 1, 2),
        F32,
    )
    orthogonal = muon([parts[0], tie(parts[1], grad_dec), *parts[2:]])
    grad_enc = back(
        (tie(grad_ez1, orthogonal), near_enc),
        (enc_back[0], enc_back[1], enc_back[3]),
        enc_qkv_full,
        (0, 1, 2),
        F32,
    )
    new_weights = adapter_weights - RATE * math.sqrt(max(1.0, D / ADAPT)) * to_rows(orthogonal)
    return (
        enc_out,
        dec_out,
        grad_enc,
        grad_dec,
        grad_bias_in,
        grad_bias_out,
        new_momenta,
        new_weights,
    )


def solution(mesh):
    both = ("wide", "narrow")
    tokens = P(both, None)
    rows_first, rows_second = P("wide", None), P(None, "wide", None)
    adapters = P(None, both, None)
    in_specs = (
        tokens,
        tokens,
        P(both),
        tokens,
        tokens,
        rows_second,
        rows_first,
        rows_first,
        rows_first,
        P(None, "wide"),
        rows_second,
        rows_second,
        rows_first,
        rows_first,
        P(None, "wide"),
        adapters,
        adapters,
        P(),
        P(),
    )
    out_specs = (
        tokens,
        tokens,
        tokens,
        tokens,
        P(None, both),
        P(None, both),
        adapters,
        adapters,
    )
    return jax.shard_map(shards, mesh=mesh, in_specs=in_specs, out_specs=out_specs, check_vma=False)
```

```python
import functools
import math

import jax
import jax.numpy as jnp
from jax import lax
from jax.experimental import pallas as pl
from jax.experimental.pallas import tpu as pltpu
from jax.sharding import PartitionSpec as P

D = 1024
HD = 64
ADAPT = 512
NS_ITERS = 5

EPSILON = 1e-05
MASKED = -1e30
NEWTON_LINEAR = 3.4445
NEWTON_QUADRATIC = -4.775
NEWTON_CUBIC = 2.0315
RATE = 0.7
DECAY = 0.5
LOG2E = 1.4426950408889634
PAIR = 2 * HD
VMEM_LIMIT = 58 * 1024 * 1024
MESH = pl.DeviceIdType.MESH


def swap(array, axis, bit):
    return lax.ppermute(array, axis, [(i, i ^ bit) for i in range(lax.axis_size(axis))])


def bfloat(tensor):
    return tensor.astype(jnp.bfloat16)


def product(left_side, right_side):
    return jnp.dot(left_side, right_side, preferred_element_type=jnp.float32)


def contract(left_side, right_side, left_dim, right_dim):
    return lax.dot_general(
        left_side,
        right_side,
        (((left_dim,), (right_dim,)), ((), ())),
        preferred_element_type=jnp.float32,
    )


def product_t(left_side, right_side):
    return contract(left_side, right_side, 1, 1)


def product_rows(left_side, right_side):
    return contract(left_side, right_side, 0, 0)


def gelu_both(tensor):
    phi = 0.5 * (1.0 + lax.erf(tensor * 0.7071067811865476))
    slope = phi + tensor * jnp.exp(-0.5 * tensor * tensor) * 0.3989422804014327
    return tensor * phi, slope


def fill_bias(half_ref, qid_ref, kid_own_ref, kid_far_ref, bias_ref, causal):
    rows = qid_ref.shape[1]
    qid = qid_ref[...]
    for part, kid_ref in enumerate((kid_own_ref, kid_far_ref)):
        allowed = kid_ref[...] == qid
        if causal:
            if part == 0:
                key_at = lax.broadcasted_iota(jnp.int32, (rows, rows), 0)
                query_at = lax.broadcasted_iota(jnp.int32, (rows, rows), 1)
                allowed = allowed & (key_at <= query_at)
            else:
                allowed = allowed & (half_ref[0] == 1)
        bias_ref[pl.ds(part * rows, rows), :] = jnp.where(allowed, 0.0, MASKED)


def head_mask(rows, head):
    return lax.broadcasted_iota(jnp.int32, (rows, PAIR), 1) // HD == head


def attend_kernel(
    causal,
    chunk,
    half_ref,
    qid_ref,
    kid_own_ref,
    kid_far_ref,
    q_ref,
    k_own_ref,
    k_far_ref,
    v_own_ref,
    v_far_ref,
    out_ref,
    lse_ref,
    bias_ref,
    score_ref,
):
    rows = q_ref.shape[0]

    @pl.when(pl.program_id(0) == 0)
    def _():
        fill_bias(half_ref, qid_ref, kid_own_ref, kid_far_ref, bias_ref, causal)

    queries = q_ref[...] * 0.125
    steps = [
        (part, at)
        for part in range(2)
        for at in range(0, rows, chunk)
    ]
    keys = (k_own_ref, k_far_ref)
    values = (v_own_ref, v_far_ref)
    mixes = []
    for head in range(2):
        q_head = jnp.where(head_mask(rows, head), queries, jnp.zeros_like(queries))
        peak = None
        for part, at in steps:
            place = pl.ds(part * rows + at, chunk)
            scores = product_t(keys[part][pl.ds(at, chunk), :], q_head)
            scores = scores * LOG2E + bias_ref[place, :]
            score_ref[head, place, :] = scores
            top = jnp.max(scores, axis=0, keepdims=True)
            peak = top if peak is None else jnp.maximum(peak, top)
        total, mix = None, None
        for part, at in steps:
            place = pl.ds(part * rows + at, chunk)
            raised = jnp.exp2(score_ref[head, place, :] - peak)
            share = jnp.sum(raised, axis=0, keepdims=True)
            piece = product_rows(values[part][pl.ds(at, chunk), :], bfloat(raised))
            total = share if total is None else total + share
            mix = piece if mix is None else mix + piece
        mixes.append((mix * (1.0 / total))[head * HD : (head + 1) * HD, :])
        lse_ref[0, pl.ds(head, 1), :] = peak + jnp.log2(total)
    out_ref[...] = bfloat(jnp.concatenate(mixes, axis=0).T)


def attend_back_kernel(
    causal,
    chunk,
    half_ref,
    qid_ref,
    kid_own_ref,
    kid_far_ref,
    q_ref,
    k_own_ref,
    k_far_ref,
    v_own_ref,
    v_far_ref,
    out_ref,
    grad_ref,
    lse_ref,
    dq_ref,
    dk_own_ref,
    dk_far_ref,
    dv_own_ref,
    dv_far_ref,
    bias_ref,
):
    rows = q_ref.shape[0]

    @pl.when(pl.program_id(0) == 0)
    def _():
        fill_bias(half_ref, qid_ref, kid_own_ref, kid_far_ref, bias_ref, causal)

    queries = q_ref[...] * 0.125
    grads = grad_ref[...]
    products = (grads.astype(jnp.float32) * out_ref[...].astype(jnp.float32)).T
    q_heads, g_heads, deltas, lses = [], [], [], []
    for head in range(2):
        chosen = head_mask(rows, head)
        q_heads.append(jnp.where(chosen, queries, jnp.zeros_like(queries)))
        g_heads.append(jnp.where(chosen, grads, jnp.zeros_like(grads)))
        deltas.append(jnp.sum(products[head * HD : (head + 1) * HD, :], axis=0, keepdims=True))
        lses.append(lse_ref[0, pl.ds(head, 1), :])
    grad_q = [None, None]
    for part in range(2):
        key_ref = (k_own_ref, k_far_ref)[part]
        value_ref = (v_own_ref, v_far_ref)[part]
        dk_ref = (dk_own_ref, dk_far_ref)[part]
        dv_ref = (dv_own_ref, dv_far_ref)[part]
        for at in range(0, rows, chunk):
            here = pl.ds(at, chunk)
            keys, values = key_ref[here, :], value_ref[here, :]
            grad_k, grad_v = None, None
            for head in range(2):
                scores = product_t(keys, q_heads[head])
                bias = bias_ref[pl.ds(part * rows + at, chunk), :]
                weights = jnp.exp2(scores * LOG2E + (bias - lses[head]))
                grad_w = product_t(values, g_heads[head])
                grad_s = bfloat(weights * (grad_w - deltas[head]))
                piece_v = product(bfloat(weights), g_heads[head])
                piece_k = product(grad_s, q_heads[head])
                piece_q = product_rows(keys, grad_s)
                grad_v = piece_v if grad_v is None else grad_v + piece_v
                grad_k = piece_k if grad_k is None else grad_k + piece_k
                grad_q[head] = piece_q if grad_q[head] is None else grad_q[head] + piece_q
            dk_ref[here, :] = grad_k.astype(dk_ref.dtype)
            dv_ref[here, :] = grad_v.astype(dv_ref.dtype)
    joined = jnp.concatenate([grad_q[h][h * HD : (h + 1) * HD, :] for h in range(2)], axis=0)
    dq_ref[...] = bfloat((joined * 0.125).T)


def attention_specs(rows):
    whole = lambda shape: pl.BlockSpec(shape, lambda i: (0,) * len(shape))
    columns = pl.BlockSpec((rows, PAIR), lambda i: (0, i))
    fixed = [
        pl.BlockSpec(memory_space=pltpu.SMEM),
        whole((1, rows)),
        whole((rows, 1)),
        whole((rows, 1)),
    ]
    return fixed, columns, pl.BlockSpec((1, 8, rows), lambda i: (i, 0, 0))


def attend(places, queries, keys, values, causal):
    rows, width = queries.shape
    pairs = width // PAIR
    fixed, columns, stat = attention_specs(rows)
    return pl.pallas_call(
        functools.partial(attend_kernel, causal, 256),
        grid=(pairs,),
        in_specs=fixed + [columns] * 5,
        out_specs=[columns, stat],
        out_shape=[
            jax.ShapeDtypeStruct((rows, width), jnp.bfloat16),
            jax.ShapeDtypeStruct((pairs, 8, rows), jnp.float32),
        ],
        scratch_shapes=[
            pltpu.VMEM((2 * rows, rows), jnp.float32),
            pltpu.VMEM((2, 2 * rows, rows), jnp.float32),
        ],
        compiler_params=pltpu.CompilerParams(vmem_limit_bytes=VMEM_LIMIT),
        cost_estimate=pl.CostEstimate(
            flops=32 * rows * rows * width, bytes_accessed=12 * rows * width, transcendentals=0
        ),
    )(*places, queries, *keys, *values)


def attend_back(places, grad_out, queries, keys, values, mix, lse, causal, after=()):
    rows, width = queries.shape
    pairs = width // PAIR
    fixed, columns, stat = attention_specs(rows)
    return pl.pallas_call(
        lambda *refs: attend_back_kernel(causal, 256, *refs[:12], *refs[12 + len(after) :]),
        grid=(pairs,),
        in_specs=fixed + [columns] * 7 + [stat] + [HBM] * len(after),
        out_specs=[columns] * 5,
        out_shape=[
            jax.ShapeDtypeStruct((rows, width), jnp.bfloat16),
        ]
        * 5,
        scratch_shapes=[pltpu.VMEM((2 * rows, rows), jnp.float32)],
        compiler_params=pltpu.CompilerParams(vmem_limit_bytes=VMEM_LIMIT),
        cost_estimate=pl.CostEstimate(
            flops=80 * rows * rows * width, bytes_accessed=24 * rows * width, transcendentals=0
        ),
    )(*places, queries, *keys, *values, mix, grad_out, lse, *after)


def flipped(me, bits):
    place = me
    bit = 1
    while bit <= bits:
        if bits & bit:
            place = place + bit * (1 - 2 * lax.rem(lax.div(me, bit), 2))
        bit *= 2
    return place


def place_of(me, piece):
    odd = lax.rem(me, 2)
    place = me
    if piece % 4 in (1, 2):
        first, second = (2, 4) if piece % 4 == 1 else (4, 2)
        place = flipped(me, first) * (1 - odd) + flipped(me, second) * odd
    elif piece % 4 == 3:
        place = flipped(me, 6)
    return place + (flipped(me, 2 * (piece - piece % 4)) - me)


class Loader:
    def __init__(self, sems):
        self.local, self.send, self.recv, self.stored = sems
        self.copies, self.stores = [], []
        self.me = lax.axis_index("wide")
        self.sibling = {"wide": flipped(self.me, 1)}
        barrier = pltpu.get_barrier_semaphore()
        pl.semaphore_signal(barrier, inc=1, device_id=self.sibling, device_id_type=MESH)
        pl.semaphore_wait(barrier, 1)

    def fetch(self, pieces, offset, height, target, columns=slice(None)):
        block = len(self.copies)
        copies = []
        for i, piece in enumerate(pieces):
            at = pl.multiple_of(place_of(self.me, i) * height, height)
            source = piece.at[pl.ds(offset, height), columns]
            place = target.at[pl.ds(at, height), columns]
            near = pltpu.make_async_copy(source, place, self.local.at[block, i])
            far = pltpu.make_async_remote_copy(
                source,
                place,
                self.send.at[block, i],
                self.recv.at[block, i],
                device_id=self.sibling,
                device_id_type=MESH,
            )
            near.start()
            far.start()
            copies.append((near, far))
        self.copies.append(copies)
        return block

    def arrived(self, block, target, out):
        for near, far in self.copies[block]:
            near.wait()
            far.wait_recv()
        store = pltpu.make_async_copy(target, out, self.stored.at[block])
        store.start()
        self.stores.append(store)

    def finish(self):
        for copies in self.copies:
            for _, far in copies:
                far.wait_send()
        for store in self.stores:
            store.wait()


def loader_sems(blocks, pieces):
    dma = pltpu.SemaphoreType.DMA
    return [dma((blocks, pieces))] * 3 + [dma((blocks,))]


def load(weights, targets, sem):
    for j, (weight, target) in enumerate(zip(weights, targets)):
        pltpu.make_async_copy(weight, target, sem.at[j]).start()


def loaded(target, sem):
    pltpu.make_async_copy(target, target, sem).wait()


def tiles(body, width, step):
    @pl.loop(0, width // step)
    def _(i):
        body(pl.ds(pl.multiple_of(i * step, step), step))


ROWS = 256
TILE = 512
STAT = 128
BIAS_ROWS = 16


def normalise(z_ref, n_ref, r_ref, gain, low_ref):
    def body(rows):
        z = z_ref[rows, :]
        centred = z - jnp.mean(z, axis=-1, keepdims=True)
        inverse = lax.rsqrt(jnp.mean(centred * centred, axis=-1, keepdims=True) + EPSILON)
        normed = centred * inverse
        n_ref[rows, :] = normed
        r_ref[rows, :] = jnp.broadcast_to(inverse, (ROWS, STAT))
        if low_ref is not None:
            low_ref[rows, :] = bfloat(normed * gain)

    tiles(body, z_ref.shape[0], ROWS)


def normalise_back(read_grad, n_ref, r_ref, gain, dz_ref, low_ref):
    def body(rows):
        scaled = read_grad(rows) * gain
        normed = n_ref[rows, :]
        dz = r_ref[rows, :][:, :1] * (
            scaled
            - jnp.mean(scaled, axis=-1, keepdims=True)
            - normed * jnp.mean(scaled * normed, axis=-1, keepdims=True)
        )
        dz_ref[rows, :] = dz
        low_ref[rows, :] = bfloat(dz)

    tiles(body, n_ref.shape[0], ROWS)


def project_kernel(n, height, offsets, x_ref, far_ref, *refs):
    count = len(offsets)
    pieces, outs, full, (weight, *sems) = refs[:n], refs[n:-6], refs[-6], refs[-5:]
    loader = Loader(sems)
    for j, offset in enumerate(offsets):
        loader.fetch(pieces, offset, height, weight.at[j])
    for j in range(count):
        loader.arrived(j, weight.at[j], full.at[j])
        far = outs[count + j - (count - 2)] if j >= count - 2 else None

        def body(columns):
            outs[j][:, columns] = bfloat(product(x_ref[...], weight[j, :, columns]))
            if far is not None:
                far[:, columns] = bfloat(product(far_ref[...], weight[j, :, columns]))

        tiles(body, outs[j].shape[1], TILE)
    loader.finish()


def settle_kernel(n, height, wo_at, q_at, gain_rows, x_ref, mix_ref, gains_ref, *refs):
    pieces, refs = refs[:n], refs[n:]
    if q_at is None:
        n_ref, r_ref, full, weight, z_ref, *sems = refs
        low_ref = None
    else:
        n_ref, r_ref, q_ref, full, weight, z_ref, low_ref, *sems = refs
    loader = Loader(sems)
    loader.fetch(pieces, wo_at, height, weight.at[0])
    if q_at is not None:
        loader.fetch(pieces, q_at, height, weight.at[1])
    loader.arrived(0, weight.at[0], full.at[0])

    def project(columns):
        x = x_ref[:, columns].astype(jnp.float32)
        if gain_rows[0] is not None:
            x = x * gains_ref[pl.ds(gain_rows[0], 1), columns]
        z_ref[:, columns] = x + product(mix_ref[...], weight[0, :, columns])

    tiles(project, z_ref.shape[1], TILE)
    gain = gains_ref[pl.ds(gain_rows[1], 1), :]
    normalise(z_ref, n_ref, r_ref, gain, low_ref)
    if q_at is not None:
        loader.arrived(1, weight.at[1], full.at[1])

        def query(columns):
            q_ref[:, columns] = bfloat(product(low_ref[...], weight[1, :, columns]))

        tiles(query, q_ref.shape[1], TILE)
    loader.finish()


def tail_up_kernel(n, height, up_at, gain_row, n_ref, gains_ref, *refs):
    pieces = refs[:n]
    slope_hbm, inner_hbm, full, up, low_ref, slope_ref, inner_ref, out_sem, *sems = refs[n:]
    blocks = up.shape[0]
    loader = Loader(sems)
    for j in range(blocks):
        loader.fetch(pieces, up_at + j * height, height, up.at[j])
    gain = gains_ref[pl.ds(gain_row, 1), :]

    def lower(rows):
        low_ref[rows, :] = bfloat(n_ref[rows, :] * gain)

    tiles(lower, n_ref.shape[0], ROWS)
    width = up.shape[2]
    outs = []
    for j in range(blocks):
        loader.arrived(j, up.at[j], full.at[j])

        def upward(columns):
            inner, slope = gelu_both(product(low_ref[...], up[j, :, columns]))
            place = pl.ds(pl.multiple_of(j * width + columns.start, TILE), TILE)
            inner_ref[:, place] = bfloat(inner)
            slope_ref[:, place] = bfloat(slope)

        tiles(upward, width, TILE)
        columns = pl.ds(j * width, width)
        for i, (ref, hbm) in enumerate(((inner_ref, inner_hbm), (slope_ref, slope_hbm))):
            out = pltpu.make_async_copy(ref.at[:, columns], hbm.at[:, columns], out_sem.at[i, j])
            out.start()
            outs.append(out)
    loader.finish()
    for out in outs:
        out.wait()


def tail_down_kernel(n, height, offsets, gain_rows, n_ref, inner_ref, gains_ref, first_ref, second_ref, *refs):
    pieces, refs = refs[:n], refs[n:]
    pre_slope_ref, adapt_ref, n_out_ref, r_out_ref, out_ref, down_full, adapt_full = refs[:7]
    down, adapt, low_ref, z_ref, *sems = refs[7:]
    down_at, adapt_at = offsets
    width = z_ref.shape[1]
    loader = Loader(sems)
    loader.fetch(pieces, adapt_at, height, adapt)
    for at in range(0, width, TILE):
        loader.fetch(pieces, down_at, down.shape[0] // width * height, down, pl.ds(at, TILE))
    gain = gains_ref[pl.ds(gain_rows[0], 1), :]

    def lower(rows):
        low_ref[rows, :] = bfloat(n_ref[rows, :] * gain)

    tiles(lower, n_ref.shape[0], ROWS)
    loader.arrived(0, adapt, adapt_full)

    def adapting(columns):
        pre = product(low_ref[...], adapt[:, columns]) + first_ref[:, columns]
        adapted, slope = gelu_both(pre)
        adapt_ref[:, columns] = bfloat(adapted)
        pre_slope_ref[:, columns] = bfloat(slope)

    tiles(adapting, ADAPT, TILE)
    for i, at in enumerate(range(0, width, TILE)):
        columns = pl.ds(at, TILE)
        loader.arrived(1 + i, down.at[:, columns], down_full.at[:, columns])
        h = n_ref[:, columns] * gains_ref[pl.ds(gain_rows[0], 1), columns]
        ffn = product(inner_ref[...], down[:, columns])
        adapted = product_t(adapt_ref[...], adapt[columns, ADAPT:]) + second_ref[:, columns]
        z_ref[:, columns] = h + ffn + 4.0 * adapted
    normalise(z_ref, n_out_ref, r_out_ref, gains_ref[pl.ds(gain_rows[1], 1), :], out_ref)
    loader.finish()


def tail_back_kernel(height, gain_rows, more, *refs):
    (cot_ref, n2_ref, r2_ref, n1_ref, r1_ref, gains_ref, slope_hbm, pre_slope_ref, adapt_low_ref) = refs[:9]
    refs = refs[9:]
    (up_hbm, down_hbm, adapt_hbm, wo_hbm), refs = refs[:4], refs[4:]
    if more:
        far_ref, refs = refs[0], refs[1:]
    out_ref, dz_ref, dmix_ref, matrices_ref = refs[:4]
    up, down, adapt, wo, dt_ref, e_ref, low_ref, du_ref, dpre_ref, sem = refs[4:]
    blocks = up.shape[0]
    load(
        [adapt_hbm, down_hbm, slope_hbm, up_hbm, wo_hbm.at[0]],
        [adapt, down, du_ref, up, wo],
        sem,
    )
    gain1 = gains_ref[pl.ds(gain_rows[0], 1), :]
    gain2 = gains_ref[pl.ds(gain_rows[1], 1), :]

    def lower(rows):
        low_ref[rows, :] = bfloat(n1_ref[rows, :] * gain1)
        out_ref[rows, :] = bfloat(n2_ref[rows, :] * gain2)

    tiles(lower, n1_ref.shape[0], ROWS)

    def arriving(rows):
        grad = cot_ref[rows, :].astype(jnp.float32)
        return grad + far_ref[rows, :].astype(jnp.float32) if more else grad

    normalise_back(arriving, n2_ref, r2_ref, gain2, dt_ref, e_ref)
    loaded(adapt, sem.at[0])

    def adapting(columns):
        back = 4.0 * product(e_ref[...], adapt[:, pl.ds(ADAPT + columns.start, TILE)])
        dpre_ref[:, columns] = bfloat(back * pre_slope_ref[:, columns].astype(jnp.float32))

    tiles(adapting, ADAPT, TILE)
    first = jnp.sum(dpre_ref[...].astype(jnp.float32), axis=0, keepdims=True)
    second = 4.0 * jnp.sum(e_ref[...].astype(jnp.float32), axis=0, keepdims=True)
    row = lax.broadcasted_iota(jnp.int32, (BIAS_ROWS, ADAPT), 0)
    biases = jnp.where(row == 1, second[:, :ADAPT], jnp.where(row == 2, second[:, ADAPT:], 0.0))
    biases = bfloat(jnp.where(row == 0, first, biases))
    for block in range(matrices_ref.shape[0]):
        matrices_ref[block, 2 * height :, :] = biases

    wide = max(height, TILE)

    def matrices(columns):
        down_grad = bfloat(product_rows(low_ref[:, columns], dpre_ref[...]))
        up_grad = bfloat(4.0 * product_rows(e_ref[:, columns], adapt_low_ref[...]))
        for i in range(wide // height):
            block, rows = columns.start // height + i, slice(i * height, (i + 1) * height)
            matrices_ref[block, :height, :] = down_grad[rows, :]
            matrices_ref[block, height : 2 * height, :] = up_grad[rows, :]

    tiles(matrices, low_ref.shape[1], wide)
    loaded(down, sem.at[1])
    loaded(du_ref, sem.at[2])

    def inner(columns):
        back = product_t(e_ref[...], down[columns, :])
        du_ref[:, columns] = bfloat(back * du_ref[:, columns].astype(jnp.float32))

    tiles(inner, du_ref.shape[1], TILE)
    loaded(up, sem.at[3])
    width = up.shape[2]

    def hidden(columns):
        total = dt_ref[:, columns] + product_t(dpre_ref[...], adapt[columns, :ADAPT])
        for j in range(blocks):
            total += product_t(du_ref[:, j * width : (j + 1) * width], up[j, columns, :])
        dt_ref[:, columns] = total

    tiles(hidden, dt_ref.shape[1], TILE)
    normalise_back(lambda rows: dt_ref[rows, :], n1_ref, r1_ref, gain1, dz_ref, e_ref)
    loaded(wo, sem.at[4])

    def mixing(columns):
        dmix_ref[:, columns] = bfloat(product_t(e_ref[...], wo[columns, :]))

    tiles(mixing, dmix_ref.shape[1], TILE)


def query_back_kernel(gain_row, dz_ref, dq_ref, n_ref, r_ref, gains_ref, weights, *refs):
    dz_out_ref, dmix_ref, weight, dy_ref, e_ref, sem = refs
    load([weights.at[1], weights.at[0]], [weight.at[0], weight.at[1]], sem)
    loaded(weight.at[0], sem.at[0])

    def back(columns):
        dy_ref[:, columns] = dz_ref[:, columns] + product_t(dq_ref[...], weight[0, columns, :])

    tiles(back, dy_ref.shape[1], TILE)
    gain = gains_ref[pl.ds(gain_row, 1), :]
    normalise_back(lambda rows: dy_ref[rows, :], n_ref, r_ref, gain, dz_out_ref, e_ref)
    loaded(weight.at[1], sem.at[1])

    def mixing(columns):
        dmix_ref[:, columns] = bfloat(product_t(e_ref[...], weight[1, columns, :]))

    tiles(mixing, dmix_ref.shape[1], TILE)


def back_kernel(indices, bases, *refs):
    count = len(indices)
    base_refs, grads = refs[:bases], refs[bases : bases + count]
    weights, out_ref, weight, sem = refs[bases + count :]
    load([weights.at[i] for i in indices], [weight.at[j] for j in range(count)], sem)
    for j in range(count):
        loaded(weight.at[j], sem.at[j])

    def back(columns):
        total = None
        for base in base_refs:
            part = base[:, columns].astype(jnp.float32)
            total = part if total is None else total + part
        for j in range(count):
            part = product_t(grads[j][...], weight[j, columns, :])
            total = part if total is None else total + part
        out_ref[:, columns] = total.astype(out_ref.dtype)

    tiles(back, out_ref.shape[1], TILE)


def split(value):
    high = bfloat(value)
    return high, bfloat(value - high.astype(jnp.float32))


def put_left(ref, value):
    high, low = split(value)
    ref[:, :ADAPT] = high
    ref[:, ADAPT : 2 * ADAPT] = high
    ref[:, 2 * ADAPT :] = low


def put_right(ref, value):
    high, low = split(value)
    ref[:ADAPT, :] = high
    ref[ADAPT : 2 * ADAPT, :] = low
    ref[2 * ADAPT :, :] = high


def multiply(out_ref, left, right):
    def body(columns):
        out_ref[:, columns] = product(left[...], right[:, columns])

    tiles(body, ADAPT, TILE)


def muon_kernel(parts, *refs):
    rows_refs, (out_ref, high, low, gram, poly, left, right, rows_left) = refs[:parts], refs[parts:]
    rows = rows_refs[0].shape[0]
    for i, ref in enumerate(rows_refs):
        high[i * rows : (i + 1) * rows, :], low[i * rows : (i + 1) * rows, :] = split(ref[...])

    def square(columns):
        gram[:, columns] = (
            product_rows(high[...], high[:, columns])
            + product_rows(high[...], low[:, columns])
            + product_rows(low[...], high[:, columns])
        )

    tiles(square, ADAPT, TILE)
    eye = lax.broadcasted_iota(jnp.int32, (ADAPT, ADAPT), 0) == lax.broadcasted_iota(
        jnp.int32, (ADAPT, ADAPT), 1
    )
    scale = 1.0 / (jnp.sqrt(jnp.sum(jnp.where(eye, gram[...], 0.0), keepdims=True)) + 1e-07)
    gram[...] = gram[...] * (scale * scale)

    def polynomial():
        put_left(left, gram[...])
        put_right(right, gram[...])
        multiply(poly, left, right)
        poly[...] = (
            jnp.where(eye, NEWTON_LINEAR, 0.0) + NEWTON_QUADRATIC * gram[...] + NEWTON_CUBIC * poly[...]
        )
        put_right(right, poly[...])
        put_left(rows_left, out_ref[...])
        multiply(out_ref, rows_left, right)

    def advance():
        multiply(gram, left, right)
        put_left(left, gram[...])
        multiply(gram, left, right)

    out_ref[...] = rows_refs[0][...] * scale

    @pl.loop(0, NS_ITERS - 1)
    def _(i):
        polynomial()
        advance()

    polynomial()


HBM = pl.BlockSpec(memory_space=pltpu.HBM)
IN_VMEM = pl.BlockSpec(memory_space=pltpu.VMEM)
F32, BF16 = jnp.float32, jnp.bfloat16


def call(kernel, ins, specs, outs, scratch, flops, collective_id=None, after=()):
    if after:
        inner, first = kernel, len(ins)
        kernel = lambda *refs: inner(*refs[:first], *refs[first + len(after) :])
        ins, specs = [*ins, *after], [*specs, *[HBM] * len(after)]
    return pl.pallas_call(
        kernel,
        in_specs=specs,
        out_specs=[IN_VMEM if len(out) == 2 else HBM for out in outs],
        out_shape=[jax.ShapeDtypeStruct(*out[:2]) for out in outs],
        scratch_shapes=scratch,
        compiler_params=pltpu.CompilerParams(
            vmem_limit_bytes=VMEM_LIMIT,
            collective_id=collective_id,
            has_side_effects=collective_id is not None,
        ),
        cost_estimate=pl.CostEstimate(
            flops=flops, bytes_accessed=sum(a.size * a.dtype.itemsize for a in ins), transcendentals=0
        ),
    )(*ins)


def squares(count):
    return pltpu.VMEM((count, D, D), BF16)


def stored(*shape):
    return (shape, BF16, HBM)


def project(collective_id, x, far, pieces, offsets):
    rows = x.shape[0]
    count, n = len(offsets), len(pieces.arrays)
    return call(
        functools.partial(project_kernel, n, pieces.height, offsets),
        [x, far, *pieces.arrays],
        [IN_VMEM] * 2 + [HBM] * n,
        [((rows, D), BF16)] * (count + 2) + [stored(count, D, D)],
        [squares(count), *loader_sems(count, n)],
        2 * rows * D * D * (count + 2),
        collective_id,
    )


def settle(collective_id, x, mix, gains, pieces, wo_at, q_at, gain_rows, after=()):
    rows = x.shape[0]
    n = len(pieces.arrays)
    count = 1 if q_at is None else 2
    outs = [((rows, D), F32), ((rows, STAT), F32)]
    scratch = [squares(count), pltpu.VMEM((rows, D), F32)]
    if q_at is not None:
        outs.append(((rows, D), BF16))
        scratch.append(pltpu.VMEM((rows, D), BF16))
    return call(
        functools.partial(settle_kernel, n, pieces.height, wo_at, q_at, gain_rows),
        [x, mix, gains, *pieces.arrays],
        [IN_VMEM] * 3 + [HBM] * n,
        outs + [stored(count, D, D)],
        scratch + loader_sems(count, n),
        2 * rows * D * D * count,
        collective_id,
        after,
    )


def tail_up(collective_id, normed, gains, pieces, up_at, gain_row):
    rows = normed.shape[0]
    n = len(pieces.arrays)
    blocks = 4
    hidden = blocks * D
    return call(
        functools.partial(tail_up_kernel, n, pieces.height, up_at, gain_row),
        [normed, gains, *pieces.arrays],
        [IN_VMEM] * 2 + [HBM] * n,
        [stored(rows, hidden), stored(rows, hidden), stored(blocks, D, D)],
        [
            squares(blocks),
            pltpu.VMEM((rows, D), BF16),
            pltpu.VMEM((rows, hidden), BF16),
            pltpu.VMEM((rows, hidden), BF16),
            pltpu.SemaphoreType.DMA((2, blocks)),
            *loader_sems(blocks, n),
        ],
        8 * rows * D * D,
        collective_id,
    )


def tail_down(collective_id, normed, inner, gains, bias_first, bias_second, pieces, offsets, gain_rows):
    rows, hidden = inner.shape
    n = len(pieces.arrays)
    return call(
        functools.partial(tail_down_kernel, n, pieces.height, offsets, gain_rows),
        [normed, inner, gains, bias_first[None], bias_second[None], *pieces.arrays],
        [IN_VMEM] * 5 + [HBM] * n,
        [
            ((rows, ADAPT), BF16),
            ((rows, ADAPT), BF16),
            ((rows, D), F32),
            ((rows, STAT), F32),
            ((rows, D), BF16),
            stored(hidden, D),
            stored(D, D),
        ],
        [
            pltpu.VMEM((hidden, D), BF16),
            pltpu.VMEM((D, D), BF16),
            pltpu.VMEM((rows, D), BF16),
            pltpu.VMEM((rows, D), F32),
            *loader_sems(1 + D // TILE, n),
        ],
        10 * rows * D * D,
        collective_id,
    )


def tail_back(height, cot, second, first, gains, slope, pre_slope, adapt_low, weights, gain_rows, more=()):
    rows = cot.shape[0]
    hidden = slope.shape[1]
    return call(
        functools.partial(tail_back_kernel, height, gain_rows, bool(more)),
        [cot, *second, *first, gains, slope, pre_slope, adapt_low, *weights, *more],
        [IN_VMEM] * 6 + [HBM] + [IN_VMEM] * 2 + [HBM] * 4 + [IN_VMEM] * len(more),
        [
            ((rows, D), BF16),
            ((rows, D), F32),
            ((rows, D), BF16),
            ((D // height, 2 * height + BIAS_ROWS, ADAPT), BF16),
        ],
        [
            squares(hidden // D),
            pltpu.VMEM((hidden, D), BF16),
            pltpu.VMEM((D, D), BF16),
            pltpu.VMEM((D, D), BF16),
            pltpu.VMEM((rows, D), F32),
            pltpu.VMEM((rows, D), BF16),
            pltpu.VMEM((rows, D), BF16),
            pltpu.VMEM((rows, hidden), BF16),
            pltpu.VMEM((rows, ADAPT), BF16),
            pltpu.SemaphoreType.DMA((5,)),
        ],
        24 * rows * D * D,
    )


def query_back(dz, dq, first, gains, weights, gain_row):
    rows = dz.shape[0]
    return call(
        functools.partial(query_back_kernel, gain_row),
        [dz, dq, *first, gains, weights],
        [IN_VMEM] * 5 + [HBM],
        [((rows, D), F32), ((rows, D), BF16)],
        [
            squares(2),
            pltpu.VMEM((rows, D), F32),
            pltpu.VMEM((rows, D), BF16),
            pltpu.SemaphoreType.DMA((2,)),
        ],
        4 * rows * D * D,
    )


def back(bases, grads, weights, indices, dtype):
    rows = grads[0].shape[0]
    count = len(indices)
    return call(
        functools.partial(back_kernel, indices, len(bases)),
        [*bases, *grads, weights],
        [IN_VMEM] * (len(bases) + count) + [HBM],
        [((rows, D), dtype)],
        [squares(count), pltpu.SemaphoreType.DMA((count,))],
        2 * rows * D * D * count,
    )[0]


def muon(parts):
    rows = parts[0].shape[0]
    full = pltpu.VMEM((ADAPT, ADAPT), F32)
    return call(
        functools.partial(muon_kernel, len(parts)),
        parts,
        [IN_VMEM] * len(parts),
        [((rows, ADAPT), F32)],
        [
            pltpu.VMEM((rows * len(parts), ADAPT), BF16),
            pltpu.VMEM((rows * len(parts), ADAPT), BF16),
            full,
            full,
            pltpu.VMEM((ADAPT, 3 * ADAPT), BF16),
            pltpu.VMEM((3 * ADAPT, ADAPT), BF16),
            pltpu.VMEM((rows, 3 * ADAPT), BF16),
        ],
        20 * 6 * ADAPT**3,
    )[0]


def axis_bits(axis):
    return [1 << b for b in range(lax.axis_size(axis).bit_length() - 1)]


def tie(array, *others):
    return lax.optimization_barrier((array, *others))[0]


class Gather:
    def __init__(self, array, height):
        self.height = height
        self.array = array

    def begin(self, *after):
        array = tie(self.array, *after) if after else self.array
        steps = ((2, 4), (4, 2))
        self.arrays = [self.array] + [
            lax.ppermute(
                array, "wide", [(i, i ^ steps[i % 2][which]) for i in range(lax.axis_size("wide"))]
            )
            for which in range(2)
        ]
        return self

    def across(self, *after):
        first = tie(self.arrays[1], *after) if after else self.arrays[1]
        self.arrays.append(
            lax.ppermute(
                first, "wide", [(i, i ^ (2 if i % 2 else 4)) for i in range(lax.axis_size("wide"))]
            )
        )
        for bit in axis_bits("wide")[3:]:
            self.arrays += [swap(piece, "wide", bit) for piece in self.arrays]
        return self


def gather_any_order(array, axis):
    blocks = array[None]
    for bit in axis_bits(axis):
        blocks = jnp.concatenate([blocks, swap(blocks, axis, bit)])
    return blocks


def shards(
    enc_in,
    dec_in,
    segment_ids,
    enc_cot,
    dec_cot,
    enc_qkv,
    enc_wo,
    enc_w_in,
    enc_w_out,
    enc_gains,
    dec_qkv,
    dec_wo,
    dec_w_in,
    dec_w_out,
    dec_gains,
    adapter_weights,
    adapter_momenta,
    bias_in,
    bias_out,
):
    height = enc_wo.shape[0]
    stack = lambda *arrays: jnp.concatenate([a.reshape(-1, D) for a in arrays])
    columns = lambda array: [array[:, j * D : (j + 1) * D] for j in range(array.shape[1] // D)]
    gain_rows = jnp.concatenate([enc_gains, dec_gains])
    gain_block = jnp.pad(gain_rows, ((0, 16 - gain_rows.shape[0]), (0, D - height)))
    gather = lambda array: Gather(array, height)
    enc_first = gather(stack(enc_qkv, gain_block))
    dec_first = gather(stack(dec_qkv[:3]))
    enc_up = gather(stack(enc_wo, *columns(enc_w_in)))
    dec_second = gather(stack(dec_wo[0], dec_qkv[3]))
    dec_third = gather(stack(dec_qkv[4:], dec_wo[1]))
    dec_up = gather(stack(*columns(dec_w_in)))

    count = lax.axis_size("wide")
    partner = lambda array: swap(array, "narrow", 1)
    rows = enc_in.shape[0]
    half = (lax.axis_index("narrow") % 2).astype(jnp.int32).reshape(1)
    at = lambda i: i * height

    enc_first.begin()
    enc_far = partner(enc_in)
    enc_first.across()
    begun = enc_first.arrays[-1]
    dec_first.begin(begun)
    dec_far = partner(tie(dec_in, begun))
    other_ids = partner(tie(segment_ids, begun))
    places = (half, segment_ids.reshape(1, rows), segment_ids.reshape(rows, 1), other_ids.reshape(rows, 1))
    found = gather_any_order(bfloat(tie(adapter_weights, begun)), "narrow")
    found = found[lax.axis_index("narrow") ^ jnp.arange(lax.axis_size("narrow"))]
    adapters = found.transpose(1, 0, 2, 3).reshape(4, height, ADAPT)
    beside = lambda l: jnp.concatenate([adapters[2 * l], adapters[2 * l + 1]], axis=1)
    enc_query, enc_key, enc_value, enc_key_far, enc_value_far, enc_qkv_full = project(
        0, tie(enc_in, begun), enc_far, enc_first, (at(0), at(1), at(2))
    )
    enc_keys, enc_values = (enc_key, enc_key_far), (enc_value, enc_value_far)

    repeat = lax.axis_size("narrow") // 4
    spread = lambda array: jnp.repeat(array, repeat, axis=0) if repeat > 1 else array
    exchange = lambda array, axis: lax.all_to_all(array, axis, split_axis=0, concat_axis=0, tiled=True)
    to_matrix = lambda array: exchange(spread(array), "narrow").reshape(-1, ADAPT)
    to_rows = lambda array: exchange(
        array.reshape(lax.axis_size("narrow"), -1, ADAPT), "narrow"
    )[::repeat]

    dec_first.across(enc_value)
    enc_up.begin(enc_value)
    enc_mix, enc_lse = attend(places, enc_query, enc_keys, enc_values, False)
    found = jnp.stack([p[at(3) : at(3) + 8, :height] for p in enc_first.arrays])
    found = jnp.concatenate([found, swap(tie(found, enc_mix), "wide", 1)])
    me = lax.axis_index("wide")
    apart = me ^ jnp.arange(count)
    odd = ((me ^ apart) & 1) == 1
    low = apart & 6
    piece = jnp.where(low == 0, 0, jnp.where(low == 6, 3, jnp.where((low == 2) ^ odd, 1, 2)))
    order = (apart & 1) * (count // 2) + (apart >> 3) * 4 + piece
    gains = found[order].transpose(1, 0, 2).reshape(8, D).astype(jnp.float32)
    enc_down = gather(stack(enc_w_out, tie(beside(0), enc_mix)))
    dec_down = gather(stack(dec_w_out, tie(beside(1), enc_mix)))
    enc_down.begin(enc_mix)
    self_query, self_key, self_value, self_key_far, self_value_far, dec_qkv_full = project(
        1, tie(dec_in, enc_mix), dec_far, dec_first, (at(0), at(1), at(2))
    )
    self_keys, self_values = (self_key, self_key_far), (self_value, self_value_far)
    enc_up.across(self_value)
    self_mix, self_lse = attend(places, self_query, self_keys, self_values, True)
    dec_second.begin(self_mix)
    *enc_norm1, enc_wo_full = settle(
        2, enc_in, tie(enc_mix, self_mix), gains, enc_up, at(0), None, (None, 0)
    )
    enc_down.across(enc_norm1[0])
    enc_slope, enc_inner, enc_up_full = tail_up(3, enc_norm1[0], gains, enc_up, at(1), 0)
    dec_second.across(enc_inner)
    dec_third.begin(enc_inner)
    enc_pre_slope, enc_adapt, *enc_norm2, enc_low, enc_down_full, enc_adapt_full = tail_down(
        4, enc_norm1[0], enc_inner, gains, bias_in[0], bias_out[0], enc_down, (0, at(4)), (0, 1)
    )
    enc_low_far = partner(enc_low)
    dec_third.across(enc_low)
    *dec_norm1, cross_query, dec_q_full = settle(
        5, dec_in, tie(self_mix, enc_low), gains, dec_second, at(0), at(1), (None, 2)
    )
    dec_up.begin(cross_query)
    dec_down.begin(cross_query)
    cross_key, cross_value, cross_key_far, cross_value_far, dec_kv_full = project(
        6, tie(enc_low, cross_query), enc_low_far, dec_third, (at(0), at(1))
    )
    cross_keys, cross_values = (cross_key, cross_key_far), (cross_value, cross_value_far)
    dec_up.across(cross_key)
    cross_mix, cross_lse = attend(places, cross_query, cross_keys, cross_values, False)
    *dec_norm2, dec_wo_full = settle(
        7, dec_norm1[0], cross_mix, gains, dec_third, at(2), None, (2, 3)
    )
    dec_down.across(dec_norm2[0])
    dec_slope, dec_inner, dec_up_full = tail_up(8, dec_norm2[0], gains, dec_up, at(0), 3)
    dec_pre_slope, dec_adapt, *dec_norm3, _, dec_down_full, dec_adapt_full = tail_down(
        9, dec_norm2[0], dec_inner, gains, bias_in[1], bias_out[1], dec_down, (0, at(4)), (3, 4)
    )

    dec_out, grad_z2, grad_cross_mix, dec_matrices = tail_back(
        height,
        dec_cot,
        dec_norm3,
        dec_norm2,
        gains,
        dec_slope,
        dec_pre_slope,
        dec_adapt,
        (dec_up_full, dec_down_full, dec_adapt_full, dec_wo_full),
        (3, 4),
    )
    total = lambda array: jnp.sum(array.astype(jnp.float32), axis=0)
    dec_matrices = exchange(dec_matrices, "wide")
    cross_back = attend_back(
        places, grad_cross_mix, cross_query, cross_keys, cross_values, cross_mix, cross_lse, False
    )
    dec_sums = total(tie(dec_matrices, cross_back[0]))
    far_encoded = back((), (tie(cross_back[2], dec_sums), cross_back[4]), dec_kv_full, (0, 1), BF16)
    near_encoded = partner(far_encoded)
    grad_encoded = back(
        (tie(enc_cot, far_encoded),), (cross_back[1], cross_back[3]), dec_kv_full, (0, 1), F32
    )
    grad_z1, grad_self_mix = query_back(
        tie(grad_z2, grad_encoded),
        cross_back[0],
        dec_norm1,
        gains,
        dec_q_full,
        2,
    )
    enc_out, grad_ez1, grad_enc_mix, enc_matrices = tail_back(
        height,
        tie(grad_encoded, grad_z1),
        enc_norm2,
        enc_norm1,
        gains,
        enc_slope,
        enc_pre_slope,
        enc_adapt,
        (enc_up_full, enc_down_full, enc_adapt_full, enc_wo_full),
        (0, 1),
        (near_encoded,),
    )
    old_momentum = to_matrix(tie(adapter_momenta, grad_z1))
    enc_matrices = exchange(tie(enc_matrices, old_momentum), "wide")

    self_back = attend_back(
        places, tie(grad_self_mix, grad_ez1), self_query, self_keys, self_values, self_mix, self_lse, True, (old_momentum,)
    )

    enc_sums = total(tie(enc_matrices, self_back[0]))
    sums = [array[at(i) : at(i + 1)] for array in (enc_sums, dec_sums) for i in range(2)]
    biases = jnp.concatenate([array[at(2) : at(2) + BIAS_ROWS // 2] for array in (enc_sums, dec_sums)])
    sums = jnp.stack([jnp.concatenate([array, biases]) for array in sums])
    sums = spread(bfloat(sums))
    far_dec = back(
        (), (tie(self_back[2], sums), self_back[4]), dec_qkv_full, (1, 2), BF16
    )
    near_dec = partner(far_dec)
    enc_back = attend_back(
        places, tie(grad_enc_mix, far_dec), enc_query, enc_keys, enc_values, enc_mix, enc_lse, False
    )
    summed = exchange(sums, "narrow")
    summed = total(tie(summed, enc_back[0]))
    momentum = DECAY * old_momentum + summed[:height]
    layers = summed[height:].reshape(2, -1, ADAPT)
    place = lax.axis_index("wide") * lax.axis_size("narrow") + lax.axis_index("narrow")
    devices = lax.axis_size("wide") * lax.axis_size("narrow")
    own_part = lambda array: lax.dynamic_slice_in_dim(
        array, place * (array.shape[1] // devices), array.shape[1] // devices, 1
    )
    grad_bias_in, grad_bias_out = own_part(layers[:, 0]), own_part(layers[:, 1:3].reshape(2, D))
    parts = [momentum] + [swap(momentum, "wide", r) for r in range(1, lax.axis_size("wide"))]
    new_momenta = to_rows(momentum)

    far_enc = back((), (tie(enc_back[2], momentum), enc_back[4]), enc_qkv_full, (1, 2), BF16)
    near_enc = partner(far_enc)
    grad_dec = back(
        (tie(grad_z1, far_enc), near_dec),
        (self_back[0], self_back[1], self_back[3]),
        dec_qkv_full,
        (0, 1, 2),
        F32,
    )
    orthogonal = muon([parts[0], tie(parts[1], grad_dec), *parts[2:]])
    grad_enc = back(
        (tie(grad_ez1, orthogonal), near_enc),
        (enc_back[0], enc_back[1], enc_back[3]),
        enc_qkv_full,
        (0, 1, 2),
        F32,
    )
    new_weights = adapter_weights - RATE * math.sqrt(max(1.0, D / ADAPT)) * tie(
        to_rows(orthogonal), grad_enc
    )
    return (
        enc_out,
        dec_out,
        grad_enc,
        grad_dec,
        grad_bias_in,
        grad_bias_out,
        new_momenta,
        new_weights,
    )


def solution(mesh):
    both = ("wide", "narrow")
    tokens = P(both, None)
    rows_first, rows_second = P("wide", None), P(None, "wide", None)
    adapters = P(None, both, None)
    in_specs = (
        tokens,
        tokens,
        P(both),
        tokens,
        tokens,
        rows_second,
        rows_first,
        rows_first,
        rows_first,
        P(None, "wide"),
        rows_second,
        rows_second,
        rows_first,
        rows_first,
        P(None, "wide"),
        adapters,
        adapters,
        P(),
        P(),
    )
    out_specs = (
        tokens,
        tokens,
        tokens,
        tokens,
        P(None, both),
        P(None, both),
        adapters,
        adapters,
    )
    return jax.shard_map(shards, mesh=mesh, in_specs=in_specs, out_specs=out_specs, check_vma=False)
```

```python
import functools
import math

import jax
import jax.numpy as jnp
from jax import lax
from jax.experimental import pallas as pl
from jax.experimental.pallas import tpu as pltpu
from jax.sharding import PartitionSpec as P

D = 1024
HD = 64
ADAPT = 512
NS_ITERS = 5

EPSILON = 1e-05
MASKED = -1e30
NEWTON_LINEAR = 3.4445
NEWTON_QUADRATIC = -4.775
NEWTON_CUBIC = 2.0315
RATE = 0.7
DECAY = 0.5
LOG2E = 1.4426950408889634
PAIR = 2 * HD
VMEM_LIMIT = 58 * 1024 * 1024
MESH = pl.DeviceIdType.MESH


def swap(array, axis, bit):
    return lax.ppermute(array, axis, [(i, i ^ bit) for i in range(lax.axis_size(axis))])


def bfloat(tensor):
    return tensor.astype(jnp.bfloat16)


def product(left_side, right_side):
    return jnp.dot(left_side, right_side, preferred_element_type=jnp.float32)


def contract(left_side, right_side, left_dim, right_dim):
    return lax.dot_general(
        left_side,
        right_side,
        (((left_dim,), (right_dim,)), ((), ())),
        preferred_element_type=jnp.float32,
    )


def product_t(left_side, right_side):
    return contract(left_side, right_side, 1, 1)


def product_rows(left_side, right_side):
    return contract(left_side, right_side, 0, 0)


def gelu_both(tensor):
    phi = 0.5 * (1.0 + lax.erf(tensor * 0.7071067811865476))
    slope = phi + tensor * jnp.exp(-0.5 * tensor * tensor) * 0.3989422804014327
    return tensor * phi, slope


def fill_bias(half_ref, qid_ref, kid_own_ref, kid_far_ref, bias_ref, causal):
    rows = qid_ref.shape[1]
    qid = qid_ref[...]
    for part, kid_ref in enumerate((kid_own_ref, kid_far_ref)):
        allowed = kid_ref[...] == qid
        if causal:
            if part == 0:
                key_at = lax.broadcasted_iota(jnp.int32, (rows, rows), 0)
                query_at = lax.broadcasted_iota(jnp.int32, (rows, rows), 1)
                allowed = allowed & (key_at <= query_at)
            else:
                allowed = allowed & (half_ref[0] == 1)
        bias_ref[pl.ds(part * rows, rows), :] = jnp.where(allowed, 0.0, MASKED)


def head_mask(rows, head):
    return lax.broadcasted_iota(jnp.int32, (rows, PAIR), 1) // HD == head


def attend_kernel(
    causal,
    chunk,
    half_ref,
    qid_ref,
    kid_own_ref,
    kid_far_ref,
    q_ref,
    k_own_ref,
    k_far_ref,
    v_own_ref,
    v_far_ref,
    out_ref,
    lse_ref,
    bias_ref,
    score_ref,
):
    rows = q_ref.shape[0]

    @pl.when(pl.program_id(0) == 0)
    def _():
        fill_bias(half_ref, qid_ref, kid_own_ref, kid_far_ref, bias_ref, causal)

    queries = q_ref[...] * 0.125
    steps = [
        (part, at)
        for part in range(2)
        for at in range(0, rows, chunk)
    ]
    keys = (k_own_ref, k_far_ref)
    values = (v_own_ref, v_far_ref)
    q_both = jnp.concatenate(
        [jnp.where(head_mask(rows, h), queries, jnp.zeros_like(queries)) for h in range(2)], axis=0
    )
    peak = None
    for part, at in steps:
        place = pl.ds(part * rows + at, chunk)
        bias = bias_ref[place, :]
        scores = product_t(keys[part][pl.ds(at, chunk), :], q_both)
        scores = scores * LOG2E + jnp.concatenate([bias, bias], axis=1)
        score_ref[place, :] = scores
        top = jnp.max(scores, axis=0, keepdims=True)
        peak = top if peak is None else jnp.maximum(peak, top)
    total, mix = None, None
    for part, at in steps:
        place = pl.ds(part * rows + at, chunk)
        raised = jnp.exp2(score_ref[place, :] - peak)
        share = jnp.sum(raised, axis=0, keepdims=True)
        piece = product_rows(values[part][pl.ds(at, chunk), :], bfloat(raised))
        total = share if total is None else total + share
        mix = piece if mix is None else mix + piece
    mix = mix * (1.0 / total)
    mixes = [mix[:HD, :rows], mix[HD:, rows:]]
    lse = peak + jnp.log2(total)
    lse_ref[0, pl.ds(0, 1), :] = lse[:, :rows]
    lse_ref[0, pl.ds(1, 1), :] = lse[:, rows:]
    out_ref[...] = bfloat(jnp.concatenate(mixes, axis=0).T)


def attend_back_kernel(
    causal,
    chunk,
    half_ref,
    qid_ref,
    kid_own_ref,
    kid_far_ref,
    q_ref,
    k_own_ref,
    k_far_ref,
    v_own_ref,
    v_far_ref,
    out_ref,
    grad_ref,
    lse_ref,
    dq_ref,
    dk_own_ref,
    dk_far_ref,
    dv_own_ref,
    dv_far_ref,
    bias_ref,
):
    rows = q_ref.shape[0]

    @pl.when(pl.program_id(0) == 0)
    def _():
        fill_bias(half_ref, qid_ref, kid_own_ref, kid_far_ref, bias_ref, causal)

    queries = q_ref[...] * 0.125
    grads = grad_ref[...]
    products = (grads.astype(jnp.float32) * out_ref[...].astype(jnp.float32)).T
    q_heads, g_heads, deltas, lses = [], [], [], []
    for head in range(2):
        chosen = head_mask(rows, head)
        q_heads.append(jnp.where(chosen, queries, jnp.zeros_like(queries)))
        g_heads.append(jnp.where(chosen, grads, jnp.zeros_like(grads)))
        deltas.append(jnp.sum(products[head * HD : (head + 1) * HD, :], axis=0, keepdims=True))
        lses.append(lse_ref[0, pl.ds(head, 1), :])
    q_both, g_both = jnp.concatenate(q_heads, axis=0), jnp.concatenate(g_heads, axis=0)
    lse, delta = jnp.concatenate(lses, axis=1), jnp.concatenate(deltas, axis=1)
    grad_q = None
    for part in range(2):
        key_ref = (k_own_ref, k_far_ref)[part]
        value_ref = (v_own_ref, v_far_ref)[part]
        dk_ref = (dk_own_ref, dk_far_ref)[part]
        dv_ref = (dv_own_ref, dv_far_ref)[part]
        for at in range(0, rows, chunk):
            here = pl.ds(at, chunk)
            keys, values = key_ref[here, :], value_ref[here, :]
            bias = bias_ref[pl.ds(part * rows + at, chunk), :]
            scores = product_t(keys, q_both)
            weights = jnp.exp2(scores * LOG2E + (jnp.concatenate([bias, bias], axis=1) - lse))
            grad_s = bfloat(weights * (product_t(values, g_both) - delta))
            dv_ref[here, :] = product(bfloat(weights), g_both).astype(dv_ref.dtype)
            dk_ref[here, :] = product(grad_s, q_both).astype(dk_ref.dtype)
            piece = product_rows(keys, grad_s)
            grad_q = piece if grad_q is None else grad_q + piece
    joined = jnp.concatenate([grad_q[:HD, :rows], grad_q[HD:, rows:]], axis=0)
    dq_ref[...] = bfloat((joined * 0.125).T)


def attention_specs(rows):
    whole = lambda shape: pl.BlockSpec(shape, lambda i: (0,) * len(shape))
    columns = pl.BlockSpec((rows, PAIR), lambda i: (0, i))
    fixed = [
        pl.BlockSpec(memory_space=pltpu.SMEM),
        whole((1, rows)),
        whole((rows, 1)),
        whole((rows, 1)),
    ]
    return fixed, columns, pl.BlockSpec((1, 8, rows), lambda i: (i, 0, 0))


def attend(places, queries, keys, values, causal):
    rows, width = queries.shape
    pairs = width // PAIR
    fixed, columns, stat = attention_specs(rows)
    return pl.pallas_call(
        functools.partial(attend_kernel, causal, 512),
        grid=(pairs,),
        in_specs=fixed + [columns] * 5,
        out_specs=[columns, stat],
        out_shape=[
            jax.ShapeDtypeStruct((rows, width), jnp.bfloat16),
            jax.ShapeDtypeStruct((pairs, 8, rows), jnp.float32),
        ],
        scratch_shapes=[
            pltpu.VMEM((2 * rows, rows), jnp.float32),
            pltpu.VMEM((2 * rows, 2 * rows), jnp.float32),
        ],
        compiler_params=pltpu.CompilerParams(vmem_limit_bytes=VMEM_LIMIT),
        cost_estimate=pl.CostEstimate(
            flops=32 * rows * rows * width, bytes_accessed=12 * rows * width, transcendentals=0
        ),
    )(*places, queries, *keys, *values)


def attend_back(places, grad_out, queries, keys, values, mix, lse, causal, after=()):
    rows, width = queries.shape
    pairs = width // PAIR
    fixed, columns, stat = attention_specs(rows)
    return pl.pallas_call(
        lambda *refs: attend_back_kernel(causal, 512, *refs[:12], *refs[12 + len(after) :]),
        grid=(pairs,),
        in_specs=fixed + [columns] * 7 + [stat] + [HBM] * len(after),
        out_specs=[columns] * 5,
        out_shape=[
            jax.ShapeDtypeStruct((rows, width), jnp.bfloat16),
        ]
        * 5,
        scratch_shapes=[pltpu.VMEM((2 * rows, rows), jnp.float32)],
        compiler_params=pltpu.CompilerParams(vmem_limit_bytes=VMEM_LIMIT),
        cost_estimate=pl.CostEstimate(
            flops=80 * rows * rows * width, bytes_accessed=24 * rows * width, transcendentals=0
        ),
    )(*places, queries, *keys, *values, mix, grad_out, lse, *after)


def flipped(me, bits):
    place = me
    bit = 1
    while bit <= bits:
        if bits & bit:
            place = place + bit * (1 - 2 * lax.rem(lax.div(me, bit), 2))
        bit *= 2
    return place


def place_of(me, piece):
    odd = lax.rem(me, 2)
    place = me
    if piece % 4 in (1, 2):
        first, second = (2, 4) if piece % 4 == 1 else (4, 2)
        place = flipped(me, first) * (1 - odd) + flipped(me, second) * odd
    elif piece % 4 == 3:
        place = flipped(me, 6)
    return place + (flipped(me, 2 * (piece - piece % 4)) - me)


class Loader:
    def __init__(self, sems):
        self.local, self.send, self.recv, self.stored = sems
        self.copies, self.stores = [], []
        self.me = lax.axis_index("wide")
        self.sibling = {"wide": flipped(self.me, 1)}
        barrier = pltpu.get_barrier_semaphore()
        pl.semaphore_signal(barrier, inc=1, device_id=self.sibling, device_id_type=MESH)
        pl.semaphore_wait(barrier, 1)

    def fetch(self, pieces, offset, height, target, columns=slice(None)):
        block = len(self.copies)
        copies = []
        for i, piece in enumerate(pieces):
            at = pl.multiple_of(place_of(self.me, i) * height, height)
            source = piece.at[pl.ds(offset, height), columns]
            place = target.at[pl.ds(at, height), columns]
            near = pltpu.make_async_copy(source, place, self.local.at[block, i])
            far = pltpu.make_async_remote_copy(
                source,
                place,
                self.send.at[block, i],
                self.recv.at[block, i],
                device_id=self.sibling,
                device_id_type=MESH,
            )
            near.start()
            far.start()
            copies.append((near, far))
        self.copies.append(copies)
        return block

    def arrived(self, block, target, out):
        for near, far in self.copies[block]:
            near.wait()
            far.wait_recv()
        store = pltpu.make_async_copy(target, out, self.stored.at[block])
        store.start()
        self.stores.append(store)

    def finish(self):
        for copies in self.copies:
            for _, far in copies:
                far.wait_send()
        for store in self.stores:
            store.wait()


def loader_sems(blocks, pieces):
    dma = pltpu.SemaphoreType.DMA
    return [dma((blocks, pieces))] * 3 + [dma((blocks,))]


def load(weights, targets, sem):
    for j, (weight, target) in enumerate(zip(weights, targets)):
        pltpu.make_async_copy(weight, target, sem.at[j]).start()


def loaded(target, sem):
    pltpu.make_async_copy(target, target, sem).wait()


def tiles(body, width, step):
    @pl.loop(0, width // step)
    def _(i):
        body(pl.ds(pl.multiple_of(i * step, step), step))


ROWS = 256
TILE = 512
STAT = 128
BIAS_ROWS = 16


def normalise(z_ref, n_ref, r_ref, gain, low_ref):
    def body(rows):
        z = z_ref[rows, :]
        centred = z - jnp.mean(z, axis=-1, keepdims=True)
        inverse = lax.rsqrt(jnp.mean(centred * centred, axis=-1, keepdims=True) + EPSILON)
        normed = centred * inverse
        n_ref[rows, :] = normed
        r_ref[rows, :] = jnp.broadcast_to(inverse, (ROWS, STAT))
        if low_ref is not None:
            low_ref[rows, :] = bfloat(normed * gain)

    tiles(body, z_ref.shape[0], ROWS)


def normalise_back(read_grad, n_ref, r_ref, gain, dz_ref, low_ref):
    def body(rows):
        scaled = read_grad(rows) * gain
        normed = n_ref[rows, :]
        dz = r_ref[rows, :][:, :1] * (
            scaled
            - jnp.mean(scaled, axis=-1, keepdims=True)
            - normed * jnp.mean(scaled * normed, axis=-1, keepdims=True)
        )
        dz_ref[rows, :] = dz
        low_ref[rows, :] = bfloat(dz)

    tiles(body, n_ref.shape[0], ROWS)


def project_kernel(n, height, offsets, x_ref, far_ref, *refs):
    count = len(offsets)
    pieces, outs, full, (weight, *sems) = refs[:n], refs[n:-6], refs[-6], refs[-5:]
    loader = Loader(sems)
    for j, offset in enumerate(offsets):
        loader.fetch(pieces, offset, height, weight.at[j])
    for j in range(count):
        loader.arrived(j, weight.at[j], full.at[j])
        far = outs[count + j - (count - 2)] if j >= count - 2 else None

        def body(columns):
            outs[j][:, columns] = bfloat(product(x_ref[...], weight[j, :, columns]))
            if far is not None:
                far[:, columns] = bfloat(product(far_ref[...], weight[j, :, columns]))

        tiles(body, outs[j].shape[1], TILE)
    loader.finish()


def settle_kernel(n, height, wo_at, q_at, gain_rows, x_ref, mix_ref, gains_ref, *refs):
    pieces, refs = refs[:n], refs[n:]
    if q_at is None:
        n_ref, r_ref, full, weight, z_ref, *sems = refs
        low_ref = None
    else:
        n_ref, r_ref, q_ref, full, weight, z_ref, low_ref, *sems = refs
    loader = Loader(sems)
    loader.fetch(pieces, wo_at, height, weight.at[0])
    if q_at is not None:
        loader.fetch(pieces, q_at, height, weight.at[1])
    loader.arrived(0, weight.at[0], full.at[0])

    def project(columns):
        x = x_ref[:, columns].astype(jnp.float32)
        if gain_rows[0] is not None:
            x = x * gains_ref[pl.ds(gain_rows[0], 1), columns]
        z_ref[:, columns] = x + product(mix_ref[...], weight[0, :, columns])

    tiles(project, z_ref.shape[1], TILE)
    gain = gains_ref[pl.ds(gain_rows[1], 1), :]
    normalise(z_ref, n_ref, r_ref, gain, low_ref)
    if q_at is not None:
        loader.arrived(1, weight.at[1], full.at[1])

        def query(columns):
            q_ref[:, columns] = bfloat(product(low_ref[...], weight[1, :, columns]))

        tiles(query, q_ref.shape[1], TILE)
    loader.finish()


def tail_up_kernel(n, height, up_at, gain_row, n_ref, gains_ref, *refs):
    pieces = refs[:n]
    slope_hbm, inner_hbm, full, up, low_ref, slope_ref, inner_ref, out_sem, *sems = refs[n:]
    blocks = up.shape[0]
    loader = Loader(sems)
    for j in range(blocks):
        loader.fetch(pieces, up_at + j * height, height, up.at[j])
    gain = gains_ref[pl.ds(gain_row, 1), :]

    def lower(rows):
        low_ref[rows, :] = bfloat(n_ref[rows, :] * gain)

    tiles(lower, n_ref.shape[0], ROWS)
    width = up.shape[2]
    outs = []
    for j in range(blocks):
        loader.arrived(j, up.at[j], full.at[j])

        def upward(columns):
            inner, slope = gelu_both(product(low_ref[...], up[j, :, columns]))
            place = pl.ds(pl.multiple_of(j * width + columns.start, TILE), TILE)
            inner_ref[:, place] = bfloat(inner)
            slope_ref[:, place] = bfloat(slope)

        tiles(upward, width, TILE)
        columns = pl.ds(j * width, width)
        for i, (ref, hbm) in enumerate(((inner_ref, inner_hbm), (slope_ref, slope_hbm))):
            out = pltpu.make_async_copy(ref.at[:, columns], hbm.at[:, columns], out_sem.at[i, j])
            out.start()
            outs.append(out)
    loader.finish()
    for out in outs:
        out.wait()


def tail_down_kernel(n, height, offsets, gain_rows, n_ref, inner_ref, gains_ref, first_ref, second_ref, *refs):
    pieces, refs = refs[:n], refs[n:]
    pre_slope_ref, adapt_ref, n_out_ref, r_out_ref, out_ref, down_full, adapt_full = refs[:7]
    down, adapt, low_ref, z_ref, *sems = refs[7:]
    down_at, adapt_at = offsets
    width = z_ref.shape[1]
    loader = Loader(sems)
    loader.fetch(pieces, adapt_at, height, adapt)
    for at in range(0, width, TILE):
        loader.fetch(pieces, down_at, down.shape[0] // width * height, down, pl.ds(at, TILE))
    gain = gains_ref[pl.ds(gain_rows[0], 1), :]

    def lower(rows):
        low_ref[rows, :] = bfloat(n_ref[rows, :] * gain)

    tiles(lower, n_ref.shape[0], ROWS)
    loader.arrived(0, adapt, adapt_full)

    def adapting(columns):
        pre = product(low_ref[...], adapt[:, columns]) + first_ref[:, columns]
        adapted, slope = gelu_both(pre)
        adapt_ref[:, columns] = bfloat(adapted)
        pre_slope_ref[:, columns] = bfloat(slope)

    tiles(adapting, ADAPT, TILE)
    for i, at in enumerate(range(0, width, TILE)):
        columns = pl.ds(at, TILE)
        loader.arrived(1 + i, down.at[:, columns], down_full.at[:, columns])
        h = n_ref[:, columns] * gains_ref[pl.ds(gain_rows[0], 1), columns]
        ffn = product(inner_ref[...], down[:, columns])
        adapted = product_t(adapt_ref[...], adapt[columns, ADAPT:]) + second_ref[:, columns]
        z_ref[:, columns] = h + ffn + 4.0 * adapted
    normalise(z_ref, n_out_ref, r_out_ref, gains_ref[pl.ds(gain_rows[1], 1), :], out_ref)
    loader.finish()


def tail_back_kernel(height, gain_rows, more, *refs):
    (cot_ref, n2_ref, r2_ref, n1_ref, r1_ref, gains_ref, slope_hbm, pre_slope_ref, adapt_low_ref) = refs[:9]
    refs = refs[9:]
    (up_hbm, down_hbm, adapt_hbm, wo_hbm), refs = refs[:4], refs[4:]
    if more:
        far_ref, refs = refs[0], refs[1:]
    out_ref, dz_ref, dmix_ref, matrices_ref = refs[:4]
    up, down, adapt, wo, dt_ref, e_ref, low_ref, du_ref, dpre_ref, sem = refs[4:]
    blocks = up.shape[0]
    load(
        [adapt_hbm, down_hbm, slope_hbm, up_hbm, wo_hbm.at[0]],
        [adapt, down, du_ref, up, wo],
        sem,
    )
    gain1 = gains_ref[pl.ds(gain_rows[0], 1), :]
    gain2 = gains_ref[pl.ds(gain_rows[1], 1), :]

    def lower(rows):
        low_ref[rows, :] = bfloat(n1_ref[rows, :] * gain1)
        out_ref[rows, :] = bfloat(n2_ref[rows, :] * gain2)

    tiles(lower, n1_ref.shape[0], ROWS)

    def arriving(rows):
        grad = cot_ref[rows, :].astype(jnp.float32)
        return grad + far_ref[rows, :].astype(jnp.float32) if more else grad

    normalise_back(arriving, n2_ref, r2_ref, gain2, dt_ref, e_ref)
    loaded(adapt, sem.at[0])

    def adapting(columns):
        back = 4.0 * product(e_ref[...], adapt[:, pl.ds(ADAPT + columns.start, TILE)])
        dpre_ref[:, columns] = bfloat(back * pre_slope_ref[:, columns].astype(jnp.float32))

    tiles(adapting, ADAPT, TILE)
    first = jnp.sum(dpre_ref[...].astype(jnp.float32), axis=0, keepdims=True)
    second = 4.0 * jnp.sum(e_ref[...].astype(jnp.float32), axis=0, keepdims=True)
    row = lax.broadcasted_iota(jnp.int32, (BIAS_ROWS, ADAPT), 0)
    biases = jnp.where(row == 1, second[:, :ADAPT], jnp.where(row == 2, second[:, ADAPT:], 0.0))
    biases = bfloat(jnp.where(row == 0, first, biases))
    for block in range(matrices_ref.shape[0]):
        matrices_ref[block, 2 * height :, :] = biases

    wide = max(height, TILE)

    def matrices(columns):
        down_grad = bfloat(product_rows(low_ref[:, columns], dpre_ref[...]))
        up_grad = bfloat(4.0 * product_rows(e_ref[:, columns], adapt_low_ref[...]))
        for i in range(wide // height):
            block, rows = columns.start // height + i, slice(i * height, (i + 1) * height)
            matrices_ref[block, :height, :] = down_grad[rows, :]
            matrices_ref[block, height : 2 * height, :] = up_grad[rows, :]

    tiles(matrices, low_ref.shape[1], wide)
    loaded(down, sem.at[1])
    loaded(du_ref, sem.at[2])

    def inner(columns):
        back = product_t(e_ref[...], down[columns, :])
        du_ref[:, columns] = bfloat(back * du_ref[:, columns].astype(jnp.float32))

    tiles(inner, du_ref.shape[1], TILE)
    loaded(up, sem.at[3])
    width = up.shape[2]

    def hidden(columns):
        total = dt_ref[:, columns] + product_t(dpre_ref[...], adapt[columns, :ADAPT])
        for j in range(blocks):
            total += product_t(du_ref[:, j * width : (j + 1) * width], up[j, columns, :])
        dt_ref[:, columns] = total

    tiles(hidden, dt_ref.shape[1], TILE)
    normalise_back(lambda rows: dt_ref[rows, :], n1_ref, r1_ref, gain1, dz_ref, e_ref)
    loaded(wo, sem.at[4])

    def mixing(columns):
        dmix_ref[:, columns] = bfloat(product_t(e_ref[...], wo[columns, :]))

    tiles(mixing, dmix_ref.shape[1], TILE)


def query_back_kernel(gain_row, dz_ref, dq_ref, n_ref, r_ref, gains_ref, weights, *refs):
    dz_out_ref, dmix_ref, weight, dy_ref, e_ref, sem = refs
    load([weights.at[1], weights.at[0]], [weight.at[0], weight.at[1]], sem)
    loaded(weight.at[0], sem.at[0])

    def back(columns):
        dy_ref[:, columns] = dz_ref[:, columns] + product_t(dq_ref[...], weight[0, columns, :])

    tiles(back, dy_ref.shape[1], TILE)
    gain = gains_ref[pl.ds(gain_row, 1), :]
    normalise_back(lambda rows: dy_ref[rows, :], n_ref, r_ref, gain, dz_out_ref, e_ref)
    loaded(weight.at[1], sem.at[1])

    def mixing(columns):
        dmix_ref[:, columns] = bfloat(product_t(e_ref[...], weight[1, columns, :]))

    tiles(mixing, dmix_ref.shape[1], TILE)


def back_kernel(indices, bases, *refs):
    count = len(indices)
    base_refs, grads = refs[:bases], refs[bases : bases + count]
    weights, out_ref, weight, sem = refs[bases + count :]
    load([weights.at[i] for i in indices], [weight.at[j] for j in range(count)], sem)
    for j in range(count):
        loaded(weight.at[j], sem.at[j])

    def back(columns):
        total = None
        for base in base_refs:
            part = base[:, columns].astype(jnp.float32)
            total = part if total is None else total + part
        for j in range(count):
            part = product_t(grads[j][...], weight[j, columns, :])
            total = part if total is None else total + part
        out_ref[:, columns] = total.astype(out_ref.dtype)

    tiles(back, out_ref.shape[1], TILE)


def split(value):
    high = bfloat(value)
    return high, bfloat(value - high.astype(jnp.float32))


def put_left(ref, value):
    high, low = split(value)
    ref[:, :ADAPT] = high
    ref[:, ADAPT : 2 * ADAPT] = high
    ref[:, 2 * ADAPT :] = low


def put_right(ref, value):
    high, low = split(value)
    ref[:ADAPT, :] = high
    ref[ADAPT : 2 * ADAPT, :] = low
    ref[2 * ADAPT :, :] = high


def multiply(out_ref, left, right):
    def body(columns):
        out_ref[:, columns] = product(left[...], right[:, columns])

    tiles(body, ADAPT, TILE)


def muon_kernel(parts, *refs):
    rows_refs, (out_ref, high, low, gram, poly, left, right, rows_left) = refs[:parts], refs[parts:]
    rows = rows_refs[0].shape[0]
    for i, ref in enumerate(rows_refs):
        high[i * rows : (i + 1) * rows, :], low[i * rows : (i + 1) * rows, :] = split(ref[...])

    def square(columns):
        gram[:, columns] = (
            product_rows(high[...], high[:, columns])
            + product_rows(high[...], low[:, columns])
            + product_rows(low[...], high[:, columns])
        )

    tiles(square, ADAPT, TILE)
    eye = lax.broadcasted_iota(jnp.int32, (ADAPT, ADAPT), 0) == lax.broadcasted_iota(
        jnp.int32, (ADAPT, ADAPT), 1
    )
    scale = 1.0 / (jnp.sqrt(jnp.sum(jnp.where(eye, gram[...], 0.0), keepdims=True)) + 1e-07)
    gram[...] = gram[...] * (scale * scale)

    def polynomial():
        put_left(left, gram[...])
        put_right(right, gram[...])
        multiply(poly, left, right)
        poly[...] = (
            jnp.where(eye, NEWTON_LINEAR, 0.0) + NEWTON_QUADRATIC * gram[...] + NEWTON_CUBIC * poly[...]
        )
        put_right(right, poly[...])
        put_left(rows_left, out_ref[...])
        multiply(out_ref, rows_left, right)

    def advance():
        multiply(gram, left, right)
        put_left(left, gram[...])
        multiply(gram, left, right)

    out_ref[...] = rows_refs[0][...] * scale

    @pl.loop(0, NS_ITERS - 1)
    def _(i):
        polynomial()
        advance()

    polynomial()


HBM = pl.BlockSpec(memory_space=pltpu.HBM)
IN_VMEM = pl.BlockSpec(memory_space=pltpu.VMEM)
F32, BF16 = jnp.float32, jnp.bfloat16


def call(kernel, ins, specs, outs, scratch, flops, collective_id=None, after=()):
    if after:
        inner, first = kernel, len(ins)
        kernel = lambda *refs: inner(*refs[:first], *refs[first + len(after) :])
        ins, specs = [*ins, *after], [*specs, *[HBM] * len(after)]
    return pl.pallas_call(
        kernel,
        in_specs=specs,
        out_specs=[IN_VMEM if len(out) == 2 else HBM for out in outs],
        out_shape=[jax.ShapeDtypeStruct(*out[:2]) for out in outs],
        scratch_shapes=scratch,
        compiler_params=pltpu.CompilerParams(
            vmem_limit_bytes=VMEM_LIMIT,
            collective_id=collective_id,
            has_side_effects=collective_id is not None,
        ),
        cost_estimate=pl.CostEstimate(
            flops=flops, bytes_accessed=sum(a.size * a.dtype.itemsize for a in ins), transcendentals=0
        ),
    )(*ins)


def squares(count):
    return pltpu.VMEM((count, D, D), BF16)


def stored(*shape):
    return (shape, BF16, HBM)


def project(collective_id, x, far, pieces, offsets):
    rows = x.shape[0]
    count, n = len(offsets), len(pieces.arrays)
    return call(
        functools.partial(project_kernel, n, pieces.height, offsets),
        [x, far, *pieces.arrays],
        [IN_VMEM] * 2 + [HBM] * n,
        [((rows, D), BF16)] * (count + 2) + [stored(count, D, D)],
        [squares(count), *loader_sems(count, n)],
        2 * rows * D * D * (count + 2),
        collective_id,
    )


def settle(collective_id, x, mix, gains, pieces, wo_at, q_at, gain_rows, after=()):
    rows = x.shape[0]
    n = len(pieces.arrays)
    count = 1 if q_at is None else 2
    outs = [((rows, D), F32), ((rows, STAT), F32)]
    scratch = [squares(count), pltpu.VMEM((rows, D), F32)]
    if q_at is not None:
        outs.append(((rows, D), BF16))
        scratch.append(pltpu.VMEM((rows, D), BF16))
    return call(
        functools.partial(settle_kernel, n, pieces.height, wo_at, q_at, gain_rows),
        [x, mix, gains, *pieces.arrays],
        [IN_VMEM] * 3 + [HBM] * n,
        outs + [stored(count, D, D)],
        scratch + loader_sems(count, n),
        2 * rows * D * D * count,
        collective_id,
        after,
    )


def tail_up(collective_id, normed, gains, pieces, up_at, gain_row):
    rows = normed.shape[0]
    n = len(pieces.arrays)
    blocks = 4
    hidden = blocks * D
    return call(
        functools.partial(tail_up_kernel, n, pieces.height, up_at, gain_row),
        [normed, gains, *pieces.arrays],
        [IN_VMEM] * 2 + [HBM] * n,
        [stored(rows, hidden), stored(rows, hidden), stored(blocks, D, D)],
        [
            squares(blocks),
            pltpu.VMEM((rows, D), BF16),
            pltpu.VMEM((rows, hidden), BF16),
            pltpu.VMEM((rows, hidden), BF16),
            pltpu.SemaphoreType.DMA((2, blocks)),
            *loader_sems(blocks, n),
        ],
        8 * rows * D * D,
        collective_id,
    )


def tail_down(collective_id, normed, inner, gains, bias_first, bias_second, pieces, offsets, gain_rows):
    rows, hidden = inner.shape
    n = len(pieces.arrays)
    return call(
        functools.partial(tail_down_kernel, n, pieces.height, offsets, gain_rows),
        [normed, inner, gains, bias_first[None], bias_second[None], *pieces.arrays],
        [IN_VMEM] * 5 + [HBM] * n,
        [
            ((rows, ADAPT), BF16),
            ((rows, ADAPT), BF16),
            ((rows, D), F32),
            ((rows, STAT), F32),
            ((rows, D), BF16),
            stored(hidden, D),
            stored(D, D),
        ],
        [
            pltpu.VMEM((hidden, D), BF16),
            pltpu.VMEM((D, D), BF16),
            pltpu.VMEM((rows, D), BF16),
            pltpu.VMEM((rows, D), F32),
            *loader_sems(1 + D // TILE, n),
        ],
        10 * rows * D * D,
        collective_id,
    )


def tail_back(height, cot, second, first, gains, slope, pre_slope, adapt_low, weights, gain_rows, more=()):
    rows = cot.shape[0]
    hidden = slope.shape[1]
    return call(
        functools.partial(tail_back_kernel, height, gain_rows, bool(more)),
        [cot, *second, *first, gains, slope, pre_slope, adapt_low, *weights, *more],
        [IN_VMEM] * 6 + [HBM] + [IN_VMEM] * 2 + [HBM] * 4 + [IN_VMEM] * len(more),
        [
            ((rows, D), BF16),
            ((rows, D), F32),
            ((rows, D), BF16),
            ((D // height, 2 * height + BIAS_ROWS, ADAPT), BF16),
        ],
        [
            squares(hidden // D),
            pltpu.VMEM((hidden, D), BF16),
            pltpu.VMEM((D, D), BF16),
            pltpu.VMEM((D, D), BF16),
            pltpu.VMEM((rows, D), F32),
            pltpu.VMEM((rows, D), BF16),
            pltpu.VMEM((rows, D), BF16),
            pltpu.VMEM((rows, hidden), BF16),
            pltpu.VMEM((rows, ADAPT), BF16),
            pltpu.SemaphoreType.DMA((5,)),
        ],
        24 * rows * D * D,
    )


def query_back(dz, dq, first, gains, weights, gain_row):
    rows = dz.shape[0]
    return call(
        functools.partial(query_back_kernel, gain_row),
        [dz, dq, *first, gains, weights],
        [IN_VMEM] * 5 + [HBM],
        [((rows, D), F32), ((rows, D), BF16)],
        [
            squares(2),
            pltpu.VMEM((rows, D), F32),
            pltpu.VMEM((rows, D), BF16),
            pltpu.SemaphoreType.DMA((2,)),
        ],
        4 * rows * D * D,
    )


def back(bases, grads, weights, indices, dtype):
    rows = grads[0].shape[0]
    count = len(indices)
    return call(
        functools.partial(back_kernel, indices, len(bases)),
        [*bases, *grads, weights],
        [IN_VMEM] * (len(bases) + count) + [HBM],
        [((rows, D), dtype)],
        [squares(count), pltpu.SemaphoreType.DMA((count,))],
        2 * rows * D * D * count,
    )[0]


def muon(parts):
    rows = parts[0].shape[0]
    full = pltpu.VMEM((ADAPT, ADAPT), F32)
    return call(
        functools.partial(muon_kernel, len(parts)),
        parts,
        [IN_VMEM] * len(parts),
        [((rows, ADAPT), F32)],
        [
            pltpu.VMEM((rows * len(parts), ADAPT), BF16),
            pltpu.VMEM((rows * len(parts), ADAPT), BF16),
            full,
            full,
            pltpu.VMEM((ADAPT, 3 * ADAPT), BF16),
            pltpu.VMEM((3 * ADAPT, ADAPT), BF16),
            pltpu.VMEM((rows, 3 * ADAPT), BF16),
        ],
        20 * 6 * ADAPT**3,
    )[0]


def axis_bits(axis):
    return [1 << b for b in range(lax.axis_size(axis).bit_length() - 1)]


def tie(array, *others):
    return lax.optimization_barrier((array, *others))[0]


class Gather:
    def __init__(self, array, height):
        self.height = height
        self.array = array

    def begin(self, *after):
        array = tie(self.array, *after) if after else self.array
        steps = ((2, 4), (4, 2))
        self.arrays = [self.array] + [
            lax.ppermute(
                array, "wide", [(i, i ^ steps[i % 2][which]) for i in range(lax.axis_size("wide"))]
            )
            for which in range(2)
        ]
        return self

    def across(self, *after):
        first = tie(self.arrays[1], *after) if after else self.arrays[1]
        self.arrays.append(
            lax.ppermute(
                first, "wide", [(i, i ^ (2 if i % 2 else 4)) for i in range(lax.axis_size("wide"))]
            )
        )
        for bit in axis_bits("wide")[3:]:
            self.arrays += [swap(piece, "wide", bit) for piece in self.arrays]
        return self


def gather_any_order(array, axis):
    blocks = array[None]
    for bit in axis_bits(axis):
        blocks = jnp.concatenate([blocks, swap(blocks, axis, bit)])
    return blocks


def shards(
    enc_in,
    dec_in,
    segment_ids,
    enc_cot,
    dec_cot,
    enc_qkv,
    enc_wo,
    enc_w_in,
    enc_w_out,
    enc_gains,
    dec_qkv,
    dec_wo,
    dec_w_in,
    dec_w_out,
    dec_gains,
    adapter_weights,
    adapter_momenta,
    bias_in,
    bias_out,
):
    height = enc_wo.shape[0]
    stack = lambda *arrays: jnp.concatenate([a.reshape(-1, D) for a in arrays])
    columns = lambda array: [array[:, j * D : (j + 1) * D] for j in range(array.shape[1] // D)]
    gain_rows = jnp.concatenate([enc_gains, dec_gains])
    gain_block = jnp.pad(gain_rows, ((0, 16 - gain_rows.shape[0]), (0, D - height)))
    gather = lambda array: Gather(array, height)
    enc_first = gather(stack(enc_qkv, gain_block))
    dec_first = gather(stack(dec_qkv[:3]))
    enc_up = gather(stack(enc_wo, *columns(enc_w_in)))
    dec_second = gather(stack(dec_wo[0], dec_qkv[3]))
    dec_third = gather(stack(dec_qkv[4:], dec_wo[1]))
    dec_up = gather(stack(*columns(dec_w_in)))

    count = lax.axis_size("wide")
    partner = lambda array: swap(array, "narrow", 1)
    rows = enc_in.shape[0]
    half = (lax.axis_index("narrow") % 2).astype(jnp.int32).reshape(1)
    at = lambda i: i * height

    enc_first.begin()
    enc_far = partner(enc_in)
    enc_first.across()
    begun = enc_first.arrays[-1]
    dec_first.begin(begun)
    dec_far = partner(tie(dec_in, begun))
    other_ids = partner(tie(segment_ids, begun))
    places = (half, segment_ids.reshape(1, rows), segment_ids.reshape(rows, 1), other_ids.reshape(rows, 1))
    found = gather_any_order(bfloat(tie(adapter_weights, begun)), "narrow")
    found = found[lax.axis_index("narrow") ^ jnp.arange(lax.axis_size("narrow"))]
    adapters = found.transpose(1, 0, 2, 3).reshape(4, height, ADAPT)
    beside = lambda l: jnp.concatenate([adapters[2 * l], adapters[2 * l + 1]], axis=1)
    enc_query, enc_key, enc_value, enc_key_far, enc_value_far, enc_qkv_full = project(
        0, tie(enc_in, begun), enc_far, enc_first, (at(0), at(1), at(2))
    )
    enc_keys, enc_values = (enc_key, enc_key_far), (enc_value, enc_value_far)

    repeat = lax.axis_size("narrow") // 4
    spread = lambda array: jnp.repeat(array, repeat, axis=0) if repeat > 1 else array
    exchange = lambda array, axis: lax.all_to_all(array, axis, split_axis=0, concat_axis=0, tiled=True)
    to_matrix = lambda array: exchange(spread(array), "narrow").reshape(-1, ADAPT)
    to_rows = lambda array: exchange(
        array.reshape(lax.axis_size("narrow"), -1, ADAPT), "narrow"
    )[::repeat]

    dec_first.across(enc_value)
    enc_up.begin(enc_value)
    enc_mix, enc_lse = attend(places, enc_query, enc_keys, enc_values, False)
    found = jnp.stack([p[at(3) : at(3) + 8, :height] for p in enc_first.arrays])
    found = jnp.concatenate([found, swap(tie(found, enc_mix), "wide", 1)])
    me = lax.axis_index("wide")
    apart = me ^ jnp.arange(count)
    odd = ((me ^ apart) & 1) == 1
    low = apart & 6
    piece = jnp.where(low == 0, 0, jnp.where(low == 6, 3, jnp.where((low == 2) ^ odd, 1, 2)))
    order = (apart & 1) * (count // 2) + (apart >> 3) * 4 + piece
    gains = found[order].transpose(1, 0, 2).reshape(8, D).astype(jnp.float32)
    enc_down = gather(stack(enc_w_out, tie(beside(0), enc_mix)))
    dec_down = gather(stack(dec_w_out, tie(beside(1), enc_mix)))
    enc_down.begin(enc_mix)
    self_query, self_key, self_value, self_key_far, self_value_far, dec_qkv_full = project(
        1, tie(dec_in, enc_mix), dec_far, dec_first, (at(0), at(1), at(2))
    )
    self_keys, self_values = (self_key, self_key_far), (self_value, self_value_far)
    enc_up.across(self_value)
    self_mix, self_lse = attend(places, self_query, self_keys, self_values, True)
    dec_second.begin(self_mix)
    *enc_norm1, enc_wo_full = settle(
        2, enc_in, tie(enc_mix, self_mix), gains, enc_up, at(0), None, (None, 0)
    )
    enc_down.across(enc_norm1[0])
    enc_slope, enc_inner, enc_up_full = tail_up(3, enc_norm1[0], gains, enc_up, at(1), 0)
    dec_second.across(enc_inner)
    dec_third.begin(enc_inner)
    enc_pre_slope, enc_adapt, *enc_norm2, enc_low, enc_down_full, enc_adapt_full = tail_down(
        4, enc_norm1[0], enc_inner, gains, bias_in[0], bias_out[0], enc_down, (0, at(4)), (0, 1)
    )
    enc_low_far = partner(enc_low)
    dec_third.across(enc_low)
    *dec_norm1, cross_query, dec_q_full = settle(
        5, dec_in, tie(self_mix, enc_low), gains, dec_second, at(0), at(1), (None, 2)
    )
    dec_up.begin(cross_query)
    dec_down.begin(cross_query)
    cross_key, cross_value, cross_key_far, cross_value_far, dec_kv_full = project(
        6, tie(enc_low, cross_query), enc_low_far, dec_third, (at(0), at(1))
    )
    cross_keys, cross_values = (cross_key, cross_key_far), (cross_value, cross_value_far)
    dec_up.across(cross_key)
    cross_mix, cross_lse = attend(places, cross_query, cross_keys, cross_values, False)
    *dec_norm2, dec_wo_full = settle(
        7, dec_norm1[0], cross_mix, gains, dec_third, at(2), None, (2, 3)
    )
    dec_down.across(dec_norm2[0])
    dec_slope, dec_inner, dec_up_full = tail_up(8, dec_norm2[0], gains, dec_up, at(0), 3)
    dec_pre_slope, dec_adapt, *dec_norm3, _, dec_down_full, dec_adapt_full = tail_down(
        9, dec_norm2[0], dec_inner, gains, bias_in[1], bias_out[1], dec_down, (0, at(4)), (3, 4)
    )

    dec_out, grad_z2, grad_cross_mix, dec_matrices = tail_back(
        height,
        dec_cot,
        dec_norm3,
        dec_norm2,
        gains,
        dec_slope,
        dec_pre_slope,
        dec_adapt,
        (dec_up_full, dec_down_full, dec_adapt_full, dec_wo_full),
        (3, 4),
    )
    total = lambda array: jnp.sum(array.astype(jnp.float32), axis=0)
    dec_matrices = exchange(dec_matrices, "wide")
    cross_back = attend_back(
        places, grad_cross_mix, cross_query, cross_keys, cross_values, cross_mix, cross_lse, False
    )
    dec_sums = total(tie(dec_matrices, cross_back[0]))
    far_encoded = back((), (tie(cross_back[2], dec_sums), cross_back[4]), dec_kv_full, (0, 1), BF16)
    near_encoded = partner(far_encoded)
    grad_encoded = back(
        (tie(enc_cot, far_encoded),), (cross_back[1], cross_back[3]), dec_kv_full, (0, 1), F32
    )
    grad_z1, grad_self_mix = query_back(
        tie(grad_z2, grad_encoded),
        cross_back[0],
        dec_norm1,
        gains,
        dec_q_full,
        2,
    )
    enc_out, grad_ez1, grad_enc_mix, enc_matrices = tail_back(
        height,
        tie(grad_encoded, grad_z1),
        enc_norm2,
        enc_norm1,
        gains,
        enc_slope,
        enc_pre_slope,
        enc_adapt,
        (enc_up_full, enc_down_full, enc_adapt_full, enc_wo_full),
        (0, 1),
        (near_encoded,),
    )
    old_momentum = to_matrix(tie(adapter_momenta, grad_z1))
    enc_matrices = exchange(tie(enc_matrices, old_momentum), "wide")

    self_back = attend_back(
        places, tie(grad_self_mix, grad_ez1), self_query, self_keys, self_values, self_mix, self_lse, True, (old_momentum,)
    )

    enc_sums = total(tie(enc_matrices, self_back[0]))
    sums = [array[at(i) : at(i + 1)] for array in (enc_sums, dec_sums) for i in range(2)]
    biases = jnp.concatenate([array[at(2) : at(2) + BIAS_ROWS // 2] for array in (enc_sums, dec_sums)])
    sums = jnp.stack([jnp.concatenate([array, biases]) for array in sums])
    sums = spread(bfloat(sums))
    far_dec = back(
        (), (tie(self_back[2], sums), self_back[4]), dec_qkv_full, (1, 2), BF16
    )
    near_dec = partner(far_dec)
    enc_back = attend_back(
        places, tie(grad_enc_mix, far_dec), enc_query, enc_keys, enc_values, enc_mix, enc_lse, False
    )
    summed = exchange(sums, "narrow")
    summed = total(tie(summed, enc_back[0]))
    momentum = DECAY * old_momentum + summed[:height]
    layers = summed[height:].reshape(2, -1, ADAPT)
    place = lax.axis_index("wide") * lax.axis_size("narrow") + lax.axis_index("narrow")
    devices = lax.axis_size("wide") * lax.axis_size("narrow")
    own_part = lambda array: lax.dynamic_slice_in_dim(
        array, place * (array.shape[1] // devices), array.shape[1] // devices, 1
    )
    grad_bias_in, grad_bias_out = own_part(layers[:, 0]), own_part(layers[:, 1:3].reshape(2, D))
    parts = [momentum] + [swap(momentum, "wide", r) for r in range(1, lax.axis_size("wide"))]
    new_momenta = to_rows(momentum)

    far_enc = back((), (tie(enc_back[2], momentum), enc_back[4]), enc_qkv_full, (1, 2), BF16)
    near_enc = partner(far_enc)
    grad_dec = back(
        (tie(grad_z1, far_enc), near_dec),
        (self_back[0], self_back[1], self_back[3]),
        dec_qkv_full,
        (0, 1, 2),
        F32,
    )
    orthogonal = muon([parts[0], tie(parts[1], grad_dec), *parts[2:]])
    grad_enc = back(
        (tie(grad_ez1, orthogonal), near_enc),
        (enc_back[0], enc_back[1], enc_back[3]),
        enc_qkv_full,
        (0, 1, 2),
        F32,
    )
    new_weights = adapter_weights - RATE * math.sqrt(max(1.0, D / ADAPT)) * tie(
        to_rows(orthogonal), grad_enc
    )
    return (
        enc_out,
        dec_out,
        grad_enc,
        grad_dec,
        grad_bias_in,
        grad_bias_out,
        new_momenta,
        new_weights,
    )


def solution(mesh):
    both = ("wide", "narrow")
    tokens = P(both, None)
    rows_first, rows_second = P("wide", None), P(None, "wide", None)
    adapters = P(None, both, None)
    in_specs = (
        tokens,
        tokens,
        P(both),
        tokens,
        tokens,
        rows_second,
        rows_first,
        rows_first,
        rows_first,
        P(None, "wide"),
        rows_second,
        rows_second,
        rows_first,
        rows_first,
        P(None, "wide"),
        adapters,
        adapters,
        P(),
        P(),
    )
    out_specs = (
        tokens,
        tokens,
        tokens,
        tokens,
        P(None, both),
        P(None, both),
        adapters,
        adapters,
    )
    return jax.shard_map(shards, mesh=mesh, in_specs=in_specs, out_specs=out_specs, check_vma=False)
```

```python
import functools
import math

import jax
import jax.numpy as jnp
from jax import lax
from jax.experimental import pallas as pl
from jax.experimental.pallas import tpu as pltpu
from jax.sharding import PartitionSpec as P

D = 1024
HD = 64
ADAPT = 512
NS_ITERS = 5

EPSILON = 1e-05
MASKED = -1e30
NEWTON_LINEAR = 3.4445
NEWTON_QUADRATIC = -4.775
NEWTON_CUBIC = 2.0315
RATE = 0.7
DECAY = 0.5
LOG2E = 1.4426950408889634
PAIR = 2 * HD
VMEM_LIMIT = 58 * 1024 * 1024
MESH = pl.DeviceIdType.MESH


def swap(array, axis, bit):
    return lax.ppermute(array, axis, [(i, i ^ bit) for i in range(lax.axis_size(axis))])


def bfloat(tensor):
    return tensor.astype(jnp.bfloat16)


def product(left_side, right_side):
    return jnp.dot(left_side, right_side, preferred_element_type=jnp.float32)


def contract(left_side, right_side, left_dim, right_dim):
    return lax.dot_general(
        left_side,
        right_side,
        (((left_dim,), (right_dim,)), ((), ())),
        preferred_element_type=jnp.float32,
    )


def product_t(left_side, right_side):
    return contract(left_side, right_side, 1, 1)


def product_rows(left_side, right_side):
    return contract(left_side, right_side, 0, 0)


def gelu_both(tensor):
    phi = 0.5 * (1.0 + lax.erf(tensor * 0.7071067811865476))
    slope = phi + tensor * jnp.exp(-0.5 * tensor * tensor) * 0.3989422804014327
    return tensor * phi, slope


def fill_bias(half_ref, qid_ref, kid_own_ref, kid_far_ref, bias_ref, causal):
    rows = qid_ref.shape[1]
    qid = qid_ref[...]
    for part, kid_ref in enumerate((kid_own_ref, kid_far_ref)):
        allowed = kid_ref[...] == qid
        if causal:
            if part == 0:
                key_at = lax.broadcasted_iota(jnp.int32, (rows, rows), 0)
                query_at = lax.broadcasted_iota(jnp.int32, (rows, rows), 1)
                allowed = allowed & (key_at <= query_at)
            else:
                allowed = allowed & (half_ref[0] == 1)
        bias_ref[pl.ds(part * rows, rows), :] = jnp.where(allowed, 0.0, MASKED)


def head_mask(rows, head):
    return lax.broadcasted_iota(jnp.int32, (rows, PAIR), 1) // HD == head


def attend_kernel(
    causal,
    chunk,
    half_ref,
    qid_ref,
    kid_own_ref,
    kid_far_ref,
    q_ref,
    k_own_ref,
    k_far_ref,
    v_own_ref,
    v_far_ref,
    out_ref,
    lse_ref,
    bias_ref,
    score_ref,
):
    rows = q_ref.shape[0]

    @pl.when(pl.program_id(0) == 0)
    def _():
        fill_bias(half_ref, qid_ref, kid_own_ref, kid_far_ref, bias_ref, causal)

    queries = q_ref[...] * 0.125
    steps = [
        (part, at)
        for part in range(2)
        for at in range(0, rows, chunk)
    ]
    keys = (k_own_ref, k_far_ref)
    values = (v_own_ref, v_far_ref)
    q_both = jnp.concatenate(
        [jnp.where(head_mask(rows, h), queries, jnp.zeros_like(queries)) for h in range(2)], axis=0
    )
    peak = None
    for part, at in steps:
        place = pl.ds(part * rows + at, chunk)
        bias = bias_ref[place, :]
        scores = product_t(keys[part][pl.ds(at, chunk), :], q_both)
        scores = scores * LOG2E + jnp.concatenate([bias, bias], axis=1)
        score_ref[place, :] = scores
        top = jnp.max(scores, axis=0, keepdims=True)
        peak = top if peak is None else jnp.maximum(peak, top)
    total, mix = None, None
    for part, at in steps:
        place = pl.ds(part * rows + at, chunk)
        raised = jnp.exp2(score_ref[place, :] - peak)
        share = jnp.sum(raised, axis=0, keepdims=True)
        piece = product_rows(values[part][pl.ds(at, chunk), :], bfloat(raised))
        total = share if total is None else total + share
        mix = piece if mix is None else mix + piece
    mix = mix * (1.0 / total)
    mixes = [mix[:HD, :rows], mix[HD:, rows:]]
    lse = peak + jnp.log2(total)
    lse_ref[0, pl.ds(0, 1), :] = lse[:, :rows]
    lse_ref[0, pl.ds(1, 1), :] = lse[:, rows:]
    out_ref[...] = bfloat(jnp.concatenate(mixes, axis=0).T)


def attend_back_kernel(
    causal,
    chunk,
    half_ref,
    qid_ref,
    kid_own_ref,
    kid_far_ref,
    q_ref,
    k_own_ref,
    k_far_ref,
    v_own_ref,
    v_far_ref,
    out_ref,
    grad_ref,
    lse_ref,
    dq_ref,
    dk_own_ref,
    dk_far_ref,
    dv_own_ref,
    dv_far_ref,
    bias_ref,
):
    rows = q_ref.shape[0]

    @pl.when(pl.program_id(0) == 0)
    def _():
        fill_bias(half_ref, qid_ref, kid_own_ref, kid_far_ref, bias_ref, causal)

    queries = q_ref[...] * 0.125
    grads = grad_ref[...]
    products = (grads.astype(jnp.float32) * out_ref[...].astype(jnp.float32)).T
    q_heads, g_heads, deltas, lses = [], [], [], []
    for head in range(2):
        chosen = head_mask(rows, head)
        q_heads.append(jnp.where(chosen, queries, jnp.zeros_like(queries)))
        g_heads.append(jnp.where(chosen, grads, jnp.zeros_like(grads)))
        deltas.append(jnp.sum(products[head * HD : (head + 1) * HD, :], axis=0, keepdims=True))
        lses.append(lse_ref[0, pl.ds(head, 1), :])
    q_both, g_both = jnp.concatenate(q_heads, axis=0), jnp.concatenate(g_heads, axis=0)
    lse, delta = jnp.concatenate(lses, axis=1), jnp.concatenate(deltas, axis=1)
    grad_q = None
    for part in range(2):
        key_ref = (k_own_ref, k_far_ref)[part]
        value_ref = (v_own_ref, v_far_ref)[part]
        dk_ref = (dk_own_ref, dk_far_ref)[part]
        dv_ref = (dv_own_ref, dv_far_ref)[part]
        for at in range(0, rows, chunk):
            here = pl.ds(at, chunk)
            keys, values = key_ref[here, :], value_ref[here, :]
            bias = bias_ref[pl.ds(part * rows + at, chunk), :]
            scores = product_t(keys, q_both)
            weights = jnp.exp2(scores * LOG2E + (jnp.concatenate([bias, bias], axis=1) - lse))
            grad_s = bfloat(weights * (product_t(values, g_both) - delta))
            dv_ref[here, :] = product(bfloat(weights), g_both).astype(dv_ref.dtype)
            dk_ref[here, :] = product(grad_s, q_both).astype(dk_ref.dtype)
            piece = product_rows(keys, grad_s)
            grad_q = piece if grad_q is None else grad_q + piece
    joined = jnp.concatenate([grad_q[:HD, :rows], grad_q[HD:, rows:]], axis=0)
    dq_ref[...] = bfloat((joined * 0.125).T)


def attention_specs(rows):
    whole = lambda shape: pl.BlockSpec(shape, lambda i: (0,) * len(shape))
    columns = pl.BlockSpec((rows, PAIR), lambda i: (0, i))
    fixed = [
        pl.BlockSpec(memory_space=pltpu.SMEM),
        whole((1, rows)),
        whole((rows, 1)),
        whole((rows, 1)),
    ]
    return fixed, columns, pl.BlockSpec((1, 8, rows), lambda i: (i, 0, 0))


def attend(places, queries, keys, values, causal):
    rows, width = queries.shape
    pairs = width // PAIR
    fixed, columns, stat = attention_specs(rows)
    return pl.pallas_call(
        functools.partial(attend_kernel, causal, 512),
        grid=(pairs,),
        in_specs=fixed + [columns] * 5,
        out_specs=[columns, stat],
        out_shape=[
            jax.ShapeDtypeStruct((rows, width), jnp.bfloat16),
            jax.ShapeDtypeStruct((pairs, 8, rows), jnp.float32),
        ],
        scratch_shapes=[
            pltpu.VMEM((2 * rows, rows), jnp.float32),
            pltpu.VMEM((2 * rows, 2 * rows), jnp.float32),
        ],
        compiler_params=pltpu.CompilerParams(vmem_limit_bytes=VMEM_LIMIT),
        cost_estimate=pl.CostEstimate(
            flops=32 * rows * rows * width, bytes_accessed=12 * rows * width, transcendentals=0
        ),
    )(*places, queries, *keys, *values)


def attend_back(places, grad_out, queries, keys, values, mix, lse, causal, after=()):
    rows, width = queries.shape
    pairs = width // PAIR
    fixed, columns, stat = attention_specs(rows)
    return pl.pallas_call(
        lambda *refs: attend_back_kernel(causal, 512, *refs[:12], *refs[12 + len(after) :]),
        grid=(pairs,),
        in_specs=fixed + [columns] * 7 + [stat] + [HBM] * len(after),
        out_specs=[columns] * 5,
        out_shape=[
            jax.ShapeDtypeStruct((rows, width), jnp.bfloat16),
        ]
        * 5,
        scratch_shapes=[pltpu.VMEM((2 * rows, rows), jnp.float32)],
        compiler_params=pltpu.CompilerParams(vmem_limit_bytes=VMEM_LIMIT),
        cost_estimate=pl.CostEstimate(
            flops=80 * rows * rows * width, bytes_accessed=24 * rows * width, transcendentals=0
        ),
    )(*places, queries, *keys, *values, mix, grad_out, lse, *after)


def flipped(me, bits):
    place = me
    bit = 1
    while bit <= bits:
        if bits & bit:
            place = place + bit * (1 - 2 * lax.rem(lax.div(me, bit), 2))
        bit *= 2
    return place


def place_of(me, piece):
    odd = lax.rem(me, 2)
    place = me
    if piece % 4 in (1, 2):
        first, second = (2, 4) if piece % 4 == 1 else (4, 2)
        place = flipped(me, first) * (1 - odd) + flipped(me, second) * odd
    elif piece % 4 == 3:
        place = flipped(me, 6)
    return place + (flipped(me, 2 * (piece - piece % 4)) - me)


class Loader:
    def __init__(self, sems):
        self.local, self.send, self.recv, self.stored = sems
        self.copies, self.stores = [], []
        self.me = lax.axis_index("wide")
        self.sibling = {"wide": flipped(self.me, 1)}
        barrier = pltpu.get_barrier_semaphore()
        pl.semaphore_signal(barrier, inc=1, device_id=self.sibling, device_id_type=MESH)
        pl.semaphore_wait(barrier, 1)

    def fetch(self, pieces, offset, height, target, columns=slice(None)):
        block = len(self.copies)
        copies = []
        for i, piece in enumerate(pieces):
            at = pl.multiple_of(place_of(self.me, i) * height, height)
            source = piece.at[pl.ds(offset, height), columns]
            place = target.at[pl.ds(at, height), columns]
            near = pltpu.make_async_copy(source, place, self.local.at[block, i])
            far = pltpu.make_async_remote_copy(
                source,
                place,
                self.send.at[block, i],
                self.recv.at[block, i],
                device_id=self.sibling,
                device_id_type=MESH,
            )
            near.start()
            far.start()
            copies.append((near, far))
        self.copies.append(copies)
        return block

    def arrived(self, block, target, out):
        for near, far in self.copies[block]:
            near.wait()
            far.wait_recv()
        store = pltpu.make_async_copy(target, out, self.stored.at[block])
        store.start()
        self.stores.append(store)

    def finish(self):
        for copies in self.copies:
            for _, far in copies:
                far.wait_send()
        for store in self.stores:
            store.wait()


def loader_sems(blocks, pieces):
    dma = pltpu.SemaphoreType.DMA
    return [dma((blocks, pieces))] * 3 + [dma((blocks,))]


def load(weights, targets, sem):
    for j, (weight, target) in enumerate(zip(weights, targets)):
        pltpu.make_async_copy(weight, target, sem.at[j]).start()


def loaded(target, sem):
    pltpu.make_async_copy(target, target, sem).wait()


def tiles(body, width, step):
    @pl.loop(0, width // step)
    def _(i):
        body(pl.ds(pl.multiple_of(i * step, step), step))


ROWS = 256
TILE = 512
STAT = 128
BIAS_ROWS = 16


def normalise(z_ref, n_ref, r_ref, gain, low_ref):
    def body(rows):
        z = z_ref[rows, :]
        centred = z - jnp.mean(z, axis=-1, keepdims=True)
        inverse = lax.rsqrt(jnp.mean(centred * centred, axis=-1, keepdims=True) + EPSILON)
        normed = centred * inverse
        n_ref[rows, :] = normed
        r_ref[rows, :] = jnp.broadcast_to(inverse, (ROWS, STAT))
        if low_ref is not None:
            low_ref[rows, :] = bfloat(normed * gain)

    tiles(body, z_ref.shape[0], ROWS)


def normalise_back(read_grad, n_ref, r_ref, gain, dz_ref, low_ref):
    def body(rows):
        scaled = read_grad(rows) * gain
        normed = n_ref[rows, :]
        dz = r_ref[rows, :][:, :1] * (
            scaled
            - jnp.mean(scaled, axis=-1, keepdims=True)
            - normed * jnp.mean(scaled * normed, axis=-1, keepdims=True)
        )
        dz_ref[rows, :] = dz
        low_ref[rows, :] = bfloat(dz)

    tiles(body, n_ref.shape[0], ROWS)


def project_kernel(n, height, offsets, x_ref, far_ref, *refs):
    count = len(offsets)
    pieces, outs, full, (weight, *sems) = refs[:n], refs[n:-6], refs[-6], refs[-5:]
    loader = Loader(sems)
    for j, offset in enumerate(offsets):
        loader.fetch(pieces, offset, height, weight.at[j])
    for j in range(count):
        loader.arrived(j, weight.at[j], full.at[j])
        far = outs[count + j - (count - 2)] if j >= count - 2 else None

        def body(columns):
            outs[j][:, columns] = bfloat(product(x_ref[...], weight[j, :, columns]))
            if far is not None:
                far[:, columns] = bfloat(product(far_ref[...], weight[j, :, columns]))

        tiles(body, outs[j].shape[1], TILE)
    loader.finish()


def settle_kernel(n, height, wo_at, q_at, gain_rows, x_ref, mix_ref, gains_ref, *refs):
    pieces, refs = refs[:n], refs[n:]
    if q_at is None:
        n_ref, r_ref, full, weight, z_ref, *sems = refs
        low_ref = None
    else:
        n_ref, r_ref, q_ref, full, weight, z_ref, low_ref, *sems = refs
    loader = Loader(sems)
    loader.fetch(pieces, wo_at, height, weight.at[0])
    if q_at is not None:
        loader.fetch(pieces, q_at, height, weight.at[1])
    loader.arrived(0, weight.at[0], full.at[0])

    def project(columns):
        x = x_ref[:, columns].astype(jnp.float32)
        if gain_rows[0] is not None:
            x = x * gains_ref[pl.ds(gain_rows[0], 1), columns]
        z_ref[:, columns] = x + product(mix_ref[...], weight[0, :, columns])

    tiles(project, z_ref.shape[1], TILE)
    gain = gains_ref[pl.ds(gain_rows[1], 1), :]
    normalise(z_ref, n_ref, r_ref, gain, low_ref)
    if q_at is not None:
        loader.arrived(1, weight.at[1], full.at[1])

        def query(columns):
            q_ref[:, columns] = bfloat(product(low_ref[...], weight[1, :, columns]))

        tiles(query, q_ref.shape[1], TILE)
    loader.finish()


def tail_up_kernel(n, height, up_at, gain_row, n_ref, gains_ref, *refs):
    pieces = refs[:n]
    slope_hbm, inner_hbm, full, up, low_ref, slope_ref, inner_ref, out_sem, *sems = refs[n:]
    blocks = up.shape[0]
    loader = Loader(sems)
    for j in range(blocks):
        loader.fetch(pieces, up_at + j * height, height, up.at[j])
    gain = gains_ref[pl.ds(gain_row, 1), :]

    def lower(rows):
        low_ref[rows, :] = bfloat(n_ref[rows, :] * gain)

    tiles(lower, n_ref.shape[0], ROWS)
    width = up.shape[2]
    outs = []
    for j in range(blocks):
        loader.arrived(j, up.at[j], full.at[j])

        def upward(columns):
            inner, slope = gelu_both(product(low_ref[...], up[j, :, columns]))
            place = pl.ds(pl.multiple_of(j * width + columns.start, TILE), TILE)
            inner_ref[:, place] = bfloat(inner)
            slope_ref[:, place] = bfloat(slope)

        tiles(upward, width, TILE)
        columns = pl.ds(j * width, width)
        for i, (ref, hbm) in enumerate(((inner_ref, inner_hbm), (slope_ref, slope_hbm))):
            out = pltpu.make_async_copy(ref.at[:, columns], hbm.at[:, columns], out_sem.at[i, j])
            out.start()
            outs.append(out)
    loader.finish()
    for out in outs:
        out.wait()


def tail_down_kernel(n, height, offsets, gain_rows, n_ref, inner_ref, gains_ref, first_ref, second_ref, *refs):
    pieces, refs = refs[:n], refs[n:]
    pre_slope_ref, adapt_ref, n_out_ref, r_out_ref, out_ref, down_full, adapt_full = refs[:7]
    down, adapt, low_ref, z_ref, *sems = refs[7:]
    down_at, adapt_at = offsets
    width = z_ref.shape[1]
    loader = Loader(sems)
    loader.fetch(pieces, adapt_at, height, adapt)
    for at in range(0, width, TILE):
        loader.fetch(pieces, down_at, down.shape[0] // width * height, down, pl.ds(at, TILE))
    gain = gains_ref[pl.ds(gain_rows[0], 1), :]

    def lower(rows):
        low_ref[rows, :] = bfloat(n_ref[rows, :] * gain)

    tiles(lower, n_ref.shape[0], ROWS)
    loader.arrived(0, adapt, adapt_full)

    def adapting(columns):
        pre = product(low_ref[...], adapt[:, columns]) + first_ref[:, columns]
        adapted, slope = gelu_both(pre)
        adapt_ref[:, columns] = bfloat(adapted)
        pre_slope_ref[:, columns] = bfloat(slope)

    tiles(adapting, ADAPT, TILE)
    for i, at in enumerate(range(0, width, TILE)):
        columns = pl.ds(at, TILE)
        loader.arrived(1 + i, down.at[:, columns], down_full.at[:, columns])
        h = n_ref[:, columns] * gains_ref[pl.ds(gain_rows[0], 1), columns]
        ffn = product(inner_ref[...], down[:, columns])
        adapted = product_t(adapt_ref[...], adapt[columns, ADAPT:]) + second_ref[:, columns]
        z_ref[:, columns] = h + ffn + 4.0 * adapted
    normalise(z_ref, n_out_ref, r_out_ref, gains_ref[pl.ds(gain_rows[1], 1), :], out_ref)
    loader.finish()


def tail_back_kernel(height, gain_rows, more, *refs):
    (cot_ref, n2_ref, r2_ref, n1_ref, r1_ref, gains_ref, slope_hbm, pre_slope_ref, adapt_low_ref) = refs[:9]
    refs = refs[9:]
    (up_hbm, down_hbm, adapt_hbm, wo_hbm), refs = refs[:4], refs[4:]
    if more:
        far_ref, refs = refs[0], refs[1:]
    out_ref, dz_ref, dmix_ref, matrices_ref = refs[:4]
    up, down, adapt, wo, dt_ref, e_ref, low_ref, du_ref, dpre_ref, sem = refs[4:]
    blocks = up.shape[0]
    load(
        [adapt_hbm, down_hbm, slope_hbm, up_hbm, wo_hbm.at[0]],
        [adapt, down, du_ref, up, wo],
        sem,
    )
    gain1 = gains_ref[pl.ds(gain_rows[0], 1), :]
    gain2 = gains_ref[pl.ds(gain_rows[1], 1), :]

    def lower(rows):
        low_ref[rows, :] = bfloat(n1_ref[rows, :] * gain1)
        out_ref[rows, :] = bfloat(n2_ref[rows, :] * gain2)

    tiles(lower, n1_ref.shape[0], ROWS)

    def arriving(rows):
        grad = cot_ref[rows, :].astype(jnp.float32)
        return grad + far_ref[rows, :].astype(jnp.float32) if more else grad

    normalise_back(arriving, n2_ref, r2_ref, gain2, dt_ref, e_ref)
    loaded(adapt, sem.at[0])

    def adapting(columns):
        back = 4.0 * product(e_ref[...], adapt[:, pl.ds(ADAPT + columns.start, TILE)])
        dpre_ref[:, columns] = bfloat(back * pre_slope_ref[:, columns].astype(jnp.float32))

    tiles(adapting, ADAPT, TILE)
    first = jnp.sum(dpre_ref[...].astype(jnp.float32), axis=0, keepdims=True)
    second = 4.0 * jnp.sum(e_ref[...].astype(jnp.float32), axis=0, keepdims=True)
    row = lax.broadcasted_iota(jnp.int32, (BIAS_ROWS, ADAPT), 0)
    biases = jnp.where(row == 1, second[:, :ADAPT], jnp.where(row == 2, second[:, ADAPT:], 0.0))
    biases = bfloat(jnp.where(row == 0, first, biases))
    for block in range(matrices_ref.shape[0]):
        matrices_ref[block, 2 * height :, :] = biases

    wide = max(height, TILE)

    def matrices(columns):
        down_grad = bfloat(product_rows(low_ref[:, columns], dpre_ref[...]))
        up_grad = bfloat(4.0 * product_rows(e_ref[:, columns], adapt_low_ref[...]))
        for i in range(wide // height):
            block, rows = columns.start // height + i, slice(i * height, (i + 1) * height)
            matrices_ref[block, :height, :] = down_grad[rows, :]
            matrices_ref[block, height : 2 * height, :] = up_grad[rows, :]

    tiles(matrices, low_ref.shape[1], wide)
    loaded(down, sem.at[1])
    loaded(du_ref, sem.at[2])

    def inner(columns):
        back = product_t(e_ref[...], down[columns, :])
        du_ref[:, columns] = bfloat(back * du_ref[:, columns].astype(jnp.float32))

    tiles(inner, du_ref.shape[1], TILE)
    loaded(up, sem.at[3])
    width = up.shape[2]

    def hidden(columns):
        total = dt_ref[:, columns] + product_t(dpre_ref[...], adapt[columns, :ADAPT])
        for j in range(blocks):
            total += product_t(du_ref[:, j * width : (j + 1) * width], up[j, columns, :])
        dt_ref[:, columns] = total

    tiles(hidden, dt_ref.shape[1], TILE)
    normalise_back(lambda rows: dt_ref[rows, :], n1_ref, r1_ref, gain1, dz_ref, e_ref)
    loaded(wo, sem.at[4])

    def mixing(columns):
        dmix_ref[:, columns] = bfloat(product_t(e_ref[...], wo[columns, :]))

    tiles(mixing, dmix_ref.shape[1], TILE)


def query_back_kernel(gain_row, dz_ref, dq_ref, n_ref, r_ref, gains_ref, weights, *refs):
    dz_out_ref, dmix_ref, weight, dy_ref, e_ref, sem = refs
    load([weights.at[1], weights.at[0]], [weight.at[0], weight.at[1]], sem)
    loaded(weight.at[0], sem.at[0])

    def back(columns):
        dy_ref[:, columns] = dz_ref[:, columns] + product_t(dq_ref[...], weight[0, columns, :])

    tiles(back, dy_ref.shape[1], TILE)
    gain = gains_ref[pl.ds(gain_row, 1), :]
    normalise_back(lambda rows: dy_ref[rows, :], n_ref, r_ref, gain, dz_out_ref, e_ref)
    loaded(weight.at[1], sem.at[1])

    def mixing(columns):
        dmix_ref[:, columns] = bfloat(product_t(e_ref[...], weight[1, columns, :]))

    tiles(mixing, dmix_ref.shape[1], TILE)


def back_kernel(indices, bases, *refs):
    count = len(indices)
    base_refs, grads = refs[:bases], refs[bases : bases + count]
    weights, out_ref, weight, sem = refs[bases + count :]
    load([weights.at[i] for i in indices], [weight.at[j] for j in range(count)], sem)
    for j in range(count):
        loaded(weight.at[j], sem.at[j])

    def back(columns):
        total = None
        for base in base_refs:
            part = base[:, columns].astype(jnp.float32)
            total = part if total is None else total + part
        for j in range(count):
            part = product_t(grads[j][...], weight[j, columns, :])
            total = part if total is None else total + part
        out_ref[:, columns] = total.astype(out_ref.dtype)

    tiles(back, out_ref.shape[1], TILE)


def split(value):
    high = bfloat(value)
    return high, bfloat(value - high.astype(jnp.float32))


def put_left(ref, value):
    high, low = split(value)
    ref[:, :ADAPT] = high
    ref[:, ADAPT : 2 * ADAPT] = high
    ref[:, 2 * ADAPT :] = low


def put_right(ref, value):
    high, low = split(value)
    ref[:ADAPT, :] = high
    ref[ADAPT : 2 * ADAPT, :] = low
    ref[2 * ADAPT :, :] = high


def multiply(out_ref, left, right):
    def body(columns):
        out_ref[:, columns] = product(left[...], right[:, columns])

    tiles(body, ADAPT, TILE)


def muon_kernel(parts, *refs):
    rows_refs, (out_ref, high, low, gram, poly, left, right, rows_left) = refs[:parts], refs[parts:]
    rows = rows_refs[0].shape[0]
    for i, ref in enumerate(rows_refs):
        high[i * rows : (i + 1) * rows, :], low[i * rows : (i + 1) * rows, :] = split(ref[...])

    def square(columns):
        gram[:, columns] = (
            product_rows(high[...], high[:, columns])
            + product_rows(high[...], low[:, columns])
            + product_rows(low[...], high[:, columns])
        )

    tiles(square, ADAPT, TILE)
    eye = lax.broadcasted_iota(jnp.int32, (ADAPT, ADAPT), 0) == lax.broadcasted_iota(
        jnp.int32, (ADAPT, ADAPT), 1
    )
    scale = 1.0 / (jnp.sqrt(jnp.sum(jnp.where(eye, gram[...], 0.0), keepdims=True)) + 1e-07)
    gram[...] = gram[...] * (scale * scale)

    def polynomial():
        put_left(left, gram[...])
        put_right(right, gram[...])
        multiply(poly, left, right)
        poly[...] = (
            jnp.where(eye, NEWTON_LINEAR, 0.0) + NEWTON_QUADRATIC * gram[...] + NEWTON_CUBIC * poly[...]
        )
        put_right(right, poly[...])
        put_left(rows_left, out_ref[...])
        multiply(out_ref, rows_left, right)

    def advance():
        multiply(gram, left, right)
        put_left(left, gram[...])
        multiply(gram, left, right)

    out_ref[...] = rows_refs[0][...] * scale

    @pl.loop(0, NS_ITERS - 1)
    def _(i):
        polynomial()
        advance()

    polynomial()


HBM = pl.BlockSpec(memory_space=pltpu.HBM)
IN_VMEM = pl.BlockSpec(memory_space=pltpu.VMEM)
F32, BF16 = jnp.float32, jnp.bfloat16


def call(kernel, ins, specs, outs, scratch, flops, collective_id=None, after=()):
    if after:
        inner, first = kernel, len(ins)
        kernel = lambda *refs: inner(*refs[:first], *refs[first + len(after) :])
        ins, specs = [*ins, *after], [*specs, *[HBM] * len(after)]
    return pl.pallas_call(
        kernel,
        in_specs=specs,
        out_specs=[IN_VMEM if len(out) == 2 else HBM for out in outs],
        out_shape=[jax.ShapeDtypeStruct(*out[:2]) for out in outs],
        scratch_shapes=scratch,
        compiler_params=pltpu.CompilerParams(
            vmem_limit_bytes=VMEM_LIMIT,
            collective_id=collective_id,
            has_side_effects=collective_id is not None,
        ),
        cost_estimate=pl.CostEstimate(
            flops=flops, bytes_accessed=sum(a.size * a.dtype.itemsize for a in ins), transcendentals=0
        ),
    )(*ins)


def squares(count):
    return pltpu.VMEM((count, D, D), BF16)


def stored(*shape):
    return (shape, BF16, HBM)


def project(collective_id, x, far, pieces, offsets):
    rows = x.shape[0]
    count, n = len(offsets), len(pieces.arrays)
    return call(
        functools.partial(project_kernel, n, pieces.height, offsets),
        [x, far, *pieces.arrays],
        [IN_VMEM] * 2 + [HBM] * n,
        [((rows, D), BF16)] * (count + 2) + [stored(count, D, D)],
        [squares(count), *loader_sems(count, n)],
        2 * rows * D * D * (count + 2),
        collective_id,
    )


def settle(collective_id, x, mix, gains, pieces, wo_at, q_at, gain_rows, after=()):
    rows = x.shape[0]
    n = len(pieces.arrays)
    count = 1 if q_at is None else 2
    outs = [((rows, D), F32), ((rows, STAT), F32)]
    scratch = [squares(count), pltpu.VMEM((rows, D), F32)]
    if q_at is not None:
        outs.append(((rows, D), BF16))
        scratch.append(pltpu.VMEM((rows, D), BF16))
    return call(
        functools.partial(settle_kernel, n, pieces.height, wo_at, q_at, gain_rows),
        [x, mix, gains, *pieces.arrays],
        [IN_VMEM] * 3 + [HBM] * n,
        outs + [stored(count, D, D)],
        scratch + loader_sems(count, n),
        2 * rows * D * D * count,
        collective_id,
        after,
    )


def tail_up(collective_id, normed, gains, pieces, up_at, gain_row):
    rows = normed.shape[0]
    n = len(pieces.arrays)
    blocks = 4
    hidden = blocks * D
    return call(
        functools.partial(tail_up_kernel, n, pieces.height, up_at, gain_row),
        [normed, gains, *pieces.arrays],
        [IN_VMEM] * 2 + [HBM] * n,
        [stored(rows, hidden), stored(rows, hidden), stored(blocks, D, D)],
        [
            squares(blocks),
            pltpu.VMEM((rows, D), BF16),
            pltpu.VMEM((rows, hidden), BF16),
            pltpu.VMEM((rows, hidden), BF16),
            pltpu.SemaphoreType.DMA((2, blocks)),
            *loader_sems(blocks, n),
        ],
        8 * rows * D * D,
        collective_id,
    )


def tail_down(collective_id, normed, inner, gains, bias_first, bias_second, pieces, offsets, gain_rows):
    rows, hidden = inner.shape
    n = len(pieces.arrays)
    return call(
        functools.partial(tail_down_kernel, n, pieces.height, offsets, gain_rows),
        [normed, inner, gains, bias_first[None], bias_second[None], *pieces.arrays],
        [IN_VMEM] * 5 + [HBM] * n,
        [
            ((rows, ADAPT), BF16),
            ((rows, ADAPT), BF16),
            ((rows, D), F32),
            ((rows, STAT), F32),
            ((rows, D), BF16),
            stored(hidden, D),
            stored(D, D),
        ],
        [
            pltpu.VMEM((hidden, D), BF16),
            pltpu.VMEM((D, D), BF16),
            pltpu.VMEM((rows, D), BF16),
            pltpu.VMEM((rows, D), F32),
            *loader_sems(1 + D // TILE, n),
        ],
        10 * rows * D * D,
        collective_id,
    )


def tail_back(height, cot, second, first, gains, slope, pre_slope, adapt_low, weights, gain_rows, more=()):
    rows = cot.shape[0]
    hidden = slope.shape[1]
    return call(
        functools.partial(tail_back_kernel, height, gain_rows, bool(more)),
        [cot, *second, *first, gains, slope, pre_slope, adapt_low, *weights, *more],
        [IN_VMEM] * 6 + [HBM] + [IN_VMEM] * 2 + [HBM] * 4 + [IN_VMEM] * len(more),
        [
            ((rows, D), BF16),
            ((rows, D), F32),
            ((rows, D), BF16),
            ((D // height, 2 * height + BIAS_ROWS, ADAPT), BF16),
        ],
        [
            squares(hidden // D),
            pltpu.VMEM((hidden, D), BF16),
            pltpu.VMEM((D, D), BF16),
            pltpu.VMEM((D, D), BF16),
            pltpu.VMEM((rows, D), F32),
            pltpu.VMEM((rows, D), BF16),
            pltpu.VMEM((rows, D), BF16),
            pltpu.VMEM((rows, hidden), BF16),
            pltpu.VMEM((rows, ADAPT), BF16),
            pltpu.SemaphoreType.DMA((5,)),
        ],
        24 * rows * D * D,
    )


def query_back(dz, dq, first, gains, weights, gain_row):
    rows = dz.shape[0]
    return call(
        functools.partial(query_back_kernel, gain_row),
        [dz, dq, *first, gains, weights],
        [IN_VMEM] * 5 + [HBM],
        [((rows, D), F32), ((rows, D), BF16)],
        [
            squares(2),
            pltpu.VMEM((rows, D), F32),
            pltpu.VMEM((rows, D), BF16),
            pltpu.SemaphoreType.DMA((2,)),
        ],
        4 * rows * D * D,
    )


def back(bases, grads, weights, indices, dtype):
    rows = grads[0].shape[0]
    count = len(indices)
    return call(
        functools.partial(back_kernel, indices, len(bases)),
        [*bases, *grads, weights],
        [IN_VMEM] * (len(bases) + count) + [HBM],
        [((rows, D), dtype)],
        [squares(count), pltpu.SemaphoreType.DMA((count,))],
        2 * rows * D * D * count,
    )[0]


def muon(parts):
    rows = parts[0].shape[0]
    full = pltpu.VMEM((ADAPT, ADAPT), F32)
    return call(
        functools.partial(muon_kernel, len(parts)),
        parts,
        [IN_VMEM] * len(parts),
        [((rows, ADAPT), F32)],
        [
            pltpu.VMEM((rows * len(parts), ADAPT), BF16),
            pltpu.VMEM((rows * len(parts), ADAPT), BF16),
            full,
            full,
            pltpu.VMEM((ADAPT, 3 * ADAPT), BF16),
            pltpu.VMEM((3 * ADAPT, ADAPT), BF16),
            pltpu.VMEM((rows, 3 * ADAPT), BF16),
        ],
        20 * 6 * ADAPT**3,
    )[0]


def axis_bits(axis):
    return [1 << b for b in range(lax.axis_size(axis).bit_length() - 1)]


def tie(array, *others):
    return lax.optimization_barrier((array, *others))[0]


class Gather:
    def __init__(self, array, height):
        self.height = height
        self.array = array

    def begin(self, *after):
        array = tie(self.array, *after) if after else self.array
        steps = ((2, 4), (4, 2))
        self.arrays = [self.array] + [
            lax.ppermute(
                array, "wide", [(i, i ^ steps[i % 2][which]) for i in range(lax.axis_size("wide"))]
            )
            for which in range(2)
        ]
        return self

    def across(self, *after):
        first = tie(self.arrays[1], *after) if after else self.arrays[1]
        self.arrays.append(
            lax.ppermute(
                first, "wide", [(i, i ^ (2 if i % 2 else 4)) for i in range(lax.axis_size("wide"))]
            )
        )
        for bit in axis_bits("wide")[3:]:
            self.arrays += [swap(piece, "wide", bit) for piece in self.arrays]
        return self


def gather_any_order(array, axis):
    blocks = array[None]
    for bit in axis_bits(axis):
        blocks = jnp.concatenate([blocks, swap(blocks, axis, bit)])
    return blocks


def shards(
    enc_in,
    dec_in,
    segment_ids,
    enc_cot,
    dec_cot,
    enc_qkv,
    enc_wo,
    enc_w_in,
    enc_w_out,
    enc_gains,
    dec_qkv,
    dec_wo,
    dec_w_in,
    dec_w_out,
    dec_gains,
    adapter_weights,
    adapter_momenta,
    bias_in,
    bias_out,
):
    height = enc_wo.shape[0]
    stack = lambda *arrays: jnp.concatenate([a.reshape(-1, D) for a in arrays])
    columns = lambda array: [array[:, j * D : (j + 1) * D] for j in range(array.shape[1] // D)]
    gain_rows = jnp.concatenate([enc_gains, dec_gains])
    gain_block = jnp.pad(gain_rows, ((0, 16 - gain_rows.shape[0]), (0, D - height)))
    gather = lambda array: Gather(array, height)
    enc_first = gather(stack(enc_qkv, gain_block))
    dec_first = gather(stack(dec_qkv[:3]))
    enc_up = gather(stack(enc_wo, *columns(enc_w_in)))
    dec_second = gather(stack(dec_wo[0], dec_qkv[3]))
    dec_third = gather(stack(dec_qkv[4:], dec_wo[1]))
    dec_up = gather(stack(*columns(dec_w_in)))

    count = lax.axis_size("wide")
    partner = lambda array: swap(array, "narrow", 1)
    rows = enc_in.shape[0]
    half = (lax.axis_index("narrow") % 2).astype(jnp.int32).reshape(1)
    at = lambda i: i * height

    enc_first.begin()
    enc_far = partner(enc_in)
    enc_first.across()
    begun = enc_first.arrays[-1]
    dec_first.begin(begun)
    dec_far = partner(tie(dec_in, begun))
    other_ids = partner(tie(segment_ids, begun))
    places = (half, segment_ids.reshape(1, rows), segment_ids.reshape(rows, 1), other_ids.reshape(rows, 1))
    found = gather_any_order(bfloat(tie(adapter_weights, begun)), "narrow")
    found = found[lax.axis_index("narrow") ^ jnp.arange(lax.axis_size("narrow"))]
    adapters = found.transpose(1, 0, 2, 3).reshape(4, height, ADAPT)
    beside = lambda l: jnp.concatenate([adapters[2 * l], adapters[2 * l + 1]], axis=1)
    enc_query, enc_key, enc_value, enc_key_far, enc_value_far, enc_qkv_full = project(
        0, tie(enc_in, begun), enc_far, enc_first, (at(0), at(1), at(2))
    )
    enc_keys, enc_values = (enc_key, enc_key_far), (enc_value, enc_value_far)

    repeat = lax.axis_size("narrow") // 4
    spread = lambda array: jnp.repeat(array, repeat, axis=0) if repeat > 1 else array
    exchange = lambda array, axis: lax.all_to_all(array, axis, split_axis=0, concat_axis=0, tiled=True)
    to_matrix = lambda array: exchange(spread(array), "narrow").reshape(-1, ADAPT)
    to_rows = lambda array: exchange(
        array.reshape(lax.axis_size("narrow"), -1, ADAPT), "narrow"
    )[::repeat]

    dec_first.across(enc_value)
    enc_up.begin(enc_value)
    enc_mix, enc_lse = attend(places, enc_query, enc_keys, enc_values, False)
    found = jnp.stack([p[at(3) : at(3) + 8, :height] for p in enc_first.arrays])
    found = jnp.concatenate([found, swap(tie(found, enc_mix), "wide", 1)])
    me = lax.axis_index("wide")
    apart = me ^ jnp.arange(count)
    odd = ((me ^ apart) & 1) == 1
    low = apart & 6
    piece = jnp.where(low == 0, 0, jnp.where(low == 6, 3, jnp.where((low == 2) ^ odd, 1, 2)))
    order = (apart & 1) * (count // 2) + (apart >> 3) * 4 + piece
    gains = found[order].transpose(1, 0, 2).reshape(8, D).astype(jnp.float32)
    enc_down = gather(stack(enc_w_out, tie(beside(0), enc_mix)))
    dec_down = gather(stack(dec_w_out, tie(beside(1), enc_mix)))
    enc_down.begin(enc_mix)
    self_query, self_key, self_value, self_key_far, self_value_far, dec_qkv_full = project(
        1, tie(dec_in, enc_mix), dec_far, dec_first, (at(0), at(1), at(2))
    )
    self_keys, self_values = (self_key, self_key_far), (self_value, self_value_far)
    enc_up.across(self_value)
    self_mix, self_lse = attend(places, self_query, self_keys, self_values, True)
    dec_second.begin(self_mix)
    *enc_norm1, enc_wo_full = settle(
        2, enc_in, tie(enc_mix, self_mix), gains, enc_up, at(0), None, (None, 0)
    )
    enc_down.across(enc_norm1[0])
    enc_slope, enc_inner, enc_up_full = tail_up(3, enc_norm1[0], gains, enc_up, at(1), 0)
    dec_second.across(enc_inner)
    dec_third.begin(enc_inner)
    enc_pre_slope, enc_adapt, *enc_norm2, enc_low, enc_down_full, enc_adapt_full = tail_down(
        4, enc_norm1[0], enc_inner, gains, bias_in[0], bias_out[0], enc_down, (0, at(4)), (0, 1)
    )
    enc_low_far = partner(enc_low)
    dec_third.across(enc_low)
    dec_up.begin(enc_low)
    *dec_norm1, cross_query, dec_q_full = settle(
        5, dec_in, tie(self_mix, enc_low), gains, dec_second, at(0), at(1), (None, 2)
    )
    cross_key, cross_value, cross_key_far, cross_value_far, dec_kv_full = project(
        6, tie(enc_low, cross_query), enc_low_far, dec_third, (at(0), at(1))
    )
    cross_keys, cross_values = (cross_key, cross_key_far), (cross_value, cross_value_far)
    dec_up.across(cross_key)
    dec_down.begin(cross_key)
    cross_mix, cross_lse = attend(places, cross_query, cross_keys, cross_values, False)
    *dec_norm2, dec_wo_full = settle(
        7, dec_norm1[0], cross_mix, gains, dec_third, at(2), None, (2, 3)
    )
    dec_down.across(dec_norm2[0])
    dec_slope, dec_inner, dec_up_full = tail_up(8, dec_norm2[0], gains, dec_up, at(0), 3)
    dec_pre_slope, dec_adapt, *dec_norm3, _, dec_down_full, dec_adapt_full = tail_down(
        9, dec_norm2[0], dec_inner, gains, bias_in[1], bias_out[1], dec_down, (0, at(4)), (3, 4)
    )

    dec_out, grad_z2, grad_cross_mix, dec_matrices = tail_back(
        height,
        dec_cot,
        dec_norm3,
        dec_norm2,
        gains,
        dec_slope,
        dec_pre_slope,
        dec_adapt,
        (dec_up_full, dec_down_full, dec_adapt_full, dec_wo_full),
        (3, 4),
    )
    total = lambda array: jnp.sum(array.astype(jnp.float32), axis=0)
    dec_matrices = exchange(dec_matrices, "wide")
    cross_back = attend_back(
        places, grad_cross_mix, cross_query, cross_keys, cross_values, cross_mix, cross_lse, False
    )
    dec_sums = total(tie(dec_matrices, cross_back[0]))
    far_encoded = back((), (tie(cross_back[2], dec_sums), cross_back[4]), dec_kv_full, (0, 1), BF16)
    near_encoded = partner(far_encoded)
    grad_encoded = back(
        (tie(enc_cot, far_encoded),), (cross_back[1], cross_back[3]), dec_kv_full, (0, 1), F32
    )
    grad_z1, grad_self_mix = query_back(
        tie(grad_z2, grad_encoded),
        cross_back[0],
        dec_norm1,
        gains,
        dec_q_full,
        2,
    )
    enc_out, grad_ez1, grad_enc_mix, enc_matrices = tail_back(
        height,
        tie(grad_encoded, grad_z1),
        enc_norm2,
        enc_norm1,
        gains,
        enc_slope,
        enc_pre_slope,
        enc_adapt,
        (enc_up_full, enc_down_full, enc_adapt_full, enc_wo_full),
        (0, 1),
        (near_encoded,),
    )
    old_momentum = to_matrix(tie(adapter_momenta, grad_z1))
    enc_matrices = exchange(tie(enc_matrices, old_momentum), "wide")

    self_back = attend_back(
        places, tie(grad_self_mix, grad_ez1), self_query, self_keys, self_values, self_mix, self_lse, True, (old_momentum,)
    )

    enc_sums = total(tie(enc_matrices, self_back[0]))
    sums = [array[at(i) : at(i + 1)] for array in (enc_sums, dec_sums) for i in range(2)]
    biases = jnp.concatenate([array[at(2) : at(2) + BIAS_ROWS // 2] for array in (enc_sums, dec_sums)])
    sums = jnp.stack([jnp.concatenate([array, biases]) for array in sums])
    sums = spread(bfloat(sums))
    far_dec = back(
        (), (tie(self_back[2], sums), self_back[4]), dec_qkv_full, (1, 2), BF16
    )
    near_dec = partner(far_dec)
    enc_back = attend_back(
        places, tie(grad_enc_mix, far_dec), enc_query, enc_keys, enc_values, enc_mix, enc_lse, False
    )
    summed = exchange(sums, "narrow")
    summed = total(tie(summed, enc_back[0]))
    momentum = DECAY * old_momentum + summed[:height]
    layers = summed[height:].reshape(2, -1, ADAPT)
    place = lax.axis_index("wide") * lax.axis_size("narrow") + lax.axis_index("narrow")
    devices = lax.axis_size("wide") * lax.axis_size("narrow")
    own_part = lambda array: lax.dynamic_slice_in_dim(
        array, place * (array.shape[1] // devices), array.shape[1] // devices, 1
    )
    grad_bias_in, grad_bias_out = own_part(layers[:, 0]), own_part(layers[:, 1:3].reshape(2, D))
    parts = [momentum] + [swap(momentum, "wide", r) for r in range(1, lax.axis_size("wide"))]
    new_momenta = to_rows(momentum)

    far_enc = back((), (tie(enc_back[2], momentum), enc_back[4]), enc_qkv_full, (1, 2), BF16)
    near_enc = partner(far_enc)
    grad_dec = back(
        (tie(grad_z1, far_enc), near_dec),
        (self_back[0], self_back[1], self_back[3]),
        dec_qkv_full,
        (0, 1, 2),
        F32,
    )
    orthogonal = muon([parts[0], tie(parts[1], grad_dec), *parts[2:]])
    grad_enc = back(
        (tie(grad_ez1, orthogonal), near_enc),
        (enc_back[0], enc_back[1], enc_back[3]),
        enc_qkv_full,
        (0, 1, 2),
        F32,
    )
    new_weights = adapter_weights - RATE * math.sqrt(max(1.0, D / ADAPT)) * tie(
        to_rows(orthogonal), grad_enc
    )
    return (
        enc_out,
        dec_out,
        grad_enc,
        grad_dec,
        grad_bias_in,
        grad_bias_out,
        new_momenta,
        new_weights,
    )


def solution(mesh):
    both = ("wide", "narrow")
    tokens = P(both, None)
    rows_first, rows_second = P("wide", None), P(None, "wide", None)
    adapters = P(None, both, None)
    in_specs = (
        tokens,
        tokens,
        P(both),
        tokens,
        tokens,
        rows_second,
        rows_first,
        rows_first,
        rows_first,
        P(None, "wide"),
        rows_second,
        rows_second,
        rows_first,
        rows_first,
        P(None, "wide"),
        adapters,
        adapters,
        P(),
        P(),
    )
    out_specs = (
        tokens,
        tokens,
        tokens,
        tokens,
        P(None, both),
        P(None, both),
        adapters,
        adapters,
    )
    return jax.shard_map(shards, mesh=mesh, in_specs=in_specs, out_specs=out_specs, check_vma=False)
```
